512 devices in a mesh: row: 16 (over y_lo, x, core), col: 32 (over y_hi, z).
Axes of the slice: x: 4, y: 8 (y_hi: 4, y_lo: 2; y = y_hi * 2 + y_lo), z: 8, core: 2. Of those that a mesh axis runs over, the one named last changes fastest.
Arguments:
- inputs: bfloat16 [2048, 4096], P('row', 'col'), may hold values from -6 to 6
- out_grad: bfloat16 [2048, 4096], P('row', 'col'), may hold values from -2 to 2
- codes: bfloat16 [3, 4096, 8192], P(None, 'row', 'col'), may hold values from -0.09375 to 0.09375
- scales: bfloat16 [3, 16, 8192], P(None, 'row', 'col'), may hold values from 0.5 to 2
Outputs:
- input_grad: bfloat16 [2048, 4096], P('row', 'col')
- weight_grad: float32 [3, 4096, 8192], P(None, 'row', 'col')
The draws below stay inside these ranges and needn't reach their ends.
All inputs are finite; a program needn't handle non-finite values.
Results may differ from the reference program's by a relative error of at most 0.022.
Values may be sent and summed in bfloat16 or wider, within the bound.
No kernel may reach another device: no remote copies, remote signals or barrier semaphores. Data moves between devices by JAX's collectives and lax.ppermute only.
A program may use at most 128 MiB of HBM per device.

```python
import math
import jax
import jax.numpy as jnp
from jax import lax

D = 4096
FF = 8192
QB = 256
TOK_DEV = 128
TOKENS = 2048
N_ROW = 16


def shard_levels(rng, dims, pieces, least, top_value):
    level = 1.0
    for dim, shards_of in pieces:
        heights = jax.random.uniform(jax.random.fold_in(jax.random.fold_in(rng, 6), dim), (shards_of,), jnp.float32, least / len(pieces), top_value / len(pieces))
        level = level * jnp.repeat(jnp.exp(heights), dims[dim] // shards_of).reshape((-1,) + (1,) * (len(dims) - 1 - dim))
    return level


def noise(rng, extent, scale, bound, pieces=(), held_as=jnp.bfloat16):
    result = scale * jax.random.normal(rng, extent, jnp.float32)
    if pieces:
        result = result * shard_levels(rng, extent, pieces, -0.22, 0.18)
    return jnp.clip(result, -bound, bound).astype(held_as)


def setup_inputs(seed: int = 0) -> dict:
    splits = jax.random.split(jax.random.key(seed), 5)
    inputs = noise(splits[0], (TOKENS, D), 1.0, 6.0, ((0, 16), (1, 32)))
    out_grad = noise(splits[1], (TOKENS, D), 0.15, 2.0, ((0, 16), (1, 32)))
    codes = noise(splits[2], (3, D, FF), D ** -0.5, 0.09375, ((1, 16), (2, 32)))
    scales = jnp.clip(jnp.exp(math.log(2.0) - 1.3862944 * jax.random.uniform(splits[3], (3, D // QB, FF), jnp.float32) ** shard_levels(splits[3], (3, D // QB, FF), ((1, 16), (2, 32)), -0.2, 0.2)), 0.5, 2.0).astype(jnp.bfloat16)
    return {"inputs": inputs, "out_grad": out_grad, "codes": codes, "scales": scales}


def dequantize(codes, scales):
    full = codes.astype(jnp.float32) * jnp.repeat(scales.astype(jnp.float32), QB, axis=1)
    return full.astype(jnp.bfloat16)


def reference(inputs, out_grad, codes, scales):
    weights = dequantize(codes, scales)
    w_gate, w_up, w_down = weights[0], weights[1], weights[2]
    gate = jnp.dot(inputs, w_gate, preferred_element_type=jnp.float32)
    up = jnp.dot(inputs, w_up, preferred_element_type=jnp.float32)
    sig = jax.nn.sigmoid(gate)
    act = gate * sig
    hidden = (act * up).astype(jnp.bfloat16)
    hidden_grad = jnp.dot(out_grad, w_down, preferred_element_type=jnp.float32)
    up_grad = (hidden_grad * act).astype(jnp.bfloat16)
    gate_grad = (hidden_grad * up * sig * (1.0 + gate * (1.0 - sig))).astype(jnp.bfloat16)
    input_grad = jnp.dot(gate_grad, w_gate.T, preferred_element_type=jnp.float32)
    input_grad = input_grad + jnp.dot(up_grad, w_up.T, preferred_element_type=jnp.float32)
    input_grad = input_grad.astype(jnp.bfloat16)

    in_blocks = inputs.reshape(N_ROW, TOK_DEV, D)
    out_blocks = out_grad.reshape(N_ROW, TOK_DEV, D)
    gate_blocks = gate_grad.reshape(N_ROW, TOK_DEV, FF)
    up_blocks = up_grad.reshape(N_ROW, TOK_DEV, FF)
    hid_blocks = hidden.reshape(N_ROW, TOK_DEV, FF)

    def accumulate(total, items):
        x_blk, dy_blk, dg_blk, du_blk, h_blk = items
        partial_value = jnp.stack([
            jnp.dot(x_blk.T, dg_blk, preferred_element_type=jnp.float32),
            jnp.dot(x_blk.T, du_blk, preferred_element_type=jnp.float32),
            jnp.dot(dy_blk.T, h_blk, preferred_element_type=jnp.float32)])
        blocked = partial_value.reshape(3, D // QB, QB, FF)
        block_scale = (jnp.max(jnp.abs(blocked), axis=2) + 1e-6).astype(jnp.bfloat16)
        wide_scale = block_scale.astype(jnp.float32)[:, :, None, :]
        packed = (blocked / wide_scale).astype(jnp.bfloat16)
        restored = packed.astype(jnp.float32) * wide_scale
        return total + restored.reshape(3, D, FF), None

    start = jnp.zeros((3, D, FF), jnp.float32)
    weight_grad, unused = lax.scan(accumulate, start, (in_blocks, out_blocks, gate_blocks, up_blocks, hid_blocks))
    return input_grad, weight_grad
```

```python
import functools

import jax
import jax.numpy as jnp
from jax import lax
from jax.experimental import pallas as pl
from jax.experimental.pallas import tpu as pltpu
from jax.sharding import Mesh, PartitionSpec as P

F32 = jnp.float32
BF16 = jnp.bfloat16
ROW = ("yl", "x", "core")
COL = ("yh", "z")
YL, X, CORE, YH, Z = 2, 4, 2, 4, 8
N_ROW = YL * X * CORE
TOK = 128
VMEM_LIMIT = 56 * 1024 * 1024


def dot(a, b, dims):
    return lax.dot_general(a, b, (dims, ((), ())), preferred_element_type=F32)


def gather_by_swap(block, axis, size):
    copies = jnp.broadcast_to(block[None], (size,) + block.shape)
    return lax.all_to_all(copies, axis, split_axis=0, concat_axis=0, tiled=True)


def features(acts_ref, which, r):
    y, z = r // 4, (r % 4) * 2
    return jnp.concatenate([acts_ref[z, y, which], acts_ref[z + 1, y, which]], axis=1)


def forward_kernel(acts_ref, w_ref, grads_ref, dx_ref):
    gate = jnp.zeros((TOK, 256), F32)
    up = jnp.zeros((TOK, 256), F32)
    hidden_grad = jnp.zeros((TOK, 256), F32)
    for r in range(N_ROW):
        tokens = features(acts_ref, 0, r)
        gate += dot(tokens, w_ref[r, 0], ((1,), (0,)))
        up += dot(tokens, w_ref[r, 1], ((1,), (0,)))
        hidden_grad += dot(features(acts_ref, 1, r), w_ref[r, 2], ((1,), (0,)))
    sig = 1.0 / (1.0 + jnp.exp(-gate))
    act = gate * sig
    gate_grad = (hidden_grad * up * sig * (1.0 + gate * (1.0 - sig))).astype(BF16)
    up_grad = (hidden_grad * act).astype(BF16)
    grads_ref[0] = gate_grad
    grads_ref[1] = up_grad
    grads_ref[2] = (act * up).astype(BF16)
    for r in range(N_ROW):
        dx = dot(gate_grad, w_ref[r, 0], ((1,), (1,))) + dot(up_grad, w_ref[r, 1], ((1,), (1,)))
        dx = dx.astype(BF16)
        y, z = r // 4, (r % 4) * 2
        dx_ref[y, z] = dx[:, :128]
        dx_ref[y, z + 1] = dx[:, 128:]


def forward(acts, weights):
    whole = pl.BlockSpec(memory_space=pltpu.VMEM)
    return pl.pallas_call(
        forward_kernel,
        out_shape=(
            jax.ShapeDtypeStruct((3, TOK, 256), BF16),
            jax.ShapeDtypeStruct((YH, Z, TOK, 128), BF16),
        ),
        in_specs=[whole, whole],
        out_specs=(whole, whole),
        compiler_params=pltpu.CompilerParams(vmem_limit_bytes=VMEM_LIMIT),
        cost_estimate=pl.CostEstimate(flops=1400000000, bytes_accessed=10000000, transcendentals=32768),
        name="forward",
    )(acts, weights)


def weight_kernel(core_ref, acts_ref, other_acts_ref, grads_ref, other_grads_ref, out_ref):
    k = core_ref[0]
    for q in range(N_ROW // 2):
        y, j = q // 2, q % 2
        z = 4 * j + 2 * k
        feats = []
        for which in range(2):
            own = jnp.concatenate([acts_ref[z, y, which], acts_ref[z + 1, y, which]], axis=1)
            other = jnp.concatenate(
                [other_acts_ref[j, 0, y, which], other_acts_ref[j, 1, y, which]], axis=1
            )
            feats.append(jnp.concatenate([own, other], axis=0))
        for p in range(3):
            grads = jnp.concatenate([grads_ref[p], other_grads_ref[p]], axis=0)
            out_ref[q, p] = dot(feats[p // 2], grads, ((0,), (0,))).astype(BF16)


def weight_terms(core, acts, other_acts, grads, other_grads):
    whole = pl.BlockSpec(memory_space=pltpu.VMEM)
    return pl.pallas_call(
        weight_kernel,
        out_shape=jax.ShapeDtypeStruct((N_ROW // 2, 3, 256, 256), BF16),
        in_specs=[pl.BlockSpec(memory_space=pltpu.SMEM)] + [whole] * 4,
        out_specs=whole,
        compiler_params=pltpu.CompilerParams(vmem_limit_bytes=VMEM_LIMIT),
        cost_estimate=pl.CostEstimate(flops=800000000, bytes_accessed=6000000, transcendentals=0),
        name="weight_terms",
    )(core, acts, other_acts, grads, other_grads)


def local(inputs, out_grad, codes, scales):
    core = lax.axis_index("core")
    swap = [(0, 1), (1, 0)]
    weights = (codes.astype(F32) * scales.astype(F32)).astype(BF16)
    weights = lax.all_gather(weights, ROW, axis=0, tiled=False)

    acts = gather_by_swap(jnp.stack([inputs, out_grad]), "yh", YH)
    acts = gather_by_swap(acts, "z", Z)

    halves = acts.reshape(2, 2, 2, YH, 2, TOK, 128)
    other_half = lax.dynamic_index_in_dim(halves, 1 - core, axis=1, keepdims=False)
    other_acts = lax.ppermute(other_half, "core", swap)

    grads, dx = forward(acts, weights)
    other_grads = lax.ppermute(grads, "core", swap)
    dx = lax.all_to_all(dx.reshape(YH * Z, TOK, 128), COL, split_axis=0, concat_axis=0, tiled=True)
    input_grad = jnp.sum(dx.astype(F32), axis=0).astype(BF16)

    terms = weight_terms(core.reshape(1), acts, other_acts, grads, other_grads)
    terms = lax.all_to_all(terms, ("yl", "x"), split_axis=0, concat_axis=0, tiled=True)
    weight_grad = jnp.sum(terms.astype(F32), axis=0)
    return input_grad, weight_grad


def solution(mesh):
    fine = Mesh(mesh.devices.reshape(YL, X, CORE, YH, Z), ROW + COL)
    return jax.shard_map(
        local,
        mesh=fine,
        in_specs=(P(ROW, COL), P(ROW, COL), P(None, ROW, COL), P(None, ROW, COL)),
        out_specs=(P(ROW, COL), P(None, ROW, COL)),
        check_vma=False,
    )
```

```python
import functools

import jax
import jax.numpy as jnp
from jax import lax
from jax.experimental import pallas as pl
from jax.experimental.pallas import tpu as pltpu
from jax.sharding import Mesh, PartitionSpec as P

F32 = jnp.float32
BF16 = jnp.bfloat16
ROW = ("yl", "x", "core")
COL = ("yh", "z")
YL, X, CORE, YH, Z = 2, 4, 2, 4, 8
N_ROW = YL * X * CORE
TOK = 128
VMEM_LIMIT = 56 * 1024 * 1024


def dot(a, b, dims):
    return lax.dot_general(a, b, (dims, ((), ())), preferred_element_type=F32)


def gather_by_swap(block, axis, size):
    copies = jnp.broadcast_to(block[None], (size,) + block.shape)
    return lax.all_to_all(copies, axis, split_axis=0, concat_axis=0, tiled=True)


def fan_out(block, axis, size):
    shifts = [[(i, (i + d) % size) for i in range(size)] for d in range(1, size)]
    return [block] + [lax.ppermute(block, axis, shift) for shift in shifts]


def forward_kernel(place_ref, x_ref, dy_ref, w_ref, grads_ref, dx_ref):
    gate = jnp.zeros((TOK, 256), F32)
    up = jnp.zeros((TOK, 256), F32)
    hidden_grad = jnp.zeros((TOK, 256), F32)
    ys = [lax.rem(place_ref[1] + YH - d, YH) for d in range(YH)]
    for d in range(YH):
        for j in range(Z // 2):
            r = ys[d] * 4 + j
            tokens = jnp.concatenate([x_ref[2 * j, d], x_ref[2 * j + 1, d]], axis=1)
            gate += dot(tokens, w_ref[r, 0], ((1,), (0,)))
            up += dot(tokens, w_ref[r, 1], ((1,), (0,)))
            cots = jnp.concatenate([dy_ref[d, 2 * j], dy_ref[d, 2 * j + 1]], axis=1)
            hidden_grad += dot(cots, w_ref[r, 2], ((1,), (0,)))
    sig = 1.0 / (1.0 + jnp.exp(-gate))
    act = gate * sig
    gate_grad = (hidden_grad * up * sig * (1.0 + gate * (1.0 - sig))).astype(BF16)
    up_grad = (hidden_grad * act).astype(BF16)
    grads_ref[0] = gate_grad
    grads_ref[1] = up_grad
    grads_ref[2] = (act * up).astype(BF16)
    for r in range(N_ROW):
        dx = dot(gate_grad, w_ref[r, 0], ((1,), (1,))) + dot(up_grad, w_ref[r, 1], ((1,), (1,)))
        dx = dx.astype(BF16)
        y, z = r // 4, (r % 4) * 2
        dx_ref[z, y] = dx[:, :128]
        dx_ref[z + 1, y] = dx[:, 128:]


def forward(place, x, dy, weights):
    whole = pl.BlockSpec(memory_space=pltpu.VMEM)
    return pl.pallas_call(
        forward_kernel,
        out_shape=(
            jax.ShapeDtypeStruct((3, TOK, 256), BF16),
            jax.ShapeDtypeStruct((Z, YH, TOK, 128), BF16),
        ),
        in_specs=[pl.BlockSpec(memory_space=pltpu.SMEM)] + [whole] * 3,
        out_specs=(whole, whole),
        compiler_params=pltpu.CompilerParams(vmem_limit_bytes=VMEM_LIMIT),
        cost_estimate=pl.CostEstimate(flops=1400000000, bytes_accessed=10000000, transcendentals=32768),
        name="forward",
    )(place, x, dy, weights)


def weight_kernel(place_ref, x_ref, dy_ref, other_x_ref, other_dy_ref, grads_ref, other_grads_ref, out_ref):
    k = place_ref[0]
    grads = [jnp.concatenate([grads_ref[p], other_grads_ref[p]], axis=0) for p in range(3)]
    for d in range(YH):
        y = lax.rem(place_ref[1] + YH - d, YH)
        for j in range(2):
            z = 4 * j + 2 * k
            x = jnp.concatenate([x_ref[z, d], x_ref[z + 1, d]], axis=1)
            other_x = jnp.concatenate([other_x_ref[j, 0, d], other_x_ref[j, 1, d]], axis=1)
            x = jnp.concatenate([x, other_x], axis=0)
            dy = jnp.concatenate([dy_ref[d, z], dy_ref[d, z + 1]], axis=1)
            other_dy = jnp.concatenate([other_dy_ref[d, j, 0], other_dy_ref[d, j, 1]], axis=1)
            dy = jnp.concatenate([dy, other_dy], axis=0)
            for p in range(3):
                term = dot(dy if p == 2 else x, grads[p], ((0,), (0,)))
                out_ref[2 * y + j, p] = term.astype(BF16)


def weight_terms(place, *arrays):
    whole = pl.BlockSpec(memory_space=pltpu.VMEM)
    return pl.pallas_call(
        weight_kernel,
        out_shape=jax.ShapeDtypeStruct((N_ROW // 2, 3, 256, 256), BF16),
        in_specs=[pl.BlockSpec(memory_space=pltpu.SMEM)] + [whole] * 6,
        out_specs=whole,
        compiler_params=pltpu.CompilerParams(vmem_limit_bytes=VMEM_LIMIT),
        cost_estimate=pl.CostEstimate(flops=800000000, bytes_accessed=6000000, transcendentals=0),
        name="weight_terms",
    )(place, *arrays)


def local(inputs, out_grad, codes, scales):
    core = lax.axis_index("core")
    yh = lax.axis_index("yh")
    place = jnp.stack([core, yh])
    swap = [(0, 1), (1, 0)]
    weights = (codes.astype(F32) * scales.astype(F32)).astype(BF16)
    weights = lax.all_gather(weights, ROW, axis=0, tiled=False)

    x = jnp.stack(fan_out(inputs, "yh", YH))
    dy = gather_by_swap(out_grad, "z", Z)
    x = gather_by_swap(x, "z", Z)
    dy = jnp.stack(fan_out(dy, "yh", YH))

    other_x = x.reshape(2, 2, 2, YH, TOK, 128)
    other_x = lax.dynamic_index_in_dim(other_x, 1 - core, axis=1, keepdims=False)
    other_x = lax.ppermute(other_x, "core", swap)
    other_dy = dy.reshape(YH, 2, 2, 2, TOK, 128)
    other_dy = lax.dynamic_index_in_dim(other_dy, 1 - core, axis=2, keepdims=False)
    other_dy = lax.ppermute(other_dy, "core", swap)

    grads, dx = forward(place, x, dy, weights)
    dx = lax.psum_scatter(dx, "z", scatter_dimension=0, tiled=False)
    other_grads = lax.ppermute(grads, "core", swap)
    terms = weight_terms(place, x, dy, other_x, other_dy, grads, other_grads)
    terms = lax.all_to_all(terms, ("yl", "x"), split_axis=0, concat_axis=0, tiled=True)

    input_grad = lax.dynamic_index_in_dim(dx, yh, axis=0, keepdims=False).astype(F32)
    for d in range(1, YH):
        part = lax.dynamic_index_in_dim(dx, lax.rem(yh + d, YH), axis=0, keepdims=False)
        part = lax.ppermute(part, "yh", [(i, (i + d) % YH) for i in range(YH)])
        input_grad += part.astype(F32)

    weight_grad = jnp.sum(terms.astype(F32), axis=0)
    return input_grad.astype(BF16), weight_grad


def solution(mesh):
    fine = Mesh(mesh.devices.reshape(YL, X, CORE, YH, Z), ROW + COL)
    return jax.shard_map(
        local,
        mesh=fine,
        in_specs=(P(ROW, COL), P(ROW, COL), P(None, ROW, COL), P(None, ROW, COL)),
        out_specs=(P(ROW, COL), P(None, ROW, COL)),
        check_vma=False,
    )
```

```python
import jax
import jax.numpy as jnp
from jax import lax
from jax.experimental import pallas as pl
from jax.experimental.pallas import tpu as pltpu
from jax.sharding import Mesh, PartitionSpec as P

F32 = jnp.float32
BF16 = jnp.bfloat16
ROW = ("yl", "x", "core")
Z = ("zh", "zl")
COL = ("yh",) + Z
SIZES = {"yl": 2, "x": 4, "core": 2, "yh": 4, "zh": 4, "zl": 2}
N_ROW, N_YH, N_Z = 16, 4, 8
HALF = N_ROW // 2
TOK = 128
VMEM_LIMIT = 56 * 1024 * 1024
WHOLE = pl.BlockSpec(memory_space=pltpu.VMEM)
SCALARS = pl.BlockSpec(memory_space=pltpu.SMEM)


def dot(a, b, dims):
    return lax.dot_general(a, b, (dims, ((), ())), preferred_element_type=F32)


def gather_by_swap(block, axis, size):
    copies = jnp.broadcast_to(block[None], (size,) + block.shape)
    return lax.all_to_all(copies, axis, split_axis=0, concat_axis=0, tiled=True)


def forward_kernel(place_ref, even_ref, x_ref, dy_ref, w_ref, keep_ref, send_ref, dx_ref):
    core, first = place_ref[0], place_ref[1] == 0
    gate = jnp.zeros((TOK, 256), F32)
    up = jnp.zeros((TOK, 256), F32)
    hidden_grad = jnp.zeros((TOK, 256), F32)
    for side in range(2):
        parity = core if side == 0 else 1 - core
        for q in range(HALF):
            y, zh = q // 2, (q % 2) * 2 + parity
            r = 2 * q + parity
            both = []
            for p, other_ref in enumerate((x_ref, dy_ref)):
                mine, other = even_ref[y, zh, p], other_ref[y, zh]
                low = jnp.where(first, mine, other)
                high = jnp.where(first, other, mine)
                both.append(jnp.concatenate([low, high], axis=1))
                if side == 0:
                    keep_ref[2 * q + p] = both[p]
                else:
                    send_ref[2 * q + p] = both[p]
            gate += dot(both[0], w_ref[r, 0], ((1,), (0,)))
            up += dot(both[0], w_ref[r, 1], ((1,), (0,)))
            hidden_grad += dot(both[1], w_ref[r, 2], ((1,), (0,)))
    sig = 1.0 / (1.0 + jnp.exp(-gate))
    act = gate * sig
    gate_grad = (hidden_grad * up * sig * (1.0 + gate * (1.0 - sig))).astype(BF16)
    up_grad = (hidden_grad * act).astype(BF16)
    hidden = (act * up).astype(BF16)
    for p, value in enumerate((gate_grad, up_grad, hidden)):
        keep_ref[N_ROW + p] = value
        send_ref[N_ROW + p] = value
    for r in range(N_ROW):
        dx = dot(gate_grad, w_ref[r, 0], ((1,), (1,))) + dot(up_grad, w_ref[r, 1], ((1,), (1,)))
        dx = dx.astype(BF16)
        y, z = r // 4, (r % 4) * 2
        dx_ref[z, y] = dx[:, :128]
        dx_ref[z + 1, y] = dx[:, 128:]


def forward(place, *arrays):
    pack = jax.ShapeDtypeStruct((N_ROW + 3, TOK, 256), BF16)
    return pl.pallas_call(
        forward_kernel,
        out_shape=(pack, pack, jax.ShapeDtypeStruct((N_Z, N_YH, TOK, 128), BF16)),
        in_specs=[SCALARS] + [WHOLE] * 4,
        out_specs=(WHOLE,) * 3,
        compiler_params=pltpu.CompilerParams(vmem_limit_bytes=VMEM_LIMIT),
        cost_estimate=pl.CostEstimate(flops=1400000000, bytes_accessed=10000000, transcendentals=32768),
        name="forward",
    )(place, *arrays)


def weight_kernel(mine_ref, other_ref, out_ref):
    grads = [
        jnp.concatenate([mine_ref[N_ROW + p], other_ref[N_ROW + p]], axis=0) for p in range(3)
    ]
    for q in range(HALF):
        x = jnp.concatenate([mine_ref[2 * q], other_ref[2 * q]], axis=0)
        dy = jnp.concatenate([mine_ref[2 * q + 1], other_ref[2 * q + 1]], axis=0)
        for p in range(3):
            term = dot(dy if p == 2 else x, grads[p], ((0,), (0,)))
            out_ref[q, p] = term.astype(BF16)


def weight_terms(mine, other):
    return pl.pallas_call(
        weight_kernel,
        out_shape=jax.ShapeDtypeStruct((HALF, 3, 256, 256), BF16),
        in_specs=[WHOLE] * 2,
        out_specs=WHOLE,
        compiler_params=pltpu.CompilerParams(vmem_limit_bytes=VMEM_LIMIT),
        cost_estimate=pl.CostEstimate(flops=8000000, bytes_accessed=60000, transcendentals=0),
        name="weight_terms",
    )(mine, other)


def local(inputs, out_grad, codes, scales):
    place = jnp.stack([lax.axis_index("core"), lax.axis_index("zl")])
    weights = (codes.astype(F32) * scales.astype(F32)).astype(BF16)
    weights = lax.all_gather(weights, ROW, axis=0, tiled=False)

    even = gather_by_swap(jnp.stack([inputs, out_grad]), ("yh", "zh"), 16)
    even = even.reshape(N_YH, 4, 2, TOK, 128)
    x = lax.ppermute(even[:, :, 0], Z, [(i, (i - 1) % N_Z) for i in range(N_Z)])
    dy = lax.ppermute(even[:, :, 1], Z, [(i, (i + 1) % N_Z) for i in range(N_Z)])

    keep, send, dx = forward(place, even, x, dy, weights)
    dx = lax.psum_scatter(dx, Z, scatter_dimension=0, tiled=False)
    other = lax.ppermute(send, "core", [(0, 1), (1, 0)])
    terms = weight_terms(keep, other)
    terms = lax.all_to_all(terms, ("yl", "x"), split_axis=0, concat_axis=0, tiled=True)

    dx, terms = lax.optimization_barrier((dx, terms))
    dx = lax.all_to_all(dx, "yh", split_axis=0, concat_axis=0, tiled=True)
    input_grad = jnp.sum(dx.astype(F32), axis=0).astype(BF16)
    weight_grad = jnp.sum(terms.astype(F32), axis=0)
    return input_grad, weight_grad


def solution(mesh):
    fine = Mesh(mesh.devices.reshape(tuple(SIZES.values())), tuple(SIZES))
    return jax.shard_map(
        local,
        mesh=fine,
        in_specs=(P(ROW, COL), P(ROW, COL), P(None, ROW, COL), P(None, ROW, COL)),
        out_specs=(P(ROW, COL), P(None, ROW, COL)),
        check_vma=False,
    )
```

```python
import jax
import jax.numpy as jnp
from jax import lax
from jax.experimental import pallas as pl
from jax.experimental.pallas import tpu as pltpu
from jax.sharding import Mesh, PartitionSpec as P

F32 = jnp.float32
BF16 = jnp.bfloat16
ROW = ("yl", "x", "core")
Z = ("zh", "zl")
COL = ("yh",) + Z
SIZES = {"yl": 2, "x": 4, "core": 2, "yh": 4, "zh": 4, "zl": 2}
N_ROW, N_YH, N_Z = 16, 4, 8
HALF = N_ROW // 2
TOK = 128
VMEM_LIMIT = 56 * 1024 * 1024
WHOLE = pl.BlockSpec(memory_space=pltpu.VMEM)
SCALARS = pl.BlockSpec(memory_space=pltpu.SMEM)


def dot(a, b, dims):
    return lax.dot_general(a, b, (dims, ((), ())), preferred_element_type=F32)


def gather_by_swap(block, axis, size):
    copies = jnp.broadcast_to(block[None], (size,) + block.shape)
    return lax.all_to_all(copies, axis, split_axis=0, concat_axis=0, tiled=True)


def forward_kernel(place_ref, even_ref, x_ref, dy_ref, w_ref, keep_ref, send_ref, dx_ref):
    core, first = place_ref[0], place_ref[1] == 0
    gate = jnp.zeros((TOK, 256), F32)
    up = jnp.zeros((TOK, 256), F32)
    hidden_grad = jnp.zeros((TOK, 256), F32)
    for side in range(2):
        parity = core if side == 0 else 1 - core
        for q in range(HALF):
            y, zh = q // 2, (q % 2) * 2 + parity
            r = 2 * q + parity
            both = []
            for p, other_ref in enumerate((x_ref, dy_ref)):
                mine, other = even_ref[zh, y, p], other_ref[zh, y]
                low = jnp.where(first, mine, other)
                high = jnp.where(first, other, mine)
                both.append(jnp.concatenate([low, high], axis=1))
                if side == 0:
                    keep_ref[2 * q + p] = both[p]
                else:
                    send_ref[2 * q + p] = both[p]
            gate += dot(both[0], w_ref[r, 0], ((1,), (0,)))
            up += dot(both[0], w_ref[r, 1], ((1,), (0,)))
            hidden_grad += dot(both[1], w_ref[r, 2], ((1,), (0,)))
    sig = 1.0 / (1.0 + jnp.exp(-gate))
    act = gate * sig
    gate_grad = (hidden_grad * up * sig * (1.0 + gate * (1.0 - sig))).astype(BF16)
    up_grad = (hidden_grad * act).astype(BF16)
    hidden = (act * up).astype(BF16)
    for p, value in enumerate((gate_grad, up_grad, hidden)):
        keep_ref[N_ROW + p] = value
        send_ref[N_ROW + p] = value
    for r in range(N_ROW):
        dx = dot(gate_grad, w_ref[r, 0], ((1,), (1,))) + dot(up_grad, w_ref[r, 1], ((1,), (1,)))
        dx = dx.astype(BF16)
        dx_ref[2 * r] = dx[:, :128]
        dx_ref[2 * r + 1] = dx[:, 128:]


def forward(place, *arrays):
    pack = jax.ShapeDtypeStruct((N_ROW + 3, TOK, 256), BF16)
    return pl.pallas_call(
        forward_kernel,
        out_shape=(pack, pack, jax.ShapeDtypeStruct((N_YH * N_Z, TOK, 128), BF16)),
        in_specs=[SCALARS] + [WHOLE] * 4,
        out_specs=(WHOLE,) * 3,
        compiler_params=pltpu.CompilerParams(vmem_limit_bytes=VMEM_LIMIT),
        cost_estimate=pl.CostEstimate(flops=1400000000, bytes_accessed=10000000, transcendentals=32768),
        name="forward",
    )(place, *arrays)


def weight_kernel(mine_ref, other_ref, top_ref, low_ref):
    grads = [
        jnp.concatenate([mine_ref[N_ROW + p], other_ref[N_ROW + p]], axis=0) for p in range(3)
    ]
    for q in range(HALF):
        x = jnp.concatenate([mine_ref[2 * q], other_ref[2 * q]], axis=0)
        dy = jnp.concatenate([mine_ref[2 * q + 1], other_ref[2 * q + 1]], axis=0)
        for p in range(3):
            term = dot(dy if p == 2 else x, grads[p], ((0,), (0,)))
            term = term.astype(BF16)
            top_ref[q, p] = term[:TOK]
            low_ref[q, p] = term[TOK:]


def weight_terms(mine, other):
    rows = jax.ShapeDtypeStruct((HALF, 3, TOK, 256), BF16)
    return pl.pallas_call(
        weight_kernel,
        out_shape=(rows, rows),
        in_specs=[WHOLE] * 2,
        out_specs=(WHOLE, WHOLE),
        compiler_params=pltpu.CompilerParams(vmem_limit_bytes=VMEM_LIMIT),
        cost_estimate=pl.CostEstimate(flops=800000000, bytes_accessed=6000000, transcendentals=0),
        name="weight_terms",
    )(mine, other)


def local(inputs, out_grad, codes, scales):
    place = jnp.stack([lax.axis_index("core"), lax.axis_index("zl")])
    weights = (codes.astype(F32) * scales.astype(F32)).astype(BF16)
    weights = lax.all_gather(weights, ROW, axis=0, tiled=False)

    even = gather_by_swap(jnp.stack([inputs, out_grad]), "yh", N_YH)
    even = gather_by_swap(even, "zh", 4)
    x = lax.ppermute(even[:, :, 0], Z, [(i, (i - 1) % N_Z) for i in range(N_Z)])
    dy = lax.ppermute(even[:, :, 1], Z, [(i, (i + 1) % N_Z) for i in range(N_Z)])

    keep, send, dx = forward(place, even, x, dy, weights)
    dx = lax.all_to_all(dx, COL, split_axis=0, concat_axis=0, tiled=True)
    input_grad = jnp.sum(dx.astype(F32), axis=0).astype(BF16)

    other = lax.ppermute(send, "core", [(0, 1), (1, 0)])
    top, low = weight_terms(keep, other)
    low = lax.psum_scatter(low, ("yl", "x"), scatter_dimension=0, tiled=False)
    top = lax.all_to_all(top, ("yl", "x"), split_axis=0, concat_axis=0, tiled=True)
    top = jnp.sum(top.astype(F32), axis=0)
    return input_grad, jnp.concatenate([top, low.astype(F32)], axis=1)


def solution(mesh):
    fine = Mesh(mesh.devices.reshape(tuple(SIZES.values())), tuple(SIZES))
    return jax.shard_map(
        local,
        mesh=fine,
        in_specs=(P(ROW, COL), P(ROW, COL), P(None, ROW, COL), P(None, ROW, COL)),
        out_specs=(P(ROW, COL), P(None, ROW, COL)),
        check_vma=False,
    )
```

```python
import jax
import jax.numpy as jnp
from jax import lax
from jax.experimental import pallas as pl
from jax.experimental.pallas import tpu as pltpu
from jax.sharding import Mesh, PartitionSpec as P

F32 = jnp.float32
BF16 = jnp.bfloat16
ROW = ("yl", "x", "core")
Z = ("zh", "zl")
COL = ("yh",) + Z
SIZES = {"yl": 2, "x": 4, "core": 2, "yh": 4, "zh": 4, "zl": 2}
N_ROW, N_YH, N_Z = 16, 4, 8
HALF = N_ROW // 2
TOK = 128
BLOCK = 256
SIDE = HALF * BLOCK
PACK = 2 * SIDE + 3 * BLOCK
TOP = 96
FORWARD_VMEM = 49 * 1024 * 1024
WEIGHT_VMEM = 24 * 1024 * 1024
ANYWHERE = pl.BlockSpec(memory_space=pl.ANY)
SCALARS = pl.BlockSpec(memory_space=pltpu.SMEM)


def dot(a, b, dims):
    return lax.dot_general(a, b, (dims, ((), ())), preferred_element_type=F32)


def gather_by_swap(block, axis, size):
    copies = jnp.broadcast_to(block[None], (size,) + block.shape)
    return lax.all_to_all(copies, axis, split_axis=0, concat_axis=0, tiled=True)


def forward_kernel(
    place_ref, same_in, upper_in, lower_in, w_in, keep_out, send_out, dx_out,
    same_ref, upper_ref, lower_ref, w_ref, pack_ref, dx_ref, in_sems, w_sems, out_sems,
):
    core, first = place_ref[0], place_ref[1] == 0

    def row(i):
        return 2 * (i % HALF) + (core if i < HALF else 1 - core)

    loads = [
        pltpu.make_async_copy(src, dst, in_sems.at[i])
        for i, (src, dst) in enumerate(((same_in, same_ref), (upper_in, upper_ref), (lower_in, lower_ref)))
    ]
    w_loads = [
        pltpu.make_async_copy(w_in.at[row(i)], w_ref.at[:, pl.ds(i * BLOCK, BLOCK)], w_sems.at[i])
        for i in range(N_ROW)
    ]
    for load in loads + w_loads:
        load.start()
    for load in loads:
        load.wait()
    sums = [jnp.zeros((TOK, BLOCK), F32) for _ in range(3)]
    stores = []
    for side in range(2):
        parity = core if side == 0 else 1 - core
        for half in range(2):
            for q in range(4 * half, 4 * half + 4):
                y, zh = q // 2, (q % 2) * 2 + parity
                other_ref = lower_ref if q % 2 else upper_ref
                for p in range(2):
                    mine, other = same_ref[zh, y, p], other_ref[parity, y, p]
                    low = jnp.where(first, mine, other)
                    high = jnp.where(first, other, mine)
                    at = p * SIDE + q * BLOCK
                    pack_ref[side, :, pl.ds(at, BLOCK)] = jnp.concatenate([low, high], axis=1)
                w_loads[side * HALF + q].wait()
            rows = pl.ds((side * 2 + half) * 4 * BLOCK, 4 * BLOCK)
            x = pack_ref[side, :, pl.ds(half * 4 * BLOCK, 4 * BLOCK)]
            dy = pack_ref[side, :, pl.ds(SIDE + half * 4 * BLOCK, 4 * BLOCK)]
            for p in range(3):
                sums[p] += dot(dy if p == 2 else x, w_ref[p, rows], ((1,), (0,)))
        out = keep_out if side == 0 else send_out
        cols = pl.ds(0, 2 * SIDE)
        stores.append(
            pltpu.make_async_copy(pack_ref.at[side, :, cols], out.at[:, cols], out_sems.at[side])
        )
        stores[-1].start()
    gate, up, hidden_grad = sums
    sig = 1.0 / (1.0 + jnp.exp(-gate))
    act = gate * sig
    gate_grad = (hidden_grad * up * sig * (1.0 + gate * (1.0 - sig))).astype(BF16)
    up_grad = (hidden_grad * act).astype(BF16)
    hidden = (act * up).astype(BF16)
    for side in range(2):
        for p, value in enumerate((gate_grad, up_grad, hidden)):
            pack_ref[side, :, pl.ds(2 * SIDE + p * BLOCK, BLOCK)] = value
        out = keep_out if side == 0 else send_out
        cols = pl.ds(2 * SIDE, 3 * BLOCK)
        stores.append(
            pltpu.make_async_copy(pack_ref.at[side, :, cols], out.at[:, cols], out_sems.at[2 + side])
        )
        stores[-1].start()
    for i in range(N_ROW):
        q, parity = i % HALF, (core if i < HALF else 1 - core)
        rows = pl.ds(i * BLOCK, BLOCK)
        dx = dot(gate_grad, w_ref[0, rows], ((1,), (1,)))
        dx = (dx + dot(up_grad, w_ref[1, rows], ((1,), (1,)))).astype(BF16)
        y, z = q // 2, 4 * (q % 2) + 2 * parity
        dx_ref[z, y] = dx[:, :TOK]
        dx_ref[z + 1, y] = dx[:, TOK:]
    stores.append(pltpu.make_async_copy(dx_ref, dx_out, out_sems.at[4]))
    stores[-1].start()
    for store in stores:
        store.wait()


def forward(place, same, upper, lower, weights):
    pack = jax.ShapeDtypeStruct((TOK, PACK), BF16)
    return pl.pallas_call(
        forward_kernel,
        out_shape=(pack, pack, jax.ShapeDtypeStruct((N_Z, N_YH, TOK, 128), BF16)),
        in_specs=[SCALARS] + [ANYWHERE] * 4,
        out_specs=(ANYWHERE,) * 3,
        scratch_shapes=[
            pltpu.VMEM(same.shape, BF16),
            pltpu.VMEM(upper.shape, BF16),
            pltpu.VMEM(lower.shape, BF16),
            pltpu.VMEM((3, N_ROW * BLOCK, BLOCK), BF16),
            pltpu.VMEM((2, TOK, PACK), BF16),
            pltpu.VMEM((N_Z, N_YH, TOK, 128), BF16),
            pltpu.SemaphoreType.DMA((3,)),
            pltpu.SemaphoreType.DMA((N_ROW,)),
            pltpu.SemaphoreType.DMA((5,)),
        ],
        compiler_params=pltpu.CompilerParams(vmem_limit_bytes=FORWARD_VMEM),
        cost_estimate=pl.CostEstimate(flops=1400000000, bytes_accessed=10000000, transcendentals=32768),
        name="forward",
    )(place, same, upper, lower, weights)


def weight_kernel(mine_in, other_in, top_out, low_out, both_ref, terms_ref, in_sems, out_sems):
    loads = [
        pltpu.make_async_copy(src, both_ref.at[pl.ds(i * TOK, TOK)], in_sems.at[i])
        for i, src in enumerate((mine_in, other_in))
    ]
    for load in loads:
        load.start()
    for load in loads:
        load.wait()
    stores = []
    for q in range(HALF):
        x = both_ref[:, pl.ds(q * BLOCK, BLOCK)]
        dy = both_ref[:, pl.ds(SIDE + q * BLOCK, BLOCK)]
        gate_up = dot(x, both_ref[:, pl.ds(2 * SIDE, 2 * BLOCK)], ((0,), (0,)))
        down = dot(dy, both_ref[:, pl.ds(2 * SIDE + 2 * BLOCK, BLOCK)], ((0,), (0,)))
        terms_ref[q, 0] = gate_up[:, :BLOCK].astype(BF16)
        terms_ref[q, 1] = gate_up[:, BLOCK:].astype(BF16)
        terms_ref[q, 2] = down.astype(BF16)
        for i, (out, rows) in enumerate(((top_out, pl.ds(0, TOP)), (low_out, pl.ds(TOP, BLOCK - TOP)))):
            stores.append(
                pltpu.make_async_copy(terms_ref.at[q, :, rows], out.at[q], out_sems.at[2 * q + i])
            )
            stores[-1].start()
    for store in stores:
        store.wait()


def weight_terms(mine, other):
    return pl.pallas_call(
        weight_kernel,
        out_shape=(
            jax.ShapeDtypeStruct((HALF, 3, TOP, BLOCK), BF16),
            jax.ShapeDtypeStruct((HALF, 3, BLOCK - TOP, BLOCK), BF16),
        ),
        in_specs=[ANYWHERE] * 2,
        out_specs=(ANYWHERE,) * 2,
        scratch_shapes=[
            pltpu.VMEM((2 * TOK, PACK), BF16),
            pltpu.VMEM((HALF, 3, BLOCK, BLOCK), BF16),
            pltpu.SemaphoreType.DMA((2,)),
            pltpu.SemaphoreType.DMA((2 * HALF,)),
        ],
        compiler_params=pltpu.CompilerParams(vmem_limit_bytes=WEIGHT_VMEM),
        cost_estimate=pl.CostEstimate(flops=800000000, bytes_accessed=6000000, transcendentals=0),
        name="weight_terms",
    )(mine, other)


def local(inputs, out_grad, codes, scales):
    place = jnp.stack([lax.axis_index("core"), lax.axis_index("zl")])
    acts = jnp.broadcast_to(jnp.stack([inputs, out_grad])[None], (N_YH, 2, TOK, 128))
    acts, codes = lax.optimization_barrier((acts, codes))
    acts = lax.all_to_all(acts, "yh", split_axis=0, concat_axis=0, tiled=True)

    weights = (codes.astype(F32) * scales.astype(F32)).astype(BF16)
    weights = lax.all_gather(weights, ROW, axis=0, tiled=False)

    same = gather_by_swap(acts, "zh", 4)
    upper = lax.ppermute(same[:2], Z, [(i, (i - 1) % N_Z) for i in range(N_Z)])
    lower = lax.ppermute(same[2:], Z, [(i, (i + 1) % N_Z) for i in range(N_Z)])

    keep, send, dx = forward(place, same, upper, lower, weights)
    dx = lax.all_to_all(dx, Z, split_axis=0, concat_axis=0, tiled=True)
    dx = jnp.sum(dx.astype(F32), axis=0).astype(BF16)
    dx = lax.all_to_all(dx, "yh", split_axis=0, concat_axis=0, tiled=True)
    input_grad = jnp.sum(dx.astype(F32), axis=0).astype(BF16)

    other = lax.ppermute(send, "core", [(0, 1), (1, 0)])
    top, low = weight_terms(keep, other)
    low = lax.psum_scatter(low, ("yl", "x"), scatter_dimension=0, tiled=False)
    top = lax.all_to_all(top, ("yl", "x"), split_axis=0, concat_axis=0, tiled=True)
    top = jnp.sum(top.astype(F32), axis=0)
    return input_grad, jnp.concatenate([top, low.astype(F32)], axis=1)


def solution(mesh):
    fine = Mesh(mesh.devices.reshape(tuple(SIZES.values())), tuple(SIZES))
    return jax.shard_map(
        local,
        mesh=fine,
        in_specs=(P(ROW, COL), P(ROW, COL), P(None, ROW, COL), P(None, ROW, COL)),
        out_specs=(P(ROW, COL), P(None, ROW, COL)),
        check_vma=False,
    )
```

```python
import jax
import jax.numpy as jnp
from jax import lax
from jax.experimental import pallas as pl
from jax.experimental.pallas import tpu as pltpu
from jax.sharding import Mesh, PartitionSpec as P

F32 = jnp.float32
BF16 = jnp.bfloat16
ROW = ("yl", "x", "core")
Z = ("zh", "zl")
COL = ("yh",) + Z
SIZES = {"yl": 2, "x": 4, "core": 2, "yh": 4, "zh": 4, "zl": 2}
N_ROW, N_YH, N_Z = 16, 4, 8
HALF = N_ROW // 2
TOK = 128
BLOCK = 256
SIDE = HALF * BLOCK
PACK = SIDE + 3 * BLOCK
FORWARD_VMEM = 49 * 1024 * 1024
WEIGHT_VMEM = 24 * 1024 * 1024
ANYWHERE = pl.BlockSpec(memory_space=pl.ANY)
SCALARS = pl.BlockSpec(memory_space=pltpu.SMEM)


def dot(a, b, dims):
    return lax.dot_general(a, b, (dims, ((), ())), preferred_element_type=F32)


def gather_by_swap(block, axis, size):
    copies = jnp.broadcast_to(block[None], (size,) + block.shape)
    return lax.all_to_all(copies, axis, split_axis=0, concat_axis=0, tiled=True)


def from_neighbours(same):
    upper = lax.ppermute(same[:2], Z, [(i, (i - 1) % N_Z) for i in range(N_Z)])
    lower = lax.ppermute(same[2:], Z, [(i, (i + 1) % N_Z) for i in range(N_Z)])
    return upper, lower


def prepare_kernel(x_ref, dy_ref, codes_ref, scales_ref, acts_ref, weights_ref):
    for y in range(N_YH):
        acts_ref[y, 0] = x_ref[...]
        acts_ref[y, 1] = dy_ref[...]
    weights_ref[...] = (codes_ref[...].astype(F32) * scales_ref[...].astype(F32)).astype(BF16)


def prepare(x, dy, codes, scales):
    whole = pl.BlockSpec(memory_space=pltpu.VMEM)
    return pl.pallas_call(
        prepare_kernel,
        out_shape=(
            jax.ShapeDtypeStruct((N_YH, 2, TOK, 128), BF16),
            jax.ShapeDtypeStruct(codes.shape, BF16),
        ),
        in_specs=[whole] * 4,
        out_specs=(whole,) * 2,
        compiler_params=pltpu.CompilerParams(vmem_limit_bytes=WEIGHT_VMEM),
        cost_estimate=pl.CostEstimate(flops=200000, bytes_accessed=1200000, transcendentals=0),
        name="prepare",
    )(x, dy, codes, scales)


def load_acts(same_in, upper_in, lower_in, same_ref, upper_ref, lower_ref, sems):
    loads = [
        pltpu.make_async_copy(src, dst, sems.at[i])
        for i, (src, dst) in enumerate(
            ((same_in, same_ref), (upper_in, upper_ref), (lower_in, lower_ref))
        )
    ]
    for load in loads:
        load.start()
    return loads


def load_weights(core, first, count, w_in, w_ref, sems):
    loads = []
    for i in range(N_ROW):
        r = 2 * (i % HALF) + (core if i < HALF else 1 - core)
        src = w_in.at[r, pl.ds(first, count)]
        dst = w_ref.at[pl.ds(first, count), pl.ds(i * BLOCK, BLOCK)]
        loads.append(pltpu.make_async_copy(src, dst, sems.at[i]))
        loads[-1].start()
    return loads


def widen(place_ref, side, q, same_ref, upper_ref, lower_ref):
    core, first = place_ref[0], place_ref[1] == 0
    parity = core if side == 0 else 1 - core
    y, zh = q // 2, (q % 2) * 2 + parity
    mine, other = same_ref[zh, y], (lower_ref if q % 2 else upper_ref)[parity, y]
    return jnp.concatenate([jnp.where(first, mine, other), jnp.where(first, other, mine)], axis=1)


def gates_kernel(
    place_ref, same_in, upper_in, lower_in, w_in, keep_out, send_out, gate_out,
    same_ref, upper_ref, lower_ref, w_ref, acts_ref, gate_ref, in_sems, w_sems, out_sems,
):
    loads = load_acts(same_in, upper_in, lower_in, same_ref, upper_ref, lower_ref, in_sems)
    w_loads = load_weights(place_ref[0], 0, 2, w_in, w_ref, w_sems)
    for load in loads:
        load.wait()
    sums = [jnp.zeros((TOK, BLOCK), F32) for _ in range(2)]
    stores = []
    for side in range(2):
        for half in range(2):
            for q in range(4 * half, 4 * half + 4):
                wide = widen(place_ref, side, q, same_ref, upper_ref, lower_ref)
                acts_ref[side, :, pl.ds(q * BLOCK, BLOCK)] = wide
                w_loads[side * HALF + q].wait()
            rows = pl.ds((side * 2 + half) * 4 * BLOCK, 4 * BLOCK)
            x = acts_ref[side, :, pl.ds(half * 4 * BLOCK, 4 * BLOCK)]
            for p in range(2):
                sums[p] += dot(x, w_ref[p, rows], ((1,), (0,)))
        out = keep_out if side == 0 else send_out
        stores.append(pltpu.make_async_copy(acts_ref.at[side], out, out_sems.at[side]))
        stores[-1].start()
    for p in range(2):
        gate_ref[p] = sums[p]
    stores.append(pltpu.make_async_copy(gate_ref, gate_out, out_sems.at[2]))
    stores[-1].start()
    for store in stores:
        store.wait()


def gates(place, same, upper, lower, weights):
    acts = jax.ShapeDtypeStruct((TOK, SIDE), BF16)
    return pl.pallas_call(
        gates_kernel,
        out_shape=(acts, acts, jax.ShapeDtypeStruct((2, TOK, BLOCK), F32)),
        in_specs=[SCALARS] + [ANYWHERE] * 4,
        out_specs=(ANYWHERE,) * 3,
        scratch_shapes=[
            pltpu.VMEM(same.shape, BF16),
            pltpu.VMEM(upper.shape, BF16),
            pltpu.VMEM(lower.shape, BF16),
            pltpu.VMEM((2, N_ROW * BLOCK, BLOCK), BF16),
            pltpu.VMEM((2, TOK, SIDE), BF16),
            pltpu.VMEM((2, TOK, BLOCK), F32),
            pltpu.SemaphoreType.DMA((3,)),
            pltpu.SemaphoreType.DMA((N_ROW,)),
            pltpu.SemaphoreType.DMA((3,)),
        ],
        compiler_params=pltpu.CompilerParams(vmem_limit_bytes=FORWARD_VMEM),
        cost_estimate=pl.CostEstimate(flops=540000000, bytes_accessed=6000000, transcendentals=0),
        name="gates",
    )(place, same, upper, lower, weights)


def hidden_kernel(
    place_ref, same_in, upper_in, lower_in, w_in, gate_in, keep_out, send_out, dx_out,
    same_ref, upper_ref, lower_ref, w_ref, gate_ref, pack_ref, dx_ref, in_sems, w_sems, w_sems2, out_sems,
):
    core = place_ref[0]
    loads = load_acts(same_in, upper_in, lower_in, same_ref, upper_ref, lower_ref, in_sems)
    loads.append(pltpu.make_async_copy(gate_in, gate_ref, in_sems.at[3]))
    loads[-1].start()
    w_loads = load_weights(core, 2, 1, w_in, w_ref, w_sems)
    w_loads2 = load_weights(core, 0, 2, w_in, w_ref, w_sems2)
    for load in loads:
        load.wait()
    hidden_grad = jnp.zeros((TOK, BLOCK), F32)
    stores = []
    for side in range(2):
        for half in range(2):
            for q in range(4 * half, 4 * half + 4):
                wide = widen(place_ref, side, q, same_ref, upper_ref, lower_ref)
                pack_ref[side, :, pl.ds(q * BLOCK, BLOCK)] = wide
                w_loads[side * HALF + q].wait()
            rows = pl.ds((side * 2 + half) * 4 * BLOCK, 4 * BLOCK)
            dy = pack_ref[side, :, pl.ds(half * 4 * BLOCK, 4 * BLOCK)]
            hidden_grad += dot(dy, w_ref[2, rows], ((1,), (0,)))
        out, cols = (keep_out if side == 0 else send_out), pl.ds(0, SIDE)
        stores.append(
            pltpu.make_async_copy(pack_ref.at[side, :, cols], out.at[:, cols], out_sems.at[side])
        )
        stores[-1].start()
    gate, up = gate_ref[0], gate_ref[1]
    sig = 1.0 / (1.0 + jnp.exp(-gate))
    act = gate * sig
    gate_grad = (hidden_grad * up * sig * (1.0 + gate * (1.0 - sig))).astype(BF16)
    up_grad = (hidden_grad * act).astype(BF16)
    hidden = (act * up).astype(BF16)
    for side in range(2):
        for p, value in enumerate((gate_grad, up_grad, hidden)):
            pack_ref[side, :, pl.ds(SIDE + p * BLOCK, BLOCK)] = value
        out, cols = (keep_out if side == 0 else send_out), pl.ds(SIDE, 3 * BLOCK)
        stores.append(
            pltpu.make_async_copy(pack_ref.at[side, :, cols], out.at[:, cols], out_sems.at[2 + side])
        )
        stores[-1].start()
    for i in range(N_ROW):
        q, parity = i % HALF, (core if i < HALF else 1 - core)
        rows = pl.ds(i * BLOCK, BLOCK)
        w_loads2[i].wait()
        dx = dot(gate_grad, w_ref[0, rows], ((1,), (1,)))
        dx = (dx + dot(up_grad, w_ref[1, rows], ((1,), (1,)))).astype(BF16)
        y, z = q // 2, 4 * (q % 2) + 2 * parity
        dx_ref[z, y] = dx[:, :TOK]
        dx_ref[z + 1, y] = dx[:, TOK:]
    stores.append(pltpu.make_async_copy(dx_ref, dx_out, out_sems.at[4]))
    stores[-1].start()
    for store in stores:
        store.wait()


def hidden_grads(place, same, upper, lower, weights, gate):
    pack = jax.ShapeDtypeStruct((TOK, PACK), BF16)
    return pl.pallas_call(
        hidden_kernel,
        out_shape=(pack, pack, jax.ShapeDtypeStruct((N_Z, N_YH, TOK, 128), BF16)),
        in_specs=[SCALARS] + [ANYWHERE] * 5,
        out_specs=(ANYWHERE,) * 3,
        scratch_shapes=[
            pltpu.VMEM(same.shape, BF16),
            pltpu.VMEM(upper.shape, BF16),
            pltpu.VMEM(lower.shape, BF16),
            pltpu.VMEM((3, N_ROW * BLOCK, BLOCK), BF16),
            pltpu.VMEM((2, TOK, BLOCK), F32),
            pltpu.VMEM((2, TOK, PACK), BF16),
            pltpu.VMEM((N_Z, N_YH, TOK, 128), BF16),
            pltpu.SemaphoreType.DMA((4,)),
            pltpu.SemaphoreType.DMA((N_ROW,)),
            pltpu.SemaphoreType.DMA((N_ROW,)),
            pltpu.SemaphoreType.DMA((5,)),
        ],
        compiler_params=pltpu.CompilerParams(vmem_limit_bytes=FORWARD_VMEM),
        cost_estimate=pl.CostEstimate(flops=800000000, bytes_accessed=9000000, transcendentals=32768),
        name="hidden_grads",
    )(place, same, upper, lower, weights, gate)


def weight_kernel(
    x_in, other_x_in, pack_in, other_pack_in, out, x_ref, pack_ref, terms_ref, in_sems, out_sems
):
    loads = []
    for i, (src, dst) in enumerate(
        ((x_in, x_ref), (other_x_in, x_ref), (pack_in, pack_ref), (other_pack_in, pack_ref))
    ):
        rows = pl.ds((i % 2) * TOK, TOK)
        loads.append(pltpu.make_async_copy(src, dst.at[rows], in_sems.at[i]))
        loads[-1].start()
    for load in loads:
        load.wait()
    stores = []
    for q in range(HALF):
        cols = pl.ds(q * BLOCK, BLOCK)
        gate_up = dot(x_ref[:, cols], pack_ref[:, pl.ds(SIDE, 2 * BLOCK)], ((0,), (0,)))
        down = dot(pack_ref[:, cols], pack_ref[:, pl.ds(SIDE + 2 * BLOCK, BLOCK)], ((0,), (0,)))
        terms_ref[q, 0] = gate_up[:, :BLOCK].astype(BF16)
        terms_ref[q, 1] = gate_up[:, BLOCK:].astype(BF16)
        terms_ref[q, 2] = down.astype(BF16)
        stores.append(pltpu.make_async_copy(terms_ref.at[q], out.at[q], out_sems.at[q]))
        stores[-1].start()
    for store in stores:
        store.wait()


def weight_terms(x, other_x, pack, other_pack):
    return pl.pallas_call(
        weight_kernel,
        out_shape=jax.ShapeDtypeStruct((HALF, 3, BLOCK, BLOCK), BF16),
        in_specs=[ANYWHERE] * 4,
        out_specs=ANYWHERE,
        scratch_shapes=[
            pltpu.VMEM((2 * TOK, SIDE), BF16),
            pltpu.VMEM((2 * TOK, PACK), BF16),
            pltpu.VMEM((HALF, 3, BLOCK, BLOCK), BF16),
            pltpu.SemaphoreType.DMA((4,)),
            pltpu.SemaphoreType.DMA((HALF,)),
        ],
        compiler_params=pltpu.CompilerParams(vmem_limit_bytes=WEIGHT_VMEM),
        cost_estimate=pl.CostEstimate(flops=800000000, bytes_accessed=6000000, transcendentals=0),
        name="weight_terms",
    )(x, other_x, pack, other_pack)


def local(inputs, out_grad, codes, scales):
    place = jnp.stack([lax.axis_index("core"), lax.axis_index("zl")])
    swap = [(0, 1), (1, 0)]
    acts, weights = prepare(inputs, out_grad, codes, scales)
    weights = lax.all_gather(weights, ROW, axis=0, tiled=False)

    acts = lax.all_to_all(acts, "yh", split_axis=0, concat_axis=0, tiled=True)
    x = gather_by_swap(acts[:, 0], "zh", 4)
    x_upper, x_lower = from_neighbours(x)
    dy = gather_by_swap(acts[:, 1], "zh", 4)
    dy_upper, dy_lower = from_neighbours(dy)

    keep_x, send_x, gate = gates(place, x, x_upper, x_lower, weights)
    other_x = lax.ppermute(send_x, "core", swap)
    keep, send, dx = hidden_grads(place, dy, dy_upper, dy_lower, weights, gate)
    other = lax.ppermute(send, "core", swap)
    terms = weight_terms(keep_x, other_x, keep, other)
    terms = lax.psum_scatter(terms, ("yl", "x"), scatter_dimension=0, tiled=False)

    dx = lax.all_to_all(dx, Z, split_axis=0, concat_axis=0, tiled=True)
    dx = jnp.sum(dx.astype(F32), axis=0).astype(BF16)
    dx = lax.all_to_all(dx, "yh", split_axis=0, concat_axis=0, tiled=True)
    input_grad = jnp.sum(dx.astype(F32), axis=0).astype(BF16)
    return input_grad, terms.astype(F32)


def solution(mesh):
    fine = Mesh(mesh.devices.reshape(tuple(SIZES.values())), tuple(SIZES))
    return jax.shard_map(
        local,
        mesh=fine,
        in_specs=(P(ROW, COL), P(ROW, COL), P(None, ROW, COL), P(None, ROW, COL)),
        out_specs=(P(ROW, COL), P(None, ROW, COL)),
        check_vma=False,
    )
```

```python
import jax
import jax.numpy as jnp
from jax import lax
from jax.experimental import pallas as pl
from jax.experimental.pallas import tpu as pltpu
from jax.sharding import Mesh, PartitionSpec as P

F32 = jnp.float32
BF16 = jnp.bfloat16
ROW = ("yl", "x", "core")
Z = ("zh", "zl")
COL = ("yh",) + Z
SIZES = {"yl": 2, "x": 4, "core": 2, "yh": 4, "zh": 4, "zl": 2}
N_ROW, N_YH, N_Z = 16, 4, 8
HALF = N_ROW // 2
TOK = 128
BLOCK = 256
SIDE = HALF * BLOCK
SMALL_VMEM = 24 * 1024 * 1024
LARGE_VMEM = 50 * 1024 * 1024
ANYWHERE = pl.BlockSpec(memory_space=pl.ANY)
SCALARS = pl.BlockSpec(memory_space=pltpu.SMEM)


def dot(a, b, dims):
    return lax.dot_general(a, b, (dims, ((), ())), preferred_element_type=F32)


def gather_by_swap(block, axis, size):
    copies = jnp.broadcast_to(block[None], (size,) + block.shape)
    return lax.all_to_all(copies, axis, split_axis=0, concat_axis=0, tiled=True)


def arrange_kernel(place_ref, acts_in, keep_out, send_out, sems):
    copies = []
    for side, out in enumerate((keep_out, send_out)):
        parity = place_ref[0] if side == 0 else 1 - place_ref[0]
        for q in range(HALF):
            y, z = q // 2, 4 * (q % 2) + 2 * parity
            for p in range(2):
                for b in range(2):
                    at = p * SIDE + q * BLOCK + b * TOK
                    copies.append(
                        pltpu.make_async_copy(
                            acts_in.at[z + b, y, p], out.at[:, pl.ds(at, TOK)], sems.at[len(copies)]
                        )
                    )
                    copies[-1].start()
    for copy in copies:
        copy.wait()


def arrange(place, acts):
    side = jax.ShapeDtypeStruct((TOK, 2 * SIDE), BF16)
    return pl.pallas_call(
        arrange_kernel,
        out_shape=(side, side),
        in_specs=[SCALARS, ANYWHERE],
        out_specs=(ANYWHERE,) * 2,
        scratch_shapes=[pltpu.SemaphoreType.DMA((2 * HALF * 4,))],
        compiler_params=pltpu.CompilerParams(vmem_limit_bytes=LARGE_VMEM),
        cost_estimate=pl.CostEstimate(flops=1000000, bytes_accessed=4000000, transcendentals=0),
        name="arrange",
    )(place, acts)


def forward_kernel(
    place_ref, keep_in, send_in, w_in, other_w_in, grads_out, dx_out,
    acts_ref, w_ref, grads_ref, dx_ref, in_sems, w_sems, out_sems,
):
    core = place_ref[0]
    loads = [
        pltpu.make_async_copy(src, acts_ref.at[side], in_sems.at[side])
        for side, src in enumerate((keep_in, send_in))
    ]
    w_loads = [
        pltpu.make_async_copy(
            (w_in if i < HALF else other_w_in).at[i % HALF],
            w_ref.at[:, pl.ds(i * BLOCK, BLOCK)],
            w_sems.at[i],
        )
        for i in range(N_ROW)
    ]
    for load in loads + w_loads:
        load.start()
    sums = [jnp.zeros((TOK, BLOCK), F32) for _ in range(3)]
    for side in range(2):
        loads[side].wait()
        for half in range(2):
            for q in range(4 * half, 4 * half + 4):
                w_loads[side * HALF + q].wait()
            rows = pl.ds((side * 2 + half) * 4 * BLOCK, 4 * BLOCK)
            x = acts_ref[side, :, pl.ds(half * 4 * BLOCK, 4 * BLOCK)]
            dy = acts_ref[side, :, pl.ds(SIDE + half * 4 * BLOCK, 4 * BLOCK)]
            for p in range(3):
                sums[p] += dot(dy if p == 2 else x, w_ref[p, rows], ((1,), (0,)))
    gate, up, hidden_grad = sums
    sig = 1.0 / (1.0 + jnp.exp(-gate))
    act = gate * sig
    gate_grad = (hidden_grad * up * sig * (1.0 + gate * (1.0 - sig))).astype(BF16)
    up_grad = (hidden_grad * act).astype(BF16)
    hidden = (act * up).astype(BF16)
    for p, value in enumerate((gate_grad, up_grad, hidden)):
        grads_ref[:, pl.ds(p * BLOCK, BLOCK)] = value
    stores = [pltpu.make_async_copy(grads_ref, grads_out, out_sems.at[0])]
    stores[-1].start()
    for i in range(N_ROW):
        q, parity = i % HALF, (core if i < HALF else 1 - core)
        rows = pl.ds(i * BLOCK, BLOCK)
        dx = dot(gate_grad, w_ref[0, rows], ((1,), (1,)))
        dx = (dx + dot(up_grad, w_ref[1, rows], ((1,), (1,)))).astype(BF16)
        y, z = q // 2, 4 * (q % 2) + 2 * parity
        dx_ref[z, y] = dx[:, :TOK]
        dx_ref[z + 1, y] = dx[:, TOK:]
    stores.append(pltpu.make_async_copy(dx_ref, dx_out, out_sems.at[1]))
    stores[-1].start()
    for store in stores:
        store.wait()


def forward(place, keep, send, weights, other_weights):
    return pl.pallas_call(
        forward_kernel,
        out_shape=(
            jax.ShapeDtypeStruct((TOK, 3 * BLOCK), BF16),
            jax.ShapeDtypeStruct((N_Z, N_YH, TOK, 128), BF16),
        ),
        in_specs=[SCALARS] + [ANYWHERE] * 4,
        out_specs=(ANYWHERE,) * 2,
        scratch_shapes=[
            pltpu.VMEM((2, TOK, 2 * SIDE), BF16),
            pltpu.VMEM((3, N_ROW * BLOCK, BLOCK), BF16),
            pltpu.VMEM((TOK, 3 * BLOCK), BF16),
            pltpu.VMEM((N_Z, N_YH, TOK, 128), BF16),
            pltpu.SemaphoreType.DMA((2,)),
            pltpu.SemaphoreType.DMA((N_ROW,)),
            pltpu.SemaphoreType.DMA((2,)),
        ],
        compiler_params=pltpu.CompilerParams(vmem_limit_bytes=SMALL_VMEM),
        cost_estimate=pl.CostEstimate(flops=1400000000, bytes_accessed=10000000, transcendentals=32768),
        name="forward",
    )(place, keep, send, weights, other_weights)


def weight_kernel(
    acts_in, other_acts_in, grads_in, other_grads_in, out, acts_ref, grads_ref, terms_ref, in_sems, out_sems
):
    loads = []
    for i, (src, dst) in enumerate(
        ((acts_in, acts_ref), (other_acts_in, acts_ref), (grads_in, grads_ref), (other_grads_in, grads_ref))
    ):
        rows = pl.ds((i % 2) * TOK, TOK)
        loads.append(pltpu.make_async_copy(src, dst.at[rows], in_sems.at[i]))
        loads[-1].start()
    for load in loads:
        load.wait()
    stores = []
    for q in range(HALF):
        x = acts_ref[:, pl.ds(q * BLOCK, BLOCK)]
        dy = acts_ref[:, pl.ds(SIDE + q * BLOCK, BLOCK)]
        gate_up = dot(x, grads_ref[:, pl.ds(0, 2 * BLOCK)], ((0,), (0,)))
        down = dot(dy, grads_ref[:, pl.ds(2 * BLOCK, BLOCK)], ((0,), (0,)))
        terms_ref[q, 0] = gate_up[:, :BLOCK].astype(BF16)
        terms_ref[q, 1] = gate_up[:, BLOCK:].astype(BF16)
        terms_ref[q, 2] = down.astype(BF16)
        stores.append(pltpu.make_async_copy(terms_ref.at[q], out.at[q], out_sems.at[q]))
        stores[-1].start()
    for store in stores:
        store.wait()


def weight_terms(acts, other_acts, grads, other_grads):
    return pl.pallas_call(
        weight_kernel,
        out_shape=jax.ShapeDtypeStruct((HALF, 3, BLOCK, BLOCK), BF16),
        in_specs=[ANYWHERE] * 4,
        out_specs=ANYWHERE,
        scratch_shapes=[
            pltpu.VMEM((2 * TOK, 2 * SIDE), BF16),
            pltpu.VMEM((2 * TOK, 3 * BLOCK), BF16),
            pltpu.VMEM((HALF, 3, BLOCK, BLOCK), BF16),
            pltpu.SemaphoreType.DMA((4,)),
            pltpu.SemaphoreType.DMA((HALF,)),
        ],
        compiler_params=pltpu.CompilerParams(vmem_limit_bytes=SMALL_VMEM),
        cost_estimate=pl.CostEstimate(flops=800000000, bytes_accessed=6000000, transcendentals=0),
        name="weight_terms",
    )(acts, other_acts, grads, other_grads)


def local(inputs, out_grad, codes, scales):
    place = lax.axis_index("core").reshape(1)
    swap = [(0, 1), (1, 0)]
    acts = gather_by_swap(jnp.stack([inputs, out_grad]), "yh", N_YH)
    acts = lax.all_gather(acts, Z, axis=0, tiled=False)

    weights = (codes.astype(F32) * scales.astype(F32)).astype(BF16)
    weights = gather_by_swap(weights, ("yl", "x"), HALF)
    other_weights = lax.ppermute(weights, "core", swap)

    keep, send = arrange(place, acts)
    other = lax.ppermute(send, "core", swap)
    grads, dx = forward(place, keep, send, weights, other_weights)
    dx = lax.all_to_all(dx, Z, split_axis=0, concat_axis=0, tiled=True)
    dx = jnp.sum(dx.astype(F32), axis=0).astype(BF16)
    dx = lax.all_to_all(dx, "yh", split_axis=0, concat_axis=0, tiled=True)
    input_grad = jnp.sum(dx.astype(F32), axis=0).astype(BF16)

    other_grads = lax.ppermute(grads, "core", swap)
    terms = weight_terms(keep, other, grads, other_grads)
    terms = lax.psum_scatter(terms, ("yl", "x"), scatter_dimension=0, tiled=False)
    return input_grad, terms.astype(F32)


def solution(mesh):
    fine = Mesh(mesh.devices.reshape(tuple(SIZES.values())), tuple(SIZES))
    return jax.shard_map(
        local,
        mesh=fine,
        in_specs=(P(ROW, COL), P(ROW, COL), P(None, ROW, COL), P(None, ROW, COL)),
        out_specs=(P(ROW, COL), P(None, ROW, COL)),
        check_vma=False,
    )
```

```python
import itertools

import jax
import jax.numpy as jnp
from jax import lax
from jax.experimental import pallas as pl
from jax.experimental.pallas import tpu as pltpu
from jax.sharding import Mesh, PartitionSpec as P

F32 = jnp.float32
BF16 = jnp.bfloat16
ROW = ("yl", "x1", "x0", "core")
COL = ("yh1", "yh0", "zh1", "zh0", "zl")
AXES = ROW + COL
SPREAD = ("yh1", "yh0", "zh1", "zh0")
REST = ("yl", "x1")
SWAP = [(0, 1), (1, 0)]
TOK = 128
BLOCK = 256
WIDE = 2 * BLOCK
HALF = 2 * TOK
SHARE = HALF // 4
GRADS = 3 * WIDE
VMEM_LIMIT = 24 * 1024 * 1024
ANYWHERE = pl.BlockSpec(memory_space=pl.ANY)
SCALARS = pl.BlockSpec(memory_space=pltpu.SMEM)


def turned():
    pairs = []
    for bits in itertools.product(range(2), repeat=len(AXES)):
        yl, x1, x0, core, yh1, yh0, zh1, zh0, zl = bits
        there = (yh1, yh0, x0, zh0, yl, x1, zh1, zl, core)
        pairs.append(tuple(sum(b << (8 - i) for i, b in enumerate(at)) for at in (bits, there)))
    return pairs


def dot(a, b, dims):
    return lax.dot_general(a, b, (dims, ((), ())), preferred_element_type=F32)


def params():
    return pltpu.CompilerParams(vmem_limit_bytes=VMEM_LIMIT)


def chunk(place_ref, i, f):
    core, x0 = place_ref[0], place_ref[1]
    t = 2 * (core if i < 2 else 1 - core) + i % 2
    return 4 * t + 2 * (x0 if f < 2 else 1 - x0) + f % 2


def load_weights(w_in, w_z_in, w_x_in, w_ref, count, sems):
    loads = []
    for i, src in enumerate((w_in, w_z_in, w_x_in.at[0], w_x_in.at[1])):
        rows, cols = pl.ds(i // 2 * BLOCK, BLOCK), pl.ds(i % 2 * BLOCK, BLOCK)
        loads.append(
            pltpu.make_async_copy(src.at[pl.ds(0, count)], w_ref.at[:, rows, cols], sems.at[i])
        )
        loads[-1].start()
    return loads


def gates_kernel(
    place_ref, acts_in, w_in, w_z_in, w_x_in, keep_out, send_out, acts_out,
    acts_ref, w_ref, keep_ref, send_ref, act_sems, w_sems, out_sems,
):
    w_loads = load_weights(w_in, w_z_in, w_x_in, w_ref, 3, w_sems)
    loads = []
    for p in range(2):
        for i in range(4):
            for f in range(4):
                src = acts_in.at[chunk(place_ref, i, f), p]
                dst = acts_ref.at[p, pl.ds(i * TOK, TOK), pl.ds(f * TOK, TOK)]
                loads.append(pltpu.make_async_copy(src, dst, act_sems.at[len(loads)]))
                loads[-1].start()
    for load in loads:
        load.wait()
    stores = [pltpu.make_async_copy(acts_ref, acts_out, out_sems.at[0])]
    stores[0].start()
    for load in w_loads:
        load.wait()
    for p in range(3):
        cols = pl.ds(p * WIDE, WIDE)
        sums = dot(acts_ref[p // 2], w_ref[p], ((1,), (0,)))
        send_ref[:, cols] = sums[HALF:].astype(BF16)
        keep_ref[:, cols] = sums[:HALF]
    for i, (src, dst) in enumerate(((send_ref, send_out), (keep_ref, keep_out))):
        stores.append(pltpu.make_async_copy(src, dst, out_sems.at[1 + i]))
        stores[-1].start()
    for store in stores:
        store.wait()


def gates(place, acts, w, w_z, w_x):
    return pl.pallas_call(
        gates_kernel,
        out_shape=(
            jax.ShapeDtypeStruct((HALF, GRADS), F32),
            jax.ShapeDtypeStruct((HALF, GRADS), BF16),
            jax.ShapeDtypeStruct((2, 2 * HALF, WIDE), BF16),
        ),
        in_specs=[SCALARS] + [ANYWHERE] * 4,
        out_specs=(ANYWHERE,) * 3,
        scratch_shapes=[
            pltpu.VMEM((2, 2 * HALF, WIDE), BF16),
            pltpu.VMEM((3, WIDE, WIDE), BF16),
            pltpu.VMEM((HALF, GRADS), F32),
            pltpu.VMEM((HALF, GRADS), BF16),
            pltpu.SemaphoreType.DMA((32,)),
            pltpu.SemaphoreType.DMA((4,)),
            pltpu.SemaphoreType.DMA((3,)),
        ],
        compiler_params=params(),
        cost_estimate=pl.CostEstimate(flops=800000000, bytes_accessed=6000000, transcendentals=0),
        name="gates",
    )(place, acts, w, w_z, w_x)


def hidden_kernel(parts_ref, out_ref):
    total = parts_ref[0].astype(F32)
    for i in range(1, 4):
        total += parts_ref[i].astype(F32)
    gate, up, hidden_grad = (total[:, p * WIDE : (p + 1) * WIDE] for p in range(3))
    sig = 1.0 / (1.0 + jnp.exp(-gate))
    act = gate * sig
    gate_grad = (hidden_grad * up * sig * (1.0 + gate * (1.0 - sig))).astype(BF16)
    up_grad = (hidden_grad * act).astype(BF16)
    hidden = (act * up).astype(BF16)
    for i in range(4):
        for p, value in enumerate((gate_grad, up_grad, hidden)):
            out_ref[i, :, pl.ds(p * WIDE, WIDE)] = value


def hidden_grads(parts):
    whole = pl.BlockSpec(memory_space=pltpu.VMEM)
    return pl.pallas_call(
        hidden_kernel,
        out_shape=jax.ShapeDtypeStruct(parts.shape, BF16),
        in_specs=[whole],
        out_specs=whole,
        compiler_params=params(),
        cost_estimate=pl.CostEstimate(flops=2000000, bytes_accessed=1600000, transcendentals=32768),
        name="hidden_grads",
    )(parts)


def load_grads(own_in, other_in, grads_ref, sems):
    loads = []
    for i, src in enumerate((own_in, other_in)):
        loads.append(
            pltpu.make_async_copy(src, grads_ref.at[pl.ds(i * HALF, HALF)], sems.at[i])
        )
        loads[-1].start()
    return loads


def input_kernel(
    place_ref, own_in, other_in, w_in, w_z_in, w_x_in, dx_out, grads_ref, w_ref, dx_ref, in_sems, w_sems, out_sem
):
    loads = load_grads(own_in, other_in, grads_ref, in_sems)
    loads += load_weights(w_in, w_z_in, w_x_in, w_ref, 2, w_sems)
    for load in loads:
        load.wait()
    dx = dot(grads_ref[:, pl.ds(0, WIDE)], w_ref[0], ((1,), (1,)))
    dx = (dx + dot(grads_ref[:, pl.ds(WIDE, WIDE)], w_ref[1], ((1,), (1,)))).astype(BF16)
    for i in range(4):
        for f in range(4):
            dx_ref[chunk(place_ref, i, f)] = dx[i * TOK : (i + 1) * TOK, f * TOK : (f + 1) * TOK]
    store = pltpu.make_async_copy(dx_ref, dx_out, out_sem)
    store.start()
    store.wait()


def input_terms(place, own, other, w, w_z, w_x):
    return pl.pallas_call(
        input_kernel,
        out_shape=jax.ShapeDtypeStruct((16, TOK, TOK), BF16),
        in_specs=[SCALARS] + [ANYWHERE] * 5,
        out_specs=ANYWHERE,
        scratch_shapes=[
            pltpu.VMEM((2 * HALF, GRADS), BF16),
            pltpu.VMEM((2, WIDE, WIDE), BF16),
            pltpu.VMEM((16, TOK, TOK), BF16),
            pltpu.SemaphoreType.DMA((2,)),
            pltpu.SemaphoreType.DMA((4,)),
            pltpu.SemaphoreType.DMA,
        ],
        compiler_params=params(),
        cost_estimate=pl.CostEstimate(flops=540000000, bytes_accessed=4000000, transcendentals=0),
        name="input_terms",
    )(place, own, other, w, w_z, w_x)


def weight_kernel(
    acts_in, own_in, other_in, keep_out, send_out,
    acts_ref, grads_ref, keep_ref, send_ref, in_sems, out_sems,
):
    loads = load_grads(own_in, other_in, grads_ref, in_sems)
    loads.append(pltpu.make_async_copy(acts_in, acts_ref, in_sems.at[2]))
    loads[-1].start()
    for load in loads:
        load.wait()
    stores = []
    for side in (1, 0):
        for p in range(3):
            x = acts_ref[p // 2, :, pl.ds(side * BLOCK, BLOCK)]
            term = dot(x, grads_ref[:, pl.ds(p * WIDE, WIDE)], ((0,), (0,)))
            for j in range(2):
                part = term[:, j * BLOCK : (j + 1) * BLOCK]
                if side == 0:
                    keep_ref[j, p] = part
                else:
                    send_ref[j, p] = part.astype(BF16)
        src, dst = ((keep_ref, keep_out), (send_ref, send_out))[side]
        stores.append(pltpu.make_async_copy(src, dst, out_sems.at[side]))
        stores[-1].start()
    for store in stores:
        store.wait()


def weight_terms(acts, own, other):
    shape = (2, 3, BLOCK, BLOCK)
    return pl.pallas_call(
        weight_kernel,
        out_shape=(jax.ShapeDtypeStruct(shape, F32), jax.ShapeDtypeStruct(shape, BF16)),
        in_specs=[ANYWHERE] * 3,
        out_specs=(ANYWHERE,) * 2,
        scratch_shapes=[
            pltpu.VMEM((2, 2 * HALF, WIDE), BF16),
            pltpu.VMEM((2 * HALF, GRADS), BF16),
            pltpu.VMEM(shape, F32),
            pltpu.VMEM(shape, BF16),
            pltpu.SemaphoreType.DMA((3,)),
            pltpu.SemaphoreType.DMA((2,)),
        ],
        compiler_params=params(),
        cost_estimate=pl.CostEstimate(flops=800000000, bytes_accessed=6000000, transcendentals=0),
        name="weight_terms",
    )(acts, own, other)


def exchange(pieces, axes):
    return lax.all_to_all(pieces, axes, split_axis=0, concat_axis=0, tiled=True)


def local(inputs, out_grad, codes, scales):
    place = jnp.stack([lax.axis_index("core"), lax.axis_index("x0")])
    there = turned()

    acts = lax.ppermute(jnp.stack([inputs, out_grad]), AXES, there)
    w = (codes.astype(F32) * scales.astype(F32)).astype(BF16)
    w_z = lax.ppermute(w, "zl", SWAP)
    w_x = lax.ppermute(jnp.stack([w, w_z]), "x0", SWAP)
    acts = exchange(jnp.broadcast_to(acts[None], (16,) + acts.shape), SPREAD)

    keep, send, acts = gates(place, acts, w, w_z, w_x)
    total = (keep + lax.ppermute(send, "core", SWAP).astype(F32)).astype(BF16)
    grads = hidden_grads(exchange(total.reshape(4, SHARE, GRADS), REST))
    own = exchange(grads, REST).reshape(HALF, GRADS)
    other = lax.ppermute(own, "core", SWAP)

    dx = exchange(input_terms(place, own, other, w, w_z, w_x), SPREAD)
    dx = jnp.sum(dx.astype(F32), axis=0).astype(BF16)
    input_grad = lax.ppermute(dx, AXES, [(b, a) for a, b in there])

    keep, send = weight_terms(acts, own, other)
    got = lax.ppermute(send, "x0", SWAP).astype(F32)
    send = (keep[1] + got[1]).astype(BF16)
    weight_grad = keep[0] + got[0] + lax.ppermute(send, "zl", SWAP).astype(F32)
    return input_grad, weight_grad


def solution(mesh):
    fine = Mesh(mesh.devices.reshape((2,) * len(AXES)), AXES)
    return jax.shard_map(
        local,
        mesh=fine,
        in_specs=(P(ROW, COL), P(ROW, COL), P(None, ROW, COL), P(None, ROW, COL)),
        out_specs=(P(ROW, COL), P(None, ROW, COL)),
        check_vma=False,
    )
```

```python
import itertools

import jax
import jax.numpy as jnp
from jax import lax
from jax.experimental import pallas as pl
from jax.experimental.pallas import tpu as pltpu
from jax.sharding import Mesh, PartitionSpec as P

F32 = jnp.float32
BF16 = jnp.bfloat16
ROW = ("yl", "x1", "x0", "core")
COL = ("yh1", "yh0", "zh1", "zh0", "zl")
AXES = ROW + COL
SPREAD = ("yh1", "yh0", "zh1", "zh0")
REST = ("yl", "x1")
SWAP = [(0, 1), (1, 0)]
TOK = 128
BLOCK = 256
WIDE = 2 * BLOCK
HALF = 2 * TOK
SHARE = HALF // 4
GRADS = 3 * WIDE
VMEM_LIMIT = 24 * 1024 * 1024
ANYWHERE = pl.BlockSpec(memory_space=pl.ANY)
SCALARS = pl.BlockSpec(memory_space=pltpu.SMEM)


def turned():
    pairs = []
    for bits in itertools.product(range(2), repeat=len(AXES)):
        yl, x1, x0, core, yh1, yh0, zh1, zh0, zl = bits
        there = (yh1, yh0, x0, zh0, yl, x1, zh1, zl, core)
        pairs.append(tuple(sum(b << (8 - i) for i, b in enumerate(at)) for at in (bits, there)))
    return pairs


def dot(a, b, dims):
    return lax.dot_general(a, b, (dims, ((), ())), preferred_element_type=F32)


def params():
    return pltpu.CompilerParams(vmem_limit_bytes=VMEM_LIMIT)


def chunk(place_ref, i, f):
    core, x0 = place_ref[0], place_ref[1]
    t = 2 * (core if i < 2 else 1 - core) + i % 2
    return 4 * t + 2 * (x0 if f < 2 else 1 - x0) + f % 2


def load_weights(w_in, w_z_in, w_x_in, w_ref, count, sems):
    loads = []
    for i, src in enumerate((w_in, w_z_in, w_x_in.at[0], w_x_in.at[1])):
        rows, cols = pl.ds(i // 2 * BLOCK, BLOCK), pl.ds(i % 2 * BLOCK, BLOCK)
        loads.append(
            pltpu.make_async_copy(src.at[pl.ds(0, count)], w_ref.at[:, rows, cols], sems.at[i])
        )
        loads[-1].start()
    return loads


def gates_kernel(
    place_ref, acts_in, w_in, w_z_in, w_x_in, keep_out, send_out, acts_out,
    acts_ref, w_ref, keep_ref, send_ref, act_sems, w_sems, out_sems,
):
    w_loads = load_weights(w_in, w_z_in, w_x_in, w_ref, 3, w_sems)
    loads = []
    for p in range(2):
        for i in range(4):
            for f in range(4):
                src = acts_in.at[chunk(place_ref, i, f), p]
                dst = acts_ref.at[p, pl.ds(i * TOK, TOK), pl.ds(f * TOK, TOK)]
                loads.append(pltpu.make_async_copy(src, dst, act_sems.at[len(loads)]))
                loads[-1].start()
    for load in loads:
        load.wait()
    stores = [pltpu.make_async_copy(acts_ref, acts_out, out_sems.at[0])]
    stores[0].start()
    for load in w_loads:
        load.wait()
    for p in range(3):
        cols = pl.ds(p * WIDE, WIDE)
        sums = dot(acts_ref[p // 2], w_ref[p], ((1,), (0,)))
        send_ref[:, cols] = sums[HALF:].astype(BF16)
        keep_ref[:, cols] = sums[:HALF]
    for i, (src, dst) in enumerate(((send_ref, send_out), (keep_ref, keep_out))):
        stores.append(pltpu.make_async_copy(src, dst, out_sems.at[1 + i]))
        stores[-1].start()
    for store in stores:
        store.wait()


def gates(place, acts, w, w_z, w_x):
    return pl.pallas_call(
        gates_kernel,
        out_shape=(
            jax.ShapeDtypeStruct((HALF, GRADS), F32),
            jax.ShapeDtypeStruct((HALF, GRADS), BF16),
            jax.ShapeDtypeStruct((2, 2 * HALF, WIDE), BF16),
        ),
        in_specs=[SCALARS] + [ANYWHERE] * 4,
        out_specs=(ANYWHERE,) * 3,
        scratch_shapes=[
            pltpu.VMEM((2, 2 * HALF, WIDE), BF16),
            pltpu.VMEM((3, WIDE, WIDE), BF16),
            pltpu.VMEM((HALF, GRADS), F32),
            pltpu.VMEM((HALF, GRADS), BF16),
            pltpu.SemaphoreType.DMA((32,)),
            pltpu.SemaphoreType.DMA((4,)),
            pltpu.SemaphoreType.DMA((3,)),
        ],
        compiler_params=params(),
        cost_estimate=pl.CostEstimate(flops=800000000, bytes_accessed=6000000, transcendentals=0),
        name="gates",
    )(place, acts, w, w_z, w_x)


def hidden_kernel(parts_ref, out_ref):
    total = parts_ref[0].astype(F32)
    for i in range(1, 4):
        total += parts_ref[i].astype(F32)
    gate, up, hidden_grad = (total[:, p * WIDE : (p + 1) * WIDE] for p in range(3))
    sig = 1.0 / (1.0 + jnp.exp(-gate))
    act = gate * sig
    gate_grad = (hidden_grad * up * sig * (1.0 + gate * (1.0 - sig))).astype(BF16)
    up_grad = (hidden_grad * act).astype(BF16)
    hidden = (act * up).astype(BF16)
    for i in range(4):
        for p, value in enumerate((gate_grad, up_grad, hidden)):
            out_ref[i, :, pl.ds(p * WIDE, WIDE)] = value


def hidden_grads(parts):
    whole = pl.BlockSpec(memory_space=pltpu.VMEM)
    return pl.pallas_call(
        hidden_kernel,
        out_shape=jax.ShapeDtypeStruct(parts.shape, BF16),
        in_specs=[whole],
        out_specs=whole,
        compiler_params=params(),
        cost_estimate=pl.CostEstimate(flops=2000000, bytes_accessed=1600000, transcendentals=32768),
        name="hidden_grads",
    )(parts)


def load_grads(own_in, other_in, grads_ref, sems):
    loads = []
    for i, src in enumerate((own_in, other_in)):
        loads.append(
            pltpu.make_async_copy(src, grads_ref.at[pl.ds(i * HALF, HALF)], sems.at[i])
        )
        loads[-1].start()
    return loads


def input_kernel(
    place_ref, own_in, other_in, w_in, w_z_in, w_x_in, dx_out, grads_ref, w_ref, dx_ref, in_sems, w_sems, out_sem
):
    loads = load_grads(own_in, other_in, grads_ref, in_sems)
    loads += load_weights(w_in, w_z_in, w_x_in, w_ref, 2, w_sems)
    for load in loads:
        load.wait()
    dx = dot(grads_ref[:, pl.ds(0, WIDE)], w_ref[0], ((1,), (1,)))
    dx = (dx + dot(grads_ref[:, pl.ds(WIDE, WIDE)], w_ref[1], ((1,), (1,)))).astype(BF16)
    for i in range(4):
        for f in range(4):
            dx_ref[chunk(place_ref, i, f)] = dx[i * TOK : (i + 1) * TOK, f * TOK : (f + 1) * TOK]
    store = pltpu.make_async_copy(dx_ref, dx_out, out_sem)
    store.start()
    store.wait()


def input_terms(place, own, other, w, w_z, w_x):
    return pl.pallas_call(
        input_kernel,
        out_shape=jax.ShapeDtypeStruct((16, TOK, TOK), BF16),
        in_specs=[SCALARS] + [ANYWHERE] * 5,
        out_specs=ANYWHERE,
        scratch_shapes=[
            pltpu.VMEM((2 * HALF, GRADS), BF16),
            pltpu.VMEM((2, WIDE, WIDE), BF16),
            pltpu.VMEM((16, TOK, TOK), BF16),
            pltpu.SemaphoreType.DMA((2,)),
            pltpu.SemaphoreType.DMA((4,)),
            pltpu.SemaphoreType.DMA,
        ],
        compiler_params=params(),
        cost_estimate=pl.CostEstimate(flops=540000000, bytes_accessed=4000000, transcendentals=0),
        name="input_terms",
    )(place, own, other, w, w_z, w_x)


def weight_kernel(
    acts_in, own_in, other_in, keep_out, send_out,
    acts_ref, grads_ref, keep_ref, send_ref, in_sems, out_sems,
):
    loads = load_grads(own_in, other_in, grads_ref, in_sems)
    loads.append(pltpu.make_async_copy(acts_in, acts_ref, in_sems.at[2]))
    loads[-1].start()
    for load in loads:
        load.wait()
    stores = []
    for side in (1, 0):
        for p in range(3):
            x = acts_ref[p // 2, :, pl.ds(side * BLOCK, BLOCK)]
            term = dot(x, grads_ref[:, pl.ds(p * WIDE, WIDE)], ((0,), (0,)))
            for j in range(2):
                part = term[:, j * BLOCK : (j + 1) * BLOCK]
                if side == 0:
                    keep_ref[j, p] = part
                else:
                    send_ref[j, p] = part.astype(BF16)
        src, dst = ((keep_ref, keep_out), (send_ref, send_out))[side]
        stores.append(pltpu.make_async_copy(src, dst, out_sems.at[side]))
        stores[-1].start()
    for store in stores:
        store.wait()


def weight_terms(acts, own, other):
    shape = (2, 3, BLOCK, BLOCK)
    return pl.pallas_call(
        weight_kernel,
        out_shape=(jax.ShapeDtypeStruct(shape, F32), jax.ShapeDtypeStruct(shape, BF16)),
        in_specs=[ANYWHERE] * 3,
        out_specs=(ANYWHERE,) * 2,
        scratch_shapes=[
            pltpu.VMEM((2, 2 * HALF, WIDE), BF16),
            pltpu.VMEM((2 * HALF, GRADS), BF16),
            pltpu.VMEM(shape, F32),
            pltpu.VMEM(shape, BF16),
            pltpu.SemaphoreType.DMA((3,)),
            pltpu.SemaphoreType.DMA((2,)),
        ],
        compiler_params=params(),
        cost_estimate=pl.CostEstimate(flops=800000000, bytes_accessed=6000000, transcendentals=0),
        name="weight_terms",
    )(acts, own, other)


def exchange(pieces, axes):
    return lax.all_to_all(pieces, axes, split_axis=0, concat_axis=0, tiled=True)


def local(inputs, out_grad, codes, scales):
    place = jnp.stack([lax.axis_index("core"), lax.axis_index("x0")])
    there = turned()

    acts = lax.ppermute(jnp.stack([inputs, out_grad]), AXES, there)
    w = (codes.astype(F32) * scales.astype(F32)).astype(BF16)
    w_z = lax.ppermute(w, "zl", SWAP)
    acts, w_z = lax.optimization_barrier((acts, w_z))
    w_x = lax.ppermute(jnp.stack([w, w_z]), "x0", SWAP)
    acts = exchange(jnp.broadcast_to(acts[None], (16,) + acts.shape), SPREAD)

    keep, send, acts = gates(place, acts, w, w_z, w_x)
    total = (keep + lax.ppermute(send, "core", SWAP).astype(F32)).astype(BF16)
    grads = hidden_grads(exchange(total.reshape(4, SHARE, GRADS), REST))
    own = exchange(grads, REST).reshape(HALF, GRADS)
    other = lax.ppermute(own, "core", SWAP)

    dx = input_terms(place, own, other, w, w_z, w_x)
    dx, acts = lax.optimization_barrier((dx, acts))
    dx = exchange(dx, SPREAD)
    dx = jnp.sum(dx.astype(F32), axis=0).astype(BF16)
    input_grad = lax.ppermute(dx, AXES, [(b, a) for a, b in there])

    keep, send = weight_terms(acts, own, other)
    got = lax.ppermute(send, "x0", SWAP).astype(F32)
    send = (keep[1] + got[1]).astype(BF16)
    weight_grad = keep[0] + got[0] + lax.ppermute(send, "zl", SWAP).astype(F32)
    return input_grad, weight_grad


def solution(mesh):
    fine = Mesh(mesh.devices.reshape((2,) * len(AXES)), AXES)
    return jax.shard_map(
        local,
        mesh=fine,
        in_specs=(P(ROW, COL), P(ROW, COL), P(None, ROW, COL), P(None, ROW, COL)),
        out_specs=(P(ROW, COL), P(None, ROW, COL)),
        check_vma=False,
    )
```

```python
import itertools

import jax
import jax.numpy as jnp
from jax import lax
from jax.experimental import pallas as pl
from jax.experimental.pallas import tpu as pltpu
from jax.sharding import Mesh, PartitionSpec as P

F32 = jnp.float32
BF16 = jnp.bfloat16
ROW = ("yl", "x1", "x0", "core")
COL = ("yh1", "yh0", "zh1", "zh0", "zl")
AXES = ROW + COL
YH = ("yh1", "yh0")
ZH = ("zh1", "zh0")
REST = ("yl", "x1")
SWAP = [(0, 1), (1, 0)]
TOK = 128
BLOCK = 256
WIDE = 2 * BLOCK
TOKENS = 2 * TOK
SHARE = TOKENS // 4
FEATURES = 4 * BLOCK
GRADS = 3 * WIDE
VMEM_LIMIT = 24 * 1024 * 1024
ANYWHERE = pl.BlockSpec(memory_space=pl.ANY)
SCALARS = pl.BlockSpec(memory_space=pltpu.SMEM)


def turned():
    pairs = []
    for bits in itertools.product(range(2), repeat=len(AXES)):
        yl, x1, x0, core, yh1, yh0, zh1, zh0, zl = bits
        there = (yh1, yh0, x0, core, yl, zl, zh1, zh0, x1)
        pairs.append(tuple(sum(b << (8 - i) for i, b in enumerate(at)) for at in (bits, there)))
    return pairs


def dot(a, b, dims):
    return lax.dot_general(a, b, (dims, ((), ())), preferred_element_type=F32)


def params():
    return pltpu.CompilerParams(vmem_limit_bytes=VMEM_LIMIT)


def chunk(place_ref, t, f):
    core, x0 = place_ref[0], place_ref[1]
    core = core if f < 4 else 1 - core
    x0 = x0 if f % 4 < 2 else 1 - x0
    return 8 * x0 + 4 * core + 2 * t + f % 2


def load_weights(w_ins, w_ref, sems):
    loads = []
    for i, src in enumerate(w_ins):
        rows, cols = pl.ds(i // 2 * BLOCK, BLOCK), pl.ds(i % 2 * BLOCK, BLOCK)
        src = src.at[pl.ds(0, w_ref.shape[0])]
        loads.append(pltpu.make_async_copy(src, w_ref.at[:, rows, cols], sems.at[i]))
        loads[-1].start()
    return loads


def gates_kernel(
    place_ref, acts_in, w0, w1, w2, w3, w4, w5, w6, w7, parts_out, keep_out, send_out,
    acts_ref, w_ref, parts_ref, act_sems, w_sems, out_sems,
):
    w_loads = load_weights((w0, w1, w2, w3, w4, w5, w6, w7), w_ref, w_sems)
    loads = []
    for p in range(2):
        for t in range(2):
            for f in range(8):
                src = acts_in.at[chunk(place_ref, t, f), p]
                dst = acts_ref.at[p, pl.ds(t * TOK, TOK), pl.ds(f * TOK, TOK)]
                loads.append(pltpu.make_async_copy(src, dst, act_sems.at[len(loads)]))
                loads[-1].start()
    for load in loads:
        load.wait()
    stores = []
    for side, out in enumerate((keep_out, send_out)):
        src = acts_ref.at[:, :, pl.ds(side * WIDE, WIDE)]
        stores.append(pltpu.make_async_copy(src, out, out_sems.at[side]))
        stores[-1].start()
    for load in w_loads:
        load.wait()
    for p in range(3):
        sums = dot(acts_ref[p // 2], w_ref[p], ((1,), (0,)))
        parts_ref[:, pl.ds(p * WIDE, WIDE)] = sums.astype(BF16)
    stores.append(pltpu.make_async_copy(parts_ref, parts_out, out_sems.at[2]))
    stores[-1].start()
    for store in stores:
        store.wait()


def gates(place, acts, *weights):
    return pl.pallas_call(
        gates_kernel,
        out_shape=(
            jax.ShapeDtypeStruct((TOKENS, GRADS), BF16),
            jax.ShapeDtypeStruct((2, TOKENS, WIDE), BF16),
            jax.ShapeDtypeStruct((2, TOKENS, WIDE), BF16),
        ),
        in_specs=[SCALARS] + [ANYWHERE] * 9,
        out_specs=(ANYWHERE,) * 3,
        scratch_shapes=[
            pltpu.VMEM((2, TOKENS, FEATURES), BF16),
            pltpu.VMEM((3, FEATURES, WIDE), BF16),
            pltpu.VMEM((TOKENS, GRADS), BF16),
            pltpu.SemaphoreType.DMA((32,)),
            pltpu.SemaphoreType.DMA((8,)),
            pltpu.SemaphoreType.DMA((3,)),
        ],
        compiler_params=params(),
        cost_estimate=pl.CostEstimate(flops=800000000, bytes_accessed=6000000, transcendentals=0),
        name="gates",
    )(place, acts, *weights)


def hidden_kernel(parts_ref, out_ref):
    total = parts_ref[0].astype(F32)
    for i in range(1, 4):
        total += parts_ref[i].astype(F32)
    gate, up, hidden_grad = (total[:, p * WIDE : (p + 1) * WIDE] for p in range(3))
    sig = 1.0 / (1.0 + jnp.exp(-gate))
    act = gate * sig
    gate_grad = (hidden_grad * up * sig * (1.0 + gate * (1.0 - sig))).astype(BF16)
    up_grad = (hidden_grad * act).astype(BF16)
    hidden = (act * up).astype(BF16)
    for i in range(4):
        for p, value in enumerate((gate_grad, up_grad, hidden)):
            out_ref[i, :, pl.ds(p * WIDE, WIDE)] = value


def hidden_grads(parts):
    whole = pl.BlockSpec(memory_space=pltpu.VMEM)
    return pl.pallas_call(
        hidden_kernel,
        out_shape=jax.ShapeDtypeStruct(parts.shape, BF16),
        in_specs=[whole],
        out_specs=whole,
        compiler_params=params(),
        cost_estimate=pl.CostEstimate(flops=2000000, bytes_accessed=1600000, transcendentals=32768),
        name="hidden_grads",
    )(parts)


def input_kernel(
    place_ref, grads_in, w0, w1, w2, w3, w4, w5, w6, w7, dx_out, grads_ref, w_ref, dx_ref, in_sem, w_sems, out_sem
):
    loads = load_weights((w0, w1, w2, w3, w4, w5, w6, w7), w_ref, w_sems)
    loads.append(pltpu.make_async_copy(grads_in, grads_ref, in_sem))
    loads[-1].start()
    for load in loads:
        load.wait()
    dx = dot(grads_ref[:, pl.ds(0, WIDE)], w_ref[0], ((1,), (1,)))
    dx = (dx + dot(grads_ref[:, pl.ds(WIDE, WIDE)], w_ref[1], ((1,), (1,)))).astype(BF16)
    for t in range(2):
        for f in range(8):
            dx_ref[chunk(place_ref, t, f)] = dx[t * TOK : (t + 1) * TOK, f * TOK : (f + 1) * TOK]
    store = pltpu.make_async_copy(dx_ref, dx_out, out_sem)
    store.start()
    store.wait()


def input_terms(place, grads, *weights):
    return pl.pallas_call(
        input_kernel,
        out_shape=jax.ShapeDtypeStruct((16, TOK, TOK), BF16),
        in_specs=[SCALARS] + [ANYWHERE] * 9,
        out_specs=ANYWHERE,
        scratch_shapes=[
            pltpu.VMEM((TOKENS, GRADS), BF16),
            pltpu.VMEM((2, FEATURES, WIDE), BF16),
            pltpu.VMEM((16, TOK, TOK), BF16),
            pltpu.SemaphoreType.DMA,
            pltpu.SemaphoreType.DMA((8,)),
            pltpu.SemaphoreType.DMA,
        ],
        compiler_params=params(),
        cost_estimate=pl.CostEstimate(flops=540000000, bytes_accessed=4000000, transcendentals=0),
        name="input_terms",
    )(place, grads, *weights)


def weight_kernel(
    acts_in, other_acts_in, grads_in, other_grads_in, keep_out, z_out, x_out, xz_out,
    acts_ref, grads_ref, keep_ref, send_ref, in_sems, out_sems,
):
    loads = []
    for i, (acts, grads) in enumerate(((acts_in, grads_in), (other_acts_in, other_grads_in))):
        rows = pl.ds(i * TOKENS, TOKENS)
        loads.append(pltpu.make_async_copy(acts, acts_ref.at[:, rows], in_sems.at[i]))
        loads.append(pltpu.make_async_copy(grads, grads_ref.at[rows], in_sems.at[2 + i]))
    for load in loads:
        load.start()
    for load in loads:
        load.wait()
    stores = []
    for side in (1, 0):
        for p in range(3):
            x = acts_ref[p // 2, :, pl.ds(side * BLOCK, BLOCK)]
            term = dot(x, grads_ref[:, pl.ds(p * WIDE, WIDE)], ((0,), (0,)))
            for j in range(2):
                part = term[:, j * BLOCK : (j + 1) * BLOCK]
                if side or j:
                    send_ref[2 * side + j - 1, p] = part.astype(BF16)
                else:
                    keep_ref[p] = part
        for j in range(2):
            out = ((keep_out, z_out), (x_out, xz_out))[side][j]
            src = send_ref.at[2 * side + j - 1] if side or j else keep_ref
            stores.append(pltpu.make_async_copy(src, out, out_sems.at[2 * side + j]))
            stores[-1].start()
    for store in stores:
        store.wait()


def weight_terms(acts, other_acts, grads, other_grads):
    shape = (3, BLOCK, BLOCK)
    send = jax.ShapeDtypeStruct(shape, BF16)
    return pl.pallas_call(
        weight_kernel,
        out_shape=(jax.ShapeDtypeStruct(shape, F32), send, send, send),
        in_specs=[ANYWHERE] * 4,
        out_specs=(ANYWHERE,) * 4,
        scratch_shapes=[
            pltpu.VMEM((2, 2 * TOKENS, WIDE), BF16),
            pltpu.VMEM((2 * TOKENS, GRADS), BF16),
            pltpu.VMEM(shape, F32),
            pltpu.VMEM((3,) + shape, BF16),
            pltpu.SemaphoreType.DMA((4,)),
            pltpu.SemaphoreType.DMA((4,)),
        ],
        compiler_params=params(),
        cost_estimate=pl.CostEstimate(flops=800000000, bytes_accessed=6000000, transcendentals=0),
        name="weight_terms",
    )(acts, other_acts, grads, other_grads)


def exchange(pieces, axes):
    return lax.all_to_all(pieces, axes, split_axis=0, concat_axis=0, tiled=True)


def local(inputs, out_grad, codes, scales):
    place = jnp.stack([lax.axis_index("core"), lax.axis_index("x0")])
    there = turned()

    acts = lax.ppermute(jnp.stack([inputs, out_grad]), AXES, there)
    acts = exchange(jnp.broadcast_to(acts[None], (4,) + acts.shape), YH)
    w = (codes.astype(F32) * scales.astype(F32)).astype(BF16)
    w_z = lax.ppermute(w, "zl", SWAP)
    w_x = lax.ppermute(w, "x0", SWAP)
    acts, w_z, w_x = lax.optimization_barrier((acts, w_z, w_x))
    weights = [w, w_z, w_x, lax.ppermute(w_z, "x0", SWAP)]
    weights += [lax.ppermute(block, "core", SWAP) for block in weights]
    acts = exchange(jnp.broadcast_to(acts[None], (4,) + acts.shape), ZH).reshape(16, 2, TOK, TOK)

    parts, acts, send = gates(place, acts, *weights)
    other_acts = lax.ppermute(send, "core", SWAP)
    parts = exchange(parts.reshape(4, SHARE, GRADS), REST)
    parts, other_acts = lax.optimization_barrier((parts, other_acts))
    grads = exchange(hidden_grads(parts), REST).reshape(TOKENS, GRADS)
    other_grads = lax.ppermute(grads, "core", SWAP)

    dx = exchange(input_terms(place, grads, *weights), ZH + YH)
    dx = jnp.sum(dx.astype(F32), axis=0).astype(BF16)
    input_grad = lax.ppermute(dx, AXES, [(b, a) for a, b in there])

    weight_grad, z, x, xz = weight_terms(acts, other_acts, grads, other_grads)
    weight_grad += lax.ppermute(z, "zl", SWAP).astype(F32)
    weight_grad += lax.ppermute(x, "x0", SWAP).astype(F32)
    weight_grad += lax.ppermute(xz, ("x0", "zl"), [(i, 3 - i) for i in range(4)]).astype(F32)
    return input_grad, weight_grad


def solution(mesh):
    fine = Mesh(mesh.devices.reshape((2,) * len(AXES)), AXES)
    return jax.shard_map(
        local,
        mesh=fine,
        in_specs=(P(ROW, COL), P(ROW, COL), P(None, ROW, COL), P(None, ROW, COL)),
        out_specs=(P(ROW, COL), P(None, ROW, COL)),
        check_vma=False,
    )
```

```python
import itertools

import jax
import jax.numpy as jnp
from jax import lax
from jax.experimental import pallas as pl
from jax.experimental.pallas import tpu as pltpu
from jax.sharding import Mesh, PartitionSpec as P

F32 = jnp.float32
BF16 = jnp.bfloat16
ROW = ("yl", "x1", "x0", "core")
COL = ("yh1", "yh0", "zh1", "zh0", "zl")
AXES = ROW + COL
YH = ("yh1", "yh0")
ZH = ("zh1", "zh0")
REST = ("yl", "x1")
SWAP = [(0, 1), (1, 0)]
TOK = 128
BLOCK = 256
WIDE = 2 * BLOCK
TOKENS = 2 * TOK
SHARE = TOKENS // 4
FEATURES = 4 * BLOCK
GRADS = 3 * WIDE
VMEM_LIMIT = 24 * 1024 * 1024
WHOLE = pl.BlockSpec(memory_space=pltpu.VMEM)
SCALARS = pl.BlockSpec(memory_space=pltpu.SMEM)


def turned():
    pairs = []
    for bits in itertools.product(range(2), repeat=len(AXES)):
        yl, x1, x0, core, yh1, yh0, zh1, zh0, zl = bits
        there = (yh1, yh0, x0, core, yl, zl, zh1, zh0, x1)
        pairs.append(tuple(sum(b << (8 - i) for i, b in enumerate(at)) for at in (bits, there)))
    return pairs


def dot(a, b, dims):
    return lax.dot_general(a, b, (dims, ((), ())), preferred_element_type=F32)


def params():
    return pltpu.CompilerParams(vmem_limit_bytes=VMEM_LIMIT)


def chunk(place_ref, t, f):
    core, x0 = place_ref[0], place_ref[1]
    core = core if f < 4 else 1 - core
    x0 = x0 if f % 4 < 2 else 1 - x0
    return 8 * x0 + 4 * core + 2 * t + f % 2


def gates_kernel(place_ref, acts_ref, *refs):
    w_refs, parts_ref, wide_ref = refs[:8], refs[8], refs[9]
    for p in range(2):
        for t in range(2):
            for f in range(8):
                block = acts_ref[chunk(place_ref, t, f), p]
                wide_ref[p, pl.ds(t * TOK, TOK), pl.ds(f * TOK, TOK)] = block
    for p in range(3):
        for j in range(2):
            total = jnp.zeros((TOKENS, BLOCK), F32)
            for s in range(4):
                total += dot(wide_ref[p // 2, :, pl.ds(s * BLOCK, BLOCK)], w_refs[2 * s + j][p], ((1,), (0,)))
            parts_ref[:, pl.ds(p * WIDE + j * BLOCK, BLOCK)] = total.astype(BF16)


def gates(place, acts, *weights):
    return pl.pallas_call(
        gates_kernel,
        out_shape=jax.ShapeDtypeStruct((TOKENS, GRADS), BF16),
        in_specs=[SCALARS] + [WHOLE] * 9,
        out_specs=WHOLE,
        scratch_shapes=[pltpu.VMEM((2, TOKENS, FEATURES), BF16)],
        compiler_params=params(),
        cost_estimate=pl.CostEstimate(flops=800000000, bytes_accessed=6000000, transcendentals=0),
        name="gates",
    )(place, acts, *weights)


def hidden_kernel(parts_ref, out_ref):
    total = parts_ref[0].astype(F32)
    for i in range(1, 4):
        total += parts_ref[i].astype(F32)
    gate, up, hidden_grad = (total[:, p * WIDE : (p + 1) * WIDE] for p in range(3))
    sig = 1.0 / (1.0 + jnp.exp(-gate))
    act = gate * sig
    gate_grad = (hidden_grad * up * sig * (1.0 + gate * (1.0 - sig))).astype(BF16)
    up_grad = (hidden_grad * act).astype(BF16)
    hidden = (act * up).astype(BF16)
    for i in range(4):
        for p, value in enumerate((gate_grad, up_grad, hidden)):
            out_ref[i, :, pl.ds(p * WIDE, WIDE)] = value


def hidden_grads(parts):
    return pl.pallas_call(
        hidden_kernel,
        out_shape=jax.ShapeDtypeStruct(parts.shape, BF16),
        in_specs=[WHOLE],
        out_specs=WHOLE,
        compiler_params=params(),
        cost_estimate=pl.CostEstimate(flops=2000000, bytes_accessed=1600000, transcendentals=32768),
        name="hidden_grads",
    )(parts)


def input_kernel(place_ref, grads_ref, *refs):
    w_refs, dx_ref = refs[:8], refs[8]
    for s in range(4):
        dx = jnp.zeros((TOKENS, BLOCK), F32)
        for p in range(2):
            for j in range(2):
                grads = grads_ref[:, pl.ds(p * WIDE + j * BLOCK, BLOCK)]
                dx += dot(grads, w_refs[2 * s + j][p], ((1,), (1,)))
        dx = dx.astype(BF16)
        for t in range(2):
            for f in range(2):
                part = dx[t * TOK : (t + 1) * TOK, f * TOK : (f + 1) * TOK]
                dx_ref[chunk(place_ref, t, 2 * s + f)] = part


def input_terms(place, grads, *weights):
    return pl.pallas_call(
        input_kernel,
        out_shape=jax.ShapeDtypeStruct((16, TOK, TOK), BF16),
        in_specs=[SCALARS] + [WHOLE] * 9,
        out_specs=WHOLE,
        compiler_params=params(),
        cost_estimate=pl.CostEstimate(flops=540000000, bytes_accessed=4000000, transcendentals=0),
        name="input_terms",
    )(place, grads, *weights)


def weight_kernel(
    place_ref, acts_ref, other_acts_ref, grads_ref, other_grads_ref, keep_ref, z_ref, x_ref, xz_ref, wide_ref
):
    for p in range(2):
        for t in range(2):
            for f in range(4):
                x0 = place_ref[1] if f < 2 else 1 - place_ref[1]
                cols = pl.ds(f * TOK, TOK)
                mine = acts_ref[chunk(place_ref, t, f), p]
                wide_ref[p, pl.ds(t * TOK, TOK), cols] = mine
                wide_ref[p, pl.ds(TOKENS + t * TOK, TOK), cols] = other_acts_ref[x0, 2 * t + f % 2, p]
    for side in (1, 0):
        for p in range(3):
            for j in range(2):
                cols = pl.ds(p * WIDE + j * BLOCK, BLOCK)
                term = jnp.zeros((BLOCK, BLOCK), F32)
                for i, ref in enumerate((grads_ref, other_grads_ref)):
                    x = wide_ref[p // 2, pl.ds(i * TOKENS, TOKENS), pl.ds(side * BLOCK, BLOCK)]
                    term += dot(x, ref[:, cols], ((0,), (0,)))
                out_ref = ((keep_ref, z_ref), (x_ref, xz_ref))[side][j]
                out_ref[p] = term.astype(out_ref.dtype)


def weight_terms(place, acts, other_acts, grads, other_grads):
    shape = (3, BLOCK, BLOCK)
    send = jax.ShapeDtypeStruct(shape, BF16)
    return pl.pallas_call(
        weight_kernel,
        out_shape=(jax.ShapeDtypeStruct(shape, F32), send, send, send),
        in_specs=[SCALARS] + [WHOLE] * 4,
        out_specs=(WHOLE,) * 4,
        scratch_shapes=[pltpu.VMEM((2, 2 * TOKENS, WIDE), BF16)],
        compiler_params=params(),
        cost_estimate=pl.CostEstimate(flops=800000000, bytes_accessed=6000000, transcendentals=0),
        name="weight_terms",
    )(place, acts, other_acts, grads, other_grads)


def exchange(pieces, axes):
    return lax.all_to_all(pieces, axes, split_axis=0, concat_axis=0, tiled=True)


def local(inputs, out_grad, codes, scales):
    place = jnp.stack([lax.axis_index("core"), lax.axis_index("x0")])
    there = turned()

    acts = lax.ppermute(jnp.stack([inputs, out_grad]), AXES, there)
    acts = exchange(jnp.broadcast_to(acts[None], (4,) + acts.shape), YH)
    w = (codes.astype(F32) * scales.astype(F32)).astype(BF16)
    w_z = lax.ppermute(w, "zl", SWAP)
    w_x = lax.ppermute(w, "x0", SWAP)
    acts, w_z, w_x = lax.optimization_barrier((acts, w_z, w_x))
    weights = [w, w_z, w_x, lax.ppermute(w_z, "x0", SWAP)]
    weights += [lax.ppermute(block, "core", SWAP) for block in weights]
    acts = exchange(jnp.broadcast_to(acts[None], (4,) + acts.shape), ZH).reshape(16, 2, TOK, TOK)

    parts = gates(place, acts, *weights)
    other_acts = acts.reshape(2, 2, 4, 2, TOK, TOK)
    other_acts = lax.dynamic_index_in_dim(other_acts, 1 - place[0], axis=1, keepdims=False)
    other_acts = lax.ppermute(other_acts, "core", SWAP)
    parts = exchange(parts.reshape(4, SHARE, GRADS), REST)
    parts, other_acts = lax.optimization_barrier((parts, other_acts))
    grads = exchange(hidden_grads(parts), REST).reshape(TOKENS, GRADS)
    other_grads = lax.ppermute(grads, "core", SWAP)

    dx = exchange(input_terms(place, grads, *weights), ZH + YH)
    dx = jnp.sum(dx.astype(F32), axis=0).astype(BF16)
    input_grad = lax.ppermute(dx, AXES, [(b, a) for a, b in there])

    weight_grad, z, x, xz = weight_terms(place, acts, other_acts, grads, other_grads)
    weight_grad += lax.ppermute(z, "zl", SWAP).astype(F32)
    weight_grad += lax.ppermute(x, "x0", SWAP).astype(F32)
    weight_grad += lax.ppermute(xz, ("x0", "zl"), [(i, 3 - i) for i in range(4)]).astype(F32)
    return input_grad, weight_grad


def solution(mesh):
    fine = Mesh(mesh.devices.reshape((2,) * len(AXES)), AXES)
    return jax.shard_map(
        local,
        mesh=fine,
        in_specs=(P(ROW, COL), P(ROW, COL), P(None, ROW, COL), P(None, ROW, COL)),
        out_specs=(P(ROW, COL), P(None, ROW, COL)),
        check_vma=False,
    )
```

```python
import itertools

import jax
import jax.numpy as jnp
from jax import lax
from jax.experimental import pallas as pl
from jax.experimental.pallas import tpu as pltpu
from jax.sharding import Mesh, PartitionSpec as P

F32 = jnp.float32
BF16 = jnp.bfloat16
ROW = ("yl", "x1", "x0", "core")
COL = ("yh1", "yh0", "zh1", "zh0", "zl")
AXES = ROW + COL
YH = ("yh1", "yh0")
ZH = ("zh1", "zh0")
REST = ("yl", "x1")
SWAP = [(0, 1), (1, 0)]
TOK = 128
BLOCK = 256
WIDE = 2 * BLOCK
TOKENS = 2 * TOK
SHARE = TOKENS // 4
FEATURES = 4 * BLOCK
GRADS = 3 * WIDE
VMEM_LIMIT = 24 * 1024 * 1024
WHOLE = pl.BlockSpec(memory_space=pltpu.VMEM)
SCALARS = pl.BlockSpec(memory_space=pltpu.SMEM)


def turned():
    pairs = []
    for bits in itertools.product(range(2), repeat=len(AXES)):
        yl, x1, x0, core, yh1, yh0, zh1, zh0, zl = bits
        there = (yh1, yh0, x0, core, yl, zl, zh1, zh0, x1)
        pairs.append(tuple(sum(b << (8 - i) for i, b in enumerate(at)) for at in (bits, there)))
    return pairs


def dot(a, b, dims):
    return lax.dot_general(a, b, (dims, ((), ())), preferred_element_type=F32)


def params():
    return pltpu.CompilerParams(vmem_limit_bytes=VMEM_LIMIT)


def chunk(place_ref, t, f):
    core, x0 = place_ref[0], place_ref[1]
    core = core if f < 4 else 1 - core
    x0 = x0 if f % 4 < 2 else 1 - x0
    return 8 * x0 + 4 * core + 2 * t + f % 2


def gates_kernel(place_ref, acts_ref, *refs):
    w_refs, parts_ref, wide_ref = refs[:8], refs[8], refs[9]
    for p in range(2):
        for t in range(2):
            for f in range(8):
                block = acts_ref[chunk(place_ref, t, f), p]
                wide_ref[p, pl.ds(t * TOK, TOK), pl.ds(f * TOK, TOK)] = block
    for p in range(3):
        for j in range(2):
            total = jnp.zeros((TOKENS, BLOCK), F32)
            for s in range(4):
                total += dot(wide_ref[p // 2, :, pl.ds(s * BLOCK, BLOCK)], w_refs[2 * s + j][p], ((1,), (0,)))
            parts_ref[:, pl.ds(p * WIDE + j * BLOCK, BLOCK)] = total.astype(BF16)


def gates(place, acts, *weights):
    return pl.pallas_call(
        gates_kernel,
        out_shape=jax.ShapeDtypeStruct((TOKENS, GRADS), BF16),
        in_specs=[SCALARS] + [WHOLE] * 9,
        out_specs=WHOLE,
        scratch_shapes=[pltpu.VMEM((2, TOKENS, FEATURES), BF16)],
        compiler_params=params(),
        cost_estimate=pl.CostEstimate(flops=800000000, bytes_accessed=6000000, transcendentals=0),
        name="gates",
    )(place, acts, *weights)


def hidden_kernel(parts_ref, out_ref):
    total = parts_ref[0].astype(F32)
    for i in range(1, 4):
        total += parts_ref[i].astype(F32)
    gate, up, hidden_grad = (total[:, p * WIDE : (p + 1) * WIDE] for p in range(3))
    sig = 1.0 / (1.0 + jnp.exp(-gate))
    act = gate * sig
    gate_grad = (hidden_grad * up * sig * (1.0 + gate * (1.0 - sig))).astype(BF16)
    up_grad = (hidden_grad * act).astype(BF16)
    hidden = (act * up).astype(BF16)
    for i in range(4):
        for p, value in enumerate((gate_grad, up_grad, hidden)):
            out_ref[i, :, pl.ds(p * WIDE, WIDE)] = value


def hidden_grads(parts):
    return pl.pallas_call(
        hidden_kernel,
        out_shape=jax.ShapeDtypeStruct(parts.shape, BF16),
        in_specs=[WHOLE],
        out_specs=WHOLE,
        compiler_params=params(),
        cost_estimate=pl.CostEstimate(flops=2000000, bytes_accessed=1600000, transcendentals=32768),
        name="hidden_grads",
    )(parts)


def input_kernel(place_ref, grads_ref, *refs):
    w_refs, dx_ref = refs[:8], refs[8]
    for s in range(4):
        dx = jnp.zeros((TOKENS, BLOCK), F32)
        for p in range(2):
            for j in range(2):
                grads = grads_ref[:, pl.ds(p * WIDE + j * BLOCK, BLOCK)]
                dx += dot(grads, w_refs[2 * s + j][p], ((1,), (1,)))
        dx = dx.astype(BF16)
        for t in range(2):
            for f in range(2):
                part = dx[t * TOK : (t + 1) * TOK, f * TOK : (f + 1) * TOK]
                dx_ref[chunk(place_ref, t, 2 * s + f)] = part


def input_terms(place, grads, *weights):
    return pl.pallas_call(
        input_kernel,
        out_shape=jax.ShapeDtypeStruct((16, TOK, TOK), BF16),
        in_specs=[SCALARS] + [WHOLE] * 9,
        out_specs=WHOLE,
        compiler_params=params(),
        cost_estimate=pl.CostEstimate(flops=540000000, bytes_accessed=4000000, transcendentals=0),
        name="input_terms",
    )(place, grads, *weights)


def weight_kernel(
    place_ref, acts_ref, other_acts_ref, grads_ref, other_grads_ref, keep_ref, z_ref, x_ref, xz_ref, wide_ref
):
    for p in range(2):
        for t in range(2):
            for f in range(4):
                x0 = place_ref[1] if f < 2 else 1 - place_ref[1]
                cols = pl.ds(f * TOK, TOK)
                mine = acts_ref[chunk(place_ref, t, f), p]
                wide_ref[p, pl.ds(t * TOK, TOK), cols] = mine
                wide_ref[p, pl.ds(TOKENS + t * TOK, TOK), cols] = other_acts_ref[x0, 2 * t + f % 2, p]
    for side in (1, 0):
        for p in range(3):
            for j in range(2):
                cols = pl.ds(p * WIDE + j * BLOCK, BLOCK)
                term = jnp.zeros((BLOCK, BLOCK), F32)
                for i, ref in enumerate((grads_ref, other_grads_ref)):
                    x = wide_ref[p // 2, pl.ds(i * TOKENS, TOKENS), pl.ds(side * BLOCK, BLOCK)]
                    term += dot(x, ref[:, cols], ((0,), (0,)))
                out_ref = ((keep_ref, z_ref), (x_ref, xz_ref))[side][j]
                out_ref[p] = term.astype(out_ref.dtype)


def weight_terms(place, acts, other_acts, grads, other_grads):
    shape = (3, BLOCK, BLOCK)
    send = jax.ShapeDtypeStruct(shape, BF16)
    return pl.pallas_call(
        weight_kernel,
        out_shape=(jax.ShapeDtypeStruct(shape, F32), send, send, send),
        in_specs=[SCALARS] + [WHOLE] * 4,
        out_specs=(WHOLE,) * 4,
        scratch_shapes=[pltpu.VMEM((2, 2 * TOKENS, WIDE), BF16)],
        compiler_params=params(),
        cost_estimate=pl.CostEstimate(flops=800000000, bytes_accessed=6000000, transcendentals=0),
        name="weight_terms",
    )(place, acts, other_acts, grads, other_grads)


def exchange(pieces, axes):
    return lax.all_to_all(pieces, axes, split_axis=0, concat_axis=0, tiled=True)


def local(inputs, out_grad, codes, scales):
    place = jnp.stack([lax.axis_index("core"), lax.axis_index("x0")])
    there = turned()

    acts = lax.ppermute(jnp.stack([inputs, out_grad]), AXES, there)
    w = (codes.astype(F32) * scales.astype(F32)).astype(BF16)
    w_z = lax.ppermute(w, "zl", SWAP)
    acts, w_z = lax.optimization_barrier((acts, w_z))
    weights = [w, w_z] + [lax.ppermute(block, "x0", SWAP) for block in (w, w_z)]
    weights += [lax.ppermute(block, "core", SWAP) for block in weights]
    acts = exchange(jnp.broadcast_to(acts[None], (16,) + acts.shape), ZH + YH)

    parts = gates(place, acts, *weights)
    other_acts = acts.reshape(2, 2, 4, 2, TOK, TOK)
    other_acts = lax.dynamic_index_in_dim(other_acts, 1 - place[0], axis=1, keepdims=False)
    other_acts = lax.ppermute(other_acts, "core", SWAP)
    parts = exchange(parts.reshape(4, SHARE, GRADS), REST)
    parts, other_acts = lax.optimization_barrier((parts, other_acts))
    grads = exchange(hidden_grads(parts), REST).reshape(TOKENS, GRADS)
    other_grads = lax.ppermute(grads, "core", SWAP)

    dx = exchange(input_terms(place, grads, *weights), ZH + YH)
    dx = jnp.sum(dx.astype(F32), axis=0).astype(BF16)
    input_grad = lax.ppermute(dx, AXES, [(b, a) for a, b in there])

    weight_grad, z, x, xz = weight_terms(place, acts, other_acts, grads, other_grads)
    weight_grad += lax.ppermute(z, "zl", SWAP).astype(F32)
    weight_grad += lax.ppermute(x, "x0", SWAP).astype(F32)
    weight_grad += lax.ppermute(xz, ("x0", "zl"), [(i, 3 - i) for i in range(4)]).astype(F32)
    return input_grad, weight_grad


def solution(mesh):
    fine = Mesh(mesh.devices.reshape((2,) * len(AXES)), AXES)
    return jax.shard_map(
        local,
        mesh=fine,
        in_specs=(P(ROW, COL), P(ROW, COL), P(None, ROW, COL), P(None, ROW, COL)),
        out_specs=(P(ROW, COL), P(None, ROW, COL)),
        check_vma=False,
    )
```

```python
import itertools

import jax
import jax.numpy as jnp
from jax import lax
from jax.experimental import pallas as pl
from jax.experimental.pallas import tpu as pltpu
from jax.sharding import Mesh, PartitionSpec as P

F32 = jnp.float32
BF16 = jnp.bfloat16
ROW = ("yl", "x1", "x0", "core")
COL = ("yh1", "yh0", "zh1", "zh0", "zl")
AXES = ROW + COL
YH = ("yh1", "yh0")
ZH = ("zh1", "zh0")
REST = ("yl", "x1")
SWAP = [(0, 1), (1, 0)]
TOK = 128
BLOCK = 256
WIDE = 2 * BLOCK
TOKENS = 2 * TOK
SHARE = TOKENS // 4
FEATURES = 4 * BLOCK
GRADS = 3 * WIDE
VMEM_LIMIT = 24 * 1024 * 1024
WHOLE = pl.BlockSpec(memory_space=pltpu.VMEM)
ANYWHERE = pl.BlockSpec(memory_space=pl.ANY)
SCALARS = pl.BlockSpec(memory_space=pltpu.SMEM)


def turned():
    pairs = []
    for bits in itertools.product(range(2), repeat=len(AXES)):
        yl, x1, x0, core, yh1, yh0, zh1, zh0, zl = bits
        there = (yh1, yh0, x0, core, yl, zl, zh1, zh0, x1)
        pairs.append(tuple(sum(b << (8 - i) for i, b in enumerate(at)) for at in (bits, there)))
    return pairs


def dot(a, b, dims):
    return lax.dot_general(a, b, (dims, ((), ())), preferred_element_type=F32)


def params():
    return pltpu.CompilerParams(vmem_limit_bytes=VMEM_LIMIT)


def chunk(place_ref, t, f):
    core, x0 = place_ref[0], place_ref[1]
    core = core if f < 4 else 1 - core
    x0 = x0 if f % 4 < 2 else 1 - x0
    return 8 * x0 + 4 * core + 2 * t + f % 2


def load_last(refs, last_ref, sems):
    loads = []
    for i, src in enumerate(refs[6:8]):
        src = src.at[pl.ds(0, last_ref.shape[1])]
        loads.append(pltpu.make_async_copy(src, last_ref.at[i], sems.at[i]))
        loads[-1].start()
    return list(refs[:6]) + [last_ref.at[0], last_ref.at[1]], loads


def gates_kernel(place_ref, acts_ref, *refs):
    parts_out, wide_ref, last_ref, parts_ref, in_sems, out_sems = refs[8:]
    w_refs, loads = load_last(refs, last_ref, in_sems)
    for p in range(2):
        for t in range(2):
            for f in range(8):
                block = acts_ref[chunk(place_ref, t, f), p]
                wide_ref[p, pl.ds(t * TOK, TOK), pl.ds(f * TOK, TOK)] = block
    stores = []
    for p in range(3):
        for j in range(2):
            total = jnp.zeros((TOKENS, BLOCK), F32)
            for s in range(4):
                if s == 3 and p == 0:
                    loads[j].wait()
                total += dot(wide_ref[p // 2, :, pl.ds(s * BLOCK, BLOCK)], w_refs[2 * s + j][p], ((1,), (0,)))
            parts_ref[:, pl.ds(p * WIDE + j * BLOCK, BLOCK)] = total.astype(BF16)
        cols = pl.ds(p * WIDE, WIDE)
        stores.append(
            pltpu.make_async_copy(parts_ref.at[:, cols], parts_out.at[:, cols], out_sems.at[p])
        )
        stores[-1].start()
    for store in stores:
        store.wait()


def gates(place, acts, *weights):
    return pl.pallas_call(
        gates_kernel,
        out_shape=jax.ShapeDtypeStruct((TOKENS, GRADS), BF16),
        in_specs=[SCALARS] + [WHOLE] * 7 + [ANYWHERE] * 2,
        out_specs=ANYWHERE,
        scratch_shapes=[
            pltpu.VMEM((2, TOKENS, FEATURES), BF16),
            pltpu.VMEM((2, 3, BLOCK, BLOCK), BF16),
            pltpu.VMEM((TOKENS, GRADS), BF16),
            pltpu.SemaphoreType.DMA((2,)),
            pltpu.SemaphoreType.DMA((3,)),
        ],
        compiler_params=params(),
        cost_estimate=pl.CostEstimate(flops=800000000, bytes_accessed=6000000, transcendentals=0),
        name="gates",
    )(place, acts, *weights)


def hidden_kernel(parts_ref, out_ref):
    total = parts_ref[0].astype(F32)
    for i in range(1, 4):
        total += parts_ref[i].astype(F32)
    gate, up, hidden_grad = (total[:, p * WIDE : (p + 1) * WIDE] for p in range(3))
    sig = 1.0 / (1.0 + jnp.exp(-gate))
    act = gate * sig
    gate_grad = (hidden_grad * up * sig * (1.0 + gate * (1.0 - sig))).astype(BF16)
    up_grad = (hidden_grad * act).astype(BF16)
    hidden = (act * up).astype(BF16)
    for i in range(4):
        for p, value in enumerate((gate_grad, up_grad, hidden)):
            out_ref[i, :, pl.ds(p * WIDE, WIDE)] = value


def hidden_grads(parts):
    return pl.pallas_call(
        hidden_kernel,
        out_shape=jax.ShapeDtypeStruct(parts.shape, BF16),
        in_specs=[WHOLE],
        out_specs=WHOLE,
        compiler_params=params(),
        cost_estimate=pl.CostEstimate(flops=2000000, bytes_accessed=1600000, transcendentals=32768),
        name="hidden_grads",
    )(parts)


def input_kernel(place_ref, grads_ref, *refs):
    dx_out, last_ref, dx_ref, in_sems, out_sems = refs[8:]
    w_refs, loads = load_last(refs, last_ref, in_sems)
    stores = []
    for s in range(4):
        if s == 3:
            for load in loads:
                load.wait()
        dx = jnp.zeros((TOKENS, BLOCK), F32)
        for p in range(2):
            for j in range(2):
                grads = grads_ref[:, pl.ds(p * WIDE + j * BLOCK, BLOCK)]
                dx += dot(grads, w_refs[2 * s + j][p], ((1,), (1,)))
        dx = dx.astype(BF16)
        for t in range(2):
            for f in range(2):
                at = chunk(place_ref, t, 2 * s + f)
                dx_ref[at] = dx[t * TOK : (t + 1) * TOK, f * TOK : (f + 1) * TOK]
                stores.append(
                    pltpu.make_async_copy(dx_ref.at[at], dx_out.at[at], out_sems.at[len(stores)])
                )
                stores[-1].start()
    for store in stores:
        store.wait()


def input_terms(place, grads, *weights):
    return pl.pallas_call(
        input_kernel,
        out_shape=jax.ShapeDtypeStruct((16, TOK, TOK), BF16),
        in_specs=[SCALARS] + [WHOLE] * 7 + [ANYWHERE] * 2,
        out_specs=ANYWHERE,
        scratch_shapes=[
            pltpu.VMEM((2, 2, BLOCK, BLOCK), BF16),
            pltpu.VMEM((16, TOK, TOK), BF16),
            pltpu.SemaphoreType.DMA((2,)),
            pltpu.SemaphoreType.DMA((16,)),
        ],
        compiler_params=params(),
        cost_estimate=pl.CostEstimate(flops=540000000, bytes_accessed=4000000, transcendentals=0),
        name="input_terms",
    )(place, grads, *weights)


def weight_kernel(
    place_ref, acts_ref, other_acts_ref, grads_ref, other_grads_in, keep_ref, z_out, x_out, xz_out,
    wide_ref, other_grads_ref, send_ref, in_sem, out_sems,
):
    load = pltpu.make_async_copy(other_grads_in, other_grads_ref, in_sem)
    load.start()
    for p in range(2):
        for t in range(2):
            for f in range(4):
                x0 = place_ref[1] if f < 2 else 1 - place_ref[1]
                cols = pl.ds(f * TOK, TOK)
                mine = acts_ref[chunk(place_ref, t, f), p]
                wide_ref[p, pl.ds(t * TOK, TOK), cols] = mine
                wide_ref[p, pl.ds(TOKENS + t * TOK, TOK), cols] = other_acts_ref[x0, 2 * t + f % 2, p]
    load.wait()
    stores = []
    for side, j in ((1, 1), (0, 1), (1, 0), (0, 0)):
        for p in range(3):
            cols = pl.ds(p * WIDE + j * BLOCK, BLOCK)
            term = jnp.zeros((BLOCK, BLOCK), F32)
            for i, ref in enumerate((grads_ref, other_grads_ref)):
                x = wide_ref[p // 2, pl.ds(i * TOKENS, TOKENS), pl.ds(side * BLOCK, BLOCK)]
                term += dot(x, ref[:, cols], ((0,), (0,)))
            if side or j:
                send_ref[2 * side + j - 1, p] = term.astype(BF16)
            else:
                keep_ref[p] = term
        if side or j:
            at = 2 * side + j - 1
            out = (z_out, x_out, xz_out)[at]
            stores.append(pltpu.make_async_copy(send_ref.at[at], out, out_sems.at[at]))
            stores[-1].start()
    for store in stores:
        store.wait()


def weight_terms(place, acts, other_acts, grads, other_grads):
    shape = (3, BLOCK, BLOCK)
    send = jax.ShapeDtypeStruct(shape, BF16)
    return pl.pallas_call(
        weight_kernel,
        out_shape=(jax.ShapeDtypeStruct(shape, F32), send, send, send),
        in_specs=[SCALARS] + [WHOLE] * 3 + [ANYWHERE],
        out_specs=(WHOLE,) + (ANYWHERE,) * 3,
        scratch_shapes=[
            pltpu.VMEM((2, 2 * TOKENS, WIDE), BF16),
            pltpu.VMEM((TOKENS, GRADS), BF16),
            pltpu.VMEM((3,) + shape, BF16),
            pltpu.SemaphoreType.DMA,
            pltpu.SemaphoreType.DMA((3,)),
        ],
        compiler_params=params(),
        cost_estimate=pl.CostEstimate(flops=800000000, bytes_accessed=6000000, transcendentals=0),
        name="weight_terms",
    )(place, acts, other_acts, grads, other_grads)


def exchange(pieces, axes):
    return lax.all_to_all(pieces, axes, split_axis=0, concat_axis=0, tiled=True)


def local(inputs, out_grad, codes, scales):
    place = jnp.stack([lax.axis_index("core"), lax.axis_index("x0")])
    there = turned()

    acts = lax.ppermute(jnp.stack([inputs, out_grad]), AXES, there)
    w = (codes.astype(F32) * scales.astype(F32)).astype(BF16)
    w_z = lax.ppermute(w, "zl", SWAP)
    acts, w_z = lax.optimization_barrier((acts, w_z))
    weights = [w, w_z] + [lax.ppermute(block, "x0", SWAP) for block in (w, w_z)]
    weights += [lax.ppermute(block, "core", SWAP) for block in weights]
    acts = exchange(jnp.broadcast_to(acts[None], (16,) + acts.shape), ZH + YH)

    parts = gates(place, acts, *weights)
    other_acts = acts.reshape(2, 2, 4, 2, TOK, TOK)
    other_acts = lax.dynamic_index_in_dim(other_acts, 1 - place[0], axis=1, keepdims=False)
    other_acts = lax.ppermute(other_acts, "core", SWAP)
    parts = exchange(parts.reshape(4, SHARE, GRADS), REST)
    parts, other_acts = lax.optimization_barrier((parts, other_acts))
    grads = exchange(hidden_grads(parts), REST).reshape(TOKENS, GRADS)
    other_grads = lax.ppermute(grads, "core", SWAP)

    dx = exchange(input_terms(place, grads, *weights), ZH + YH)
    dx = jnp.sum(dx.astype(F32), axis=0).astype(BF16)
    input_grad = lax.ppermute(dx, AXES, [(b, a) for a, b in there])

    weight_grad, z, x, xz = weight_terms(place, acts, other_acts, grads, other_grads)
    weight_grad += lax.ppermute(z, "zl", SWAP).astype(F32)
    weight_grad += lax.ppermute(x, "x0", SWAP).astype(F32)
    weight_grad += lax.ppermute(xz, ("x0", "zl"), [(i, 3 - i) for i in range(4)]).astype(F32)
    return input_grad, weight_grad


def solution(mesh):
    fine = Mesh(mesh.devices.reshape((2,) * len(AXES)), AXES)
    return jax.shard_map(
        local,
        mesh=fine,
        in_specs=(P(ROW, COL), P(ROW, COL), P(None, ROW, COL), P(None, ROW, COL)),
        out_specs=(P(ROW, COL), P(None, ROW, COL)),
        check_vma=False,
    )
```

```python
import itertools

import jax
import jax.numpy as jnp
from jax import lax
from jax.experimental import pallas as pl
from jax.experimental.pallas import tpu as pltpu
from jax.sharding import Mesh, PartitionSpec as P

F32 = jnp.float32
BF16 = jnp.bfloat16
ROW = ("yl", "x1", "x0", "core")
COL = ("yh1", "yh0", "zh1", "zh0", "zl")
AXES = ROW + COL
SPREAD = ("zh1", "zh0", "yh0")
REST = ("yl", "x1")
SWAP = [(0, 1), (1, 0)]
TOK = 128
BLOCK = 256
WIDE = 2 * BLOCK
TOKENS = 2 * TOK
SHARE = TOKENS // 4
FEATURES = 4 * BLOCK
GRADS = 3 * WIDE
VMEM_LIMIT = 24 * 1024 * 1024
WHOLE = pl.BlockSpec(memory_space=pltpu.VMEM)
SCALARS = pl.BlockSpec(memory_space=pltpu.SMEM)


def turned(flip):
    pairs = []
    for bits in itertools.product(range(2), repeat=len(AXES)):
        yl, x1, x0, core, yh1, yh0, zh1, zh0, zl = bits
        there = (yh1, yh0, x0, core, yl ^ flip, zl, zh1, zh0, x1)
        pairs.append(tuple(sum(b << (8 - i) for i, b in enumerate(at)) for at in (bits, there)))
    return pairs


def dot(a, b, dims):
    return lax.dot_general(a, b, (dims, ((), ())), preferred_element_type=F32)


def params():
    return pltpu.CompilerParams(vmem_limit_bytes=VMEM_LIMIT)


def chunk(place_ref, f):
    core, x0 = place_ref[0], place_ref[1]
    core = core if f < 4 else 1 - core
    x0 = x0 if f % 4 < 2 else 1 - x0
    return 4 * x0 + 2 * core + f % 2


def gates_kernel(place_ref, acts_ref, *refs):
    w_refs, parts_ref, wide_ref = refs[:8], refs[8], refs[9]
    for p in range(2):
        for t in range(2):
            for f in range(8):
                block = acts_ref[chunk(place_ref, f), t, p]
                wide_ref[p, pl.ds(t * TOK, TOK), pl.ds(f * TOK, TOK)] = block
    for p in range(3):
        for j in range(2):
            total = jnp.zeros((TOKENS, BLOCK), F32)
            for s in range(4):
                total += dot(wide_ref[p // 2, :, pl.ds(s * BLOCK, BLOCK)], w_refs[2 * s + j][p], ((1,), (0,)))
            parts_ref[:, pl.ds(p * WIDE + j * BLOCK, BLOCK)] = total.astype(BF16)


def gates(place, acts, *weights):
    return pl.pallas_call(
        gates_kernel,
        out_shape=jax.ShapeDtypeStruct((TOKENS, GRADS), BF16),
        in_specs=[SCALARS] + [WHOLE] * 9,
        out_specs=WHOLE,
        scratch_shapes=[pltpu.VMEM((2, TOKENS, FEATURES), BF16)],
        compiler_params=params(),
        cost_estimate=pl.CostEstimate(flops=800000000, bytes_accessed=6000000, transcendentals=0),
        name="gates",
    )(place, acts, *weights)


def hidden_kernel(parts_ref, out_ref):
    total = parts_ref[0].astype(F32)
    for i in range(1, 4):
        total += parts_ref[i].astype(F32)
    gate, up, hidden_grad = (total[:, p * WIDE : (p + 1) * WIDE] for p in range(3))
    sig = 1.0 / (1.0 + jnp.exp(-gate))
    act = gate * sig
    gate_grad = (hidden_grad * up * sig * (1.0 + gate * (1.0 - sig))).astype(BF16)
    up_grad = (hidden_grad * act).astype(BF16)
    hidden = (act * up).astype(BF16)
    for i in range(4):
        for p, value in enumerate((gate_grad, up_grad, hidden)):
            out_ref[i, :, pl.ds(p * WIDE, WIDE)] = value


def hidden_grads(parts):
    return pl.pallas_call(
        hidden_kernel,
        out_shape=jax.ShapeDtypeStruct(parts.shape, BF16),
        in_specs=[WHOLE],
        out_specs=WHOLE,
        compiler_params=params(),
        cost_estimate=pl.CostEstimate(flops=2000000, bytes_accessed=1600000, transcendentals=32768),
        name="hidden_grads",
    )(parts)


def input_kernel(place_ref, grads_ref, *refs):
    w_refs, dx_ref = refs[:8], refs[8]
    for s in range(4):
        dx = jnp.zeros((TOKENS, BLOCK), F32)
        for p in range(2):
            for j in range(2):
                grads = grads_ref[:, pl.ds(p * WIDE + j * BLOCK, BLOCK)]
                dx += dot(grads, w_refs[2 * s + j][p], ((1,), (1,)))
        dx = dx.astype(BF16)
        for t in range(2):
            for f in range(2):
                part = dx[t * TOK : (t + 1) * TOK, f * TOK : (f + 1) * TOK]
                dx_ref[chunk(place_ref, 2 * s + f), t] = part


def input_terms(place, grads, *weights):
    return pl.pallas_call(
        input_kernel,
        out_shape=jax.ShapeDtypeStruct((8, 2, TOK, TOK), BF16),
        in_specs=[SCALARS] + [WHOLE] * 9,
        out_specs=WHOLE,
        compiler_params=params(),
        cost_estimate=pl.CostEstimate(flops=540000000, bytes_accessed=4000000, transcendentals=0),
        name="input_terms",
    )(place, grads, *weights)


def weight_kernel(
    place_ref, acts_ref, other_acts_ref, grads_ref, other_grads_ref, keep_ref, z_ref, x_ref, xz_ref, wide_ref
):
    for p in range(2):
        for t in range(2):
            for f in range(4):
                x0 = place_ref[1] if f < 2 else 1 - place_ref[1]
                cols = pl.ds(f * TOK, TOK)
                mine = acts_ref[chunk(place_ref, f), t, p]
                wide_ref[p, pl.ds(t * TOK, TOK), cols] = mine
                wide_ref[p, pl.ds(TOKENS + t * TOK, TOK), cols] = other_acts_ref[x0, f % 2, t, p]
    for side in (1, 0):
        for p in range(3):
            for j in range(2):
                cols = pl.ds(p * WIDE + j * BLOCK, BLOCK)
                term = jnp.zeros((BLOCK, BLOCK), F32)
                for i, ref in enumerate((grads_ref, other_grads_ref)):
                    x = wide_ref[p // 2, pl.ds(i * TOKENS, TOKENS), pl.ds(side * BLOCK, BLOCK)]
                    term += dot(x, ref[:, cols], ((0,), (0,)))
                out_ref = ((keep_ref, z_ref), (x_ref, xz_ref))[side][j]
                out_ref[p] = term.astype(out_ref.dtype)


def weight_terms(place, acts, other_acts, grads, other_grads):
    shape = (3, BLOCK, BLOCK)
    send = jax.ShapeDtypeStruct(shape, BF16)
    return pl.pallas_call(
        weight_kernel,
        out_shape=(jax.ShapeDtypeStruct(shape, F32), send, send, send),
        in_specs=[SCALARS] + [WHOLE] * 4,
        out_specs=(WHOLE,) * 4,
        scratch_shapes=[pltpu.VMEM((2, 2 * TOKENS, WIDE), BF16)],
        compiler_params=params(),
        cost_estimate=pl.CostEstimate(flops=800000000, bytes_accessed=6000000, transcendentals=0),
        name="weight_terms",
    )(place, acts, other_acts, grads, other_grads)


def exchange(pieces, axes):
    return lax.all_to_all(pieces, axes, split_axis=0, concat_axis=0, tiled=True)


def local(inputs, out_grad, codes, scales):
    place = jnp.stack([lax.axis_index("core"), lax.axis_index("x0")])
    there = [turned(flip) for flip in range(2)]

    acts = jnp.stack([inputs, out_grad])
    acts = jnp.stack([lax.ppermute(acts, AXES, pairs) for pairs in there])
    w = (codes.astype(F32) * scales.astype(F32)).astype(BF16)
    w_z = lax.ppermute(w, "zl", SWAP)
    acts, w_z = lax.optimization_barrier((acts, w_z))
    weights = [w, w_z] + [lax.ppermute(block, "x0", SWAP) for block in (w, w_z)]
    weights += [lax.ppermute(block, "core", SWAP) for block in weights]
    acts = exchange(jnp.broadcast_to(acts[None], (8,) + acts.shape), SPREAD)

    parts = gates(place, acts, *weights)
    other_acts = acts.reshape(2, 2, 2, 2, 2, TOK, TOK)
    other_acts = lax.dynamic_index_in_dim(other_acts, 1 - place[0], axis=1, keepdims=False)
    other_acts = lax.ppermute(other_acts, "core", SWAP)
    parts = exchange(parts.reshape(4, SHARE, GRADS), REST)
    parts, other_acts = lax.optimization_barrier((parts, other_acts))
    grads = exchange(hidden_grads(parts), REST).reshape(TOKENS, GRADS)
    other_grads = lax.ppermute(grads, "core", SWAP)

    dx = exchange(input_terms(place, grads, *weights), SPREAD)
    dx = jnp.sum(dx.astype(F32), axis=0).astype(BF16)
    back = [lax.ppermute(dx[i], AXES, [(b, a) for a, b in there[i]]) for i in range(2)]
    input_grad = (back[0].astype(F32) + back[1].astype(F32)).astype(BF16)

    weight_grad, z, x, xz = weight_terms(place, acts, other_acts, grads, other_grads)
    weight_grad += lax.ppermute(z, "zl", SWAP).astype(F32)
    weight_grad += lax.ppermute(x, "x0", SWAP).astype(F32)
    weight_grad += lax.ppermute(xz, ("x0", "zl"), [(i, 3 - i) for i in range(4)]).astype(F32)
    return input_grad, weight_grad


def solution(mesh):
    fine = Mesh(mesh.devices.reshape((2,) * len(AXES)), AXES)
    return jax.shard_map(
        local,
        mesh=fine,
        in_specs=(P(ROW, COL), P(ROW, COL), P(None, ROW, COL), P(None, ROW, COL)),
        out_specs=(P(ROW, COL), P(None, ROW, COL)),
        check_vma=False,
    )
```

```python
import itertools

import jax
import jax.numpy as jnp
from jax import lax
from jax.experimental import pallas as pl
from jax.experimental.pallas import tpu as pltpu
from jax.sharding import Mesh, PartitionSpec as P

F32 = jnp.float32
BF16 = jnp.bfloat16
ROW = ("yl", "x1", "x0", "core")
COL = ("yh1", "yh0", "zh1", "zh0", "zl")
AXES = ROW + COL
SPREAD = ("zh1", "zh0", "yh0")
GATHER = SPREAD + ("yh1",)
REST = ("yl", "x1")
SWAP = [(0, 1), (1, 0)]
TOK = 128
BLOCK = 256
WIDE = 2 * BLOCK
TOKENS = 2 * TOK
SHARE = TOKENS // 4
FEATURES = 4 * BLOCK
GRADS = 3 * WIDE
VMEM_LIMIT = 24 * 1024 * 1024
WHOLE = pl.BlockSpec(memory_space=pltpu.VMEM)
SCALARS = pl.BlockSpec(memory_space=pltpu.SMEM)


def turned(flip):
    pairs = []
    for bits in itertools.product(range(2), repeat=len(AXES)):
        yl, x1, x0, core, yh1, yh0, zh1, zh0, zl = bits
        there = (yh1, yh0, x0, core, yl ^ flip, zl, zh1, zh0, x1)
        pairs.append(tuple(sum(b << (8 - i) for i, b in enumerate(at)) for at in (bits, there)))
    return pairs


def dot(a, b, dims):
    return lax.dot_general(a, b, (dims, ((), ())), preferred_element_type=F32)


def params():
    return pltpu.CompilerParams(vmem_limit_bytes=VMEM_LIMIT)


def chunk(place_ref, f):
    core, x0 = place_ref[0], place_ref[1]
    core = core if f < 4 else 1 - core
    x0 = x0 if f % 4 < 2 else 1 - x0
    return 4 * x0 + 2 * core + f % 2


def half(place_ref, t):
    return place_ref[2] if t == 0 else 1 - place_ref[2]


def spread_kernel(acts_ref, copies_out, sems):
    copies = [pltpu.make_async_copy(acts_ref, copies_out.at[i], sems.at[i]) for i in range(16)]
    for copy in copies:
        copy.start()
    for copy in copies:
        copy.wait()


def spread(acts):
    return pl.pallas_call(
        spread_kernel,
        out_shape=jax.ShapeDtypeStruct((16,) + acts.shape, BF16),
        in_specs=[WHOLE],
        out_specs=pl.BlockSpec(memory_space=pl.ANY),
        scratch_shapes=[pltpu.SemaphoreType.DMA((16,))],
        compiler_params=params(),
        cost_estimate=pl.CostEstimate(flops=0, bytes_accessed=1100000, transcendentals=0),
        name="spread",
    )(acts)


def gates_kernel(place_ref, acts_ref, *refs):
    w_refs, parts_ref, wide_ref = refs[:8], refs[8], refs[9]
    for p in range(2):
        for t in range(2):
            for f in range(8):
                block = acts_ref[chunk(place_ref, f), half(place_ref, t), p]
                wide_ref[p, pl.ds(t * TOK, TOK), pl.ds(f * TOK, TOK)] = block
    for p in range(3):
        for j in range(2):
            total = jnp.zeros((TOKENS, BLOCK), F32)
            for s in range(4):
                total += dot(wide_ref[p // 2, :, pl.ds(s * BLOCK, BLOCK)], w_refs[2 * s + j][p], ((1,), (0,)))
            parts_ref[:, pl.ds(p * WIDE + j * BLOCK, BLOCK)] = total.astype(BF16)


def gates(place, acts, *weights):
    return pl.pallas_call(
        gates_kernel,
        out_shape=jax.ShapeDtypeStruct((TOKENS, GRADS), BF16),
        in_specs=[SCALARS] + [WHOLE] * 9,
        out_specs=WHOLE,
        scratch_shapes=[pltpu.VMEM((2, TOKENS, FEATURES), BF16)],
        compiler_params=params(),
        cost_estimate=pl.CostEstimate(flops=800000000, bytes_accessed=6000000, transcendentals=0),
        name="gates",
    )(place, acts, *weights)


def hidden_kernel(parts_ref, out_ref):
    total = parts_ref[0].astype(F32)
    for i in range(1, 4):
        total += parts_ref[i].astype(F32)
    gate, up, hidden_grad = (total[:, p * WIDE : (p + 1) * WIDE] for p in range(3))
    sig = 1.0 / (1.0 + jnp.exp(-gate))
    act = gate * sig
    gate_grad = (hidden_grad * up * sig * (1.0 + gate * (1.0 - sig))).astype(BF16)
    up_grad = (hidden_grad * act).astype(BF16)
    hidden = (act * up).astype(BF16)
    for i in range(4):
        for p, value in enumerate((gate_grad, up_grad, hidden)):
            out_ref[i, :, pl.ds(p * WIDE, WIDE)] = value


def hidden_grads(parts):
    return pl.pallas_call(
        hidden_kernel,
        out_shape=jax.ShapeDtypeStruct(parts.shape, BF16),
        in_specs=[WHOLE],
        out_specs=WHOLE,
        compiler_params=params(),
        cost_estimate=pl.CostEstimate(flops=2000000, bytes_accessed=1600000, transcendentals=32768),
        name="hidden_grads",
    )(parts)


def input_kernel(place_ref, grads_ref, *refs):
    w_refs, dx_ref = refs[:8], refs[8]
    for s in range(4):
        dx = jnp.zeros((TOKENS, BLOCK), F32)
        for p in range(2):
            for j in range(2):
                grads = grads_ref[:, pl.ds(p * WIDE + j * BLOCK, BLOCK)]
                dx += dot(grads, w_refs[2 * s + j][p], ((1,), (1,)))
        dx = dx.astype(BF16)
        for t in range(2):
            for f in range(2):
                part = dx[t * TOK : (t + 1) * TOK, f * TOK : (f + 1) * TOK]
                dx_ref[chunk(place_ref, 2 * s + f), t] = part


def input_terms(place, grads, *weights):
    return pl.pallas_call(
        input_kernel,
        out_shape=jax.ShapeDtypeStruct((8, 2, TOK, TOK), BF16),
        in_specs=[SCALARS] + [WHOLE] * 9,
        out_specs=WHOLE,
        compiler_params=params(),
        cost_estimate=pl.CostEstimate(flops=540000000, bytes_accessed=4000000, transcendentals=0),
        name="input_terms",
    )(place, grads, *weights)


def weight_kernel(
    place_ref, acts_ref, other_acts_ref, grads_ref, other_grads_ref, keep_ref, z_ref, x_ref, xz_ref, wide_ref
):
    for p in range(2):
        for t in range(2):
            for f in range(4):
                x0 = place_ref[1] if f < 2 else 1 - place_ref[1]
                cols = pl.ds(f * TOK, TOK)
                mine = acts_ref[chunk(place_ref, f), half(place_ref, t), p]
                wide_ref[p, pl.ds(t * TOK, TOK), cols] = mine
                wide_ref[p, pl.ds(TOKENS + t * TOK, TOK), cols] = other_acts_ref[x0, f % 2, half(place_ref, t), p]
    for side in (1, 0):
        for p in range(3):
            for j in range(2):
                cols = pl.ds(p * WIDE + j * BLOCK, BLOCK)
                term = jnp.zeros((BLOCK, BLOCK), F32)
                for i, ref in enumerate((grads_ref, other_grads_ref)):
                    x = wide_ref[p // 2, pl.ds(i * TOKENS, TOKENS), pl.ds(side * BLOCK, BLOCK)]
                    term += dot(x, ref[:, cols], ((0,), (0,)))
                out_ref = ((keep_ref, z_ref), (x_ref, xz_ref))[side][j]
                out_ref[p] = term.astype(out_ref.dtype)


def weight_terms(place, acts, other_acts, grads, other_grads):
    shape = (3, BLOCK, BLOCK)
    send = jax.ShapeDtypeStruct(shape, BF16)
    return pl.pallas_call(
        weight_kernel,
        out_shape=(jax.ShapeDtypeStruct(shape, F32), send, send, send),
        in_specs=[SCALARS] + [WHOLE] * 4,
        out_specs=(WHOLE,) * 4,
        scratch_shapes=[pltpu.VMEM((2, 2 * TOKENS, WIDE), BF16)],
        compiler_params=params(),
        cost_estimate=pl.CostEstimate(flops=800000000, bytes_accessed=6000000, transcendentals=0),
        name="weight_terms",
    )(place, acts, other_acts, grads, other_grads)


def exchange(pieces, axes):
    return lax.all_to_all(pieces, axes, split_axis=0, concat_axis=0, tiled=True)


def local(inputs, out_grad, codes, scales):
    place = jnp.stack([lax.axis_index("core"), lax.axis_index("x0"), lax.axis_index("yh1")])
    there = [turned(flip) for flip in range(2)]

    acts = spread(lax.ppermute(jnp.stack([inputs, out_grad]), AXES, there[0]))
    w = (codes.astype(F32) * scales.astype(F32)).astype(BF16)
    w_z = lax.ppermute(w, "zl", SWAP)
    acts, w_z = lax.optimization_barrier((acts, w_z))
    weights = [w, w_z] + [lax.ppermute(block, "x0", SWAP) for block in (w, w_z)]
    weights += [lax.ppermute(block, "core", SWAP) for block in weights]
    acts = exchange(acts, GATHER).reshape(8, 2, 2, TOK, TOK)

    parts = gates(place, acts, *weights)
    other_acts = acts.reshape(2, 2, 2, 2, 2, TOK, TOK)
    other_acts = lax.dynamic_index_in_dim(other_acts, 1 - place[0], axis=1, keepdims=False)
    other_acts = lax.ppermute(other_acts, "core", SWAP)
    parts = exchange(parts.reshape(4, SHARE, GRADS), REST)
    parts, other_acts = lax.optimization_barrier((parts, other_acts))
    grads = exchange(hidden_grads(parts), REST).reshape(TOKENS, GRADS)
    other_grads = lax.ppermute(grads, "core", SWAP)

    dx = exchange(input_terms(place, grads, *weights), SPREAD)
    dx = jnp.sum(dx.astype(F32), axis=0).astype(BF16)
    back = [lax.ppermute(dx[i], AXES, [(b, a) for a, b in there[i]]) for i in range(2)]
    input_grad = (back[0].astype(F32) + back[1].astype(F32)).astype(BF16)

    weight_grad, z, x, xz = weight_terms(place, acts, other_acts, grads, other_grads)
    weight_grad += lax.ppermute(z, "zl", SWAP).astype(F32)
    weight_grad += lax.ppermute(x, "x0", SWAP).astype(F32)
    weight_grad += lax.ppermute(xz, ("x0", "zl"), [(i, 3 - i) for i in range(4)]).astype(F32)
    return input_grad, weight_grad


def solution(mesh):
    fine = Mesh(mesh.devices.reshape((2,) * len(AXES)), AXES)
    return jax.shard_map(
        local,
        mesh=fine,
        in_specs=(P(ROW, COL), P(ROW, COL), P(None, ROW, COL), P(None, ROW, COL)),
        out_specs=(P(ROW, COL), P(None, ROW, COL)),
        check_vma=False,
    )
```

```python
import itertools

import jax
import jax.numpy as jnp
from jax import lax
from jax.experimental import pallas as pl
from jax.experimental.pallas import tpu as pltpu
from jax.sharding import Mesh, PartitionSpec as P

F32 = jnp.float32
BF16 = jnp.bfloat16
ROW = ("yl", "x1", "x0", "core")
COL = ("yh1", "yh0", "zh1", "zh0", "zl")
AXES = ROW + COL
SPREAD = ("zh1", "zh0", "yh0")
GATHER = SPREAD + ("yh1",)
REST = ("yl", "x1")
SWAP = [(0, 1), (1, 0)]
TOK = 128
BLOCK = 256
WIDE = 2 * BLOCK
TOKENS = 2 * TOK
SHARE = TOKENS // 4
FEATURES = 4 * BLOCK
GRADS = 3 * WIDE
EARLY = 2
VMEM_LIMIT = 24 * 1024 * 1024
WHOLE = pl.BlockSpec(memory_space=pltpu.VMEM)
SCALARS = pl.BlockSpec(memory_space=pltpu.SMEM)


def turned(flip):
    pairs = []
    for bits in itertools.product(range(2), repeat=len(AXES)):
        yl, x1, x0, core, yh1, yh0, zh1, zh0, zl = bits
        there = (yh1, yh0, x0, core, yl ^ flip, zl, zh1, zh0, x1)
        pairs.append(tuple(sum(b << (8 - i) for i, b in enumerate(at)) for at in (bits, there)))
    return pairs


def dot(a, b, dims):
    return lax.dot_general(a, b, (dims, ((), ())), preferred_element_type=F32)


def params():
    return pltpu.CompilerParams(vmem_limit_bytes=VMEM_LIMIT)


def chunk(place_ref, f):
    core, x0 = place_ref[0], place_ref[1]
    core = core if f < 4 else 1 - core
    x0 = x0 if f % 4 < 2 else 1 - x0
    return 4 * x0 + 2 * core + f % 2


def half(place_ref, t):
    return place_ref[2] if t == 0 else 1 - place_ref[2]


def spread_kernel(acts_ref, copies_out, sems):
    copies = [pltpu.make_async_copy(acts_ref, copies_out.at[i], sems.at[i]) for i in range(16)]
    for copy in copies:
        copy.start()
    for copy in copies:
        copy.wait()


def spread(acts):
    return pl.pallas_call(
        spread_kernel,
        out_shape=jax.ShapeDtypeStruct((16,) + acts.shape, BF16),
        in_specs=[WHOLE],
        out_specs=pl.BlockSpec(memory_space=pl.ANY),
        scratch_shapes=[pltpu.SemaphoreType.DMA((16,))],
        compiler_params=params(),
        cost_estimate=pl.CostEstimate(flops=0, bytes_accessed=1100000, transcendentals=0),
        name="spread",
    )(acts)


def block_of(w_refs, s, j, p):
    if s < 2:
        return w_refs[2 * s + j][p]
    if s == 3:
        return w_refs[4][3 * j + p]
    if j == 0:
        return w_refs[5][p]
    return w_refs[4][6 + p] if p < EARLY else w_refs[5][3 + p - EARLY]


def gates_kernel(place_ref, acts_ref, *refs):
    w_refs, parts_ref, wide_ref = refs[:6], refs[6], refs[7]
    for p in range(2):
        for t in range(2):
            for f in range(8):
                block = acts_ref[chunk(place_ref, f), half(place_ref, t), p]
                wide_ref[p, pl.ds(t * TOK, TOK), pl.ds(f * TOK, TOK)] = block
    for p in range(3):
        for j in range(2):
            total = jnp.zeros((TOKENS, BLOCK), F32)
            for s in range(4):
                total += dot(wide_ref[p // 2, :, pl.ds(s * BLOCK, BLOCK)], block_of(w_refs, s, j, p), ((1,), (0,)))
            parts_ref[:, pl.ds(p * WIDE + j * BLOCK, BLOCK)] = total.astype(BF16)


def gates(place, acts, *weights):
    return pl.pallas_call(
        gates_kernel,
        out_shape=jax.ShapeDtypeStruct((TOKENS, GRADS), BF16),
        in_specs=[SCALARS] + [WHOLE] * 7,
        out_specs=WHOLE,
        scratch_shapes=[pltpu.VMEM((2, TOKENS, FEATURES), BF16)],
        compiler_params=params(),
        cost_estimate=pl.CostEstimate(flops=800000000, bytes_accessed=6000000, transcendentals=0),
        name="gates",
    )(place, acts, *weights)


def hidden_kernel(parts_ref, out_ref):
    total = parts_ref[0].astype(F32)
    for i in range(1, 4):
        total += parts_ref[i].astype(F32)
    gate, up, hidden_grad = (total[:, p * WIDE : (p + 1) * WIDE] for p in range(3))
    sig = 1.0 / (1.0 + jnp.exp(-gate))
    act = gate * sig
    gate_grad = (hidden_grad * up * sig * (1.0 + gate * (1.0 - sig))).astype(BF16)
    up_grad = (hidden_grad * act).astype(BF16)
    hidden = (act * up).astype(BF16)
    for i in range(4):
        for p, value in enumerate((gate_grad, up_grad, hidden)):
            out_ref[i, :, pl.ds(p * WIDE, WIDE)] = value


def hidden_grads(parts):
    return pl.pallas_call(
        hidden_kernel,
        out_shape=jax.ShapeDtypeStruct(parts.shape, BF16),
        in_specs=[WHOLE],
        out_specs=WHOLE,
        compiler_params=params(),
        cost_estimate=pl.CostEstimate(flops=2000000, bytes_accessed=1600000, transcendentals=32768),
        name="hidden_grads",
    )(parts)


def input_kernel(place_ref, grads_ref, *refs):
    w_refs, dx_ref = refs[:6], refs[6]
    for s in range(4):
        dx = jnp.zeros((TOKENS, BLOCK), F32)
        for p in range(2):
            for j in range(2):
                grads = grads_ref[:, pl.ds(p * WIDE + j * BLOCK, BLOCK)]
                dx += dot(grads, block_of(w_refs, s, j, p), ((1,), (1,)))
        dx = dx.astype(BF16)
        for t in range(2):
            for f in range(2):
                part = dx[t * TOK : (t + 1) * TOK, f * TOK : (f + 1) * TOK]
                dx_ref[chunk(place_ref, 2 * s + f), t] = part


def input_terms(place, grads, *weights):
    return pl.pallas_call(
        input_kernel,
        out_shape=jax.ShapeDtypeStruct((8, 2, TOK, TOK), BF16),
        in_specs=[SCALARS] + [WHOLE] * 7,
        out_specs=WHOLE,
        compiler_params=params(),
        cost_estimate=pl.CostEstimate(flops=540000000, bytes_accessed=4000000, transcendentals=0),
        name="input_terms",
    )(place, grads, *weights)


def weight_kernel(
    place_ref, acts_ref, other_acts_ref, grads_ref, other_grads_ref, keep_ref, z_ref, x_ref, xz_ref, wide_ref
):
    for p in range(2):
        for t in range(2):
            for f in range(4):
                x0 = place_ref[1] if f < 2 else 1 - place_ref[1]
                cols = pl.ds(f * TOK, TOK)
                mine = acts_ref[chunk(place_ref, f), half(place_ref, t), p]
                wide_ref[p, pl.ds(t * TOK, TOK), cols] = mine
                wide_ref[p, pl.ds(TOKENS + t * TOK, TOK), cols] = other_acts_ref[x0, f % 2, half(place_ref, t), p]
    for side in (1, 0):
        for p in range(3):
            for j in range(2):
                cols = pl.ds(p * WIDE + j * BLOCK, BLOCK)
                term = jnp.zeros((BLOCK, BLOCK), F32)
                for i, ref in enumerate((grads_ref, other_grads_ref)):
                    x = wide_ref[p // 2, pl.ds(i * TOKENS, TOKENS), pl.ds(side * BLOCK, BLOCK)]
                    term += dot(x, ref[:, cols], ((0,), (0,)))
                out_ref = ((keep_ref, z_ref), (x_ref, xz_ref))[side][j]
                out_ref[p] = term.astype(out_ref.dtype)


def weight_terms(place, acts, other_acts, grads, other_grads):
    shape = (3, BLOCK, BLOCK)
    send = jax.ShapeDtypeStruct(shape, BF16)
    return pl.pallas_call(
        weight_kernel,
        out_shape=(jax.ShapeDtypeStruct(shape, F32), send, send, send),
        in_specs=[SCALARS] + [WHOLE] * 4,
        out_specs=(WHOLE,) * 4,
        scratch_shapes=[pltpu.VMEM((2, 2 * TOKENS, WIDE), BF16)],
        compiler_params=params(),
        cost_estimate=pl.CostEstimate(flops=800000000, bytes_accessed=6000000, transcendentals=0),
        name="weight_terms",
    )(place, acts, other_acts, grads, other_grads)


def exchange(pieces, axes):
    return lax.all_to_all(pieces, axes, split_axis=0, concat_axis=0, tiled=True)


def local(inputs, out_grad, codes, scales):
    place = jnp.stack([lax.axis_index("core"), lax.axis_index("x0"), lax.axis_index("yh1")])
    there = [turned(flip) for flip in range(2)]

    acts = spread(lax.ppermute(jnp.stack([inputs, out_grad]), AXES, there[0]))
    w = (codes.astype(F32) * scales.astype(F32)).astype(BF16)
    w_z = lax.ppermute(w, "zl", SWAP)
    weights = [w, w_z] + [lax.ppermute(block, "x0", SWAP) for block in (w, w_z)]
    blocks = (weights[2], weights[3], w_z[:EARLY]), (w, w_z[EARLY:])
    weights += [lax.ppermute(jnp.concatenate(part), "core", SWAP) for part in blocks]
    acts = exchange(acts, GATHER).reshape(8, 2, 2, TOK, TOK)

    parts = gates(place, acts, *weights)
    other_acts = acts.reshape(2, 2, 2, 2, 2, TOK, TOK)
    other_acts = lax.dynamic_index_in_dim(other_acts, 1 - place[0], axis=1, keepdims=False)
    other_acts = lax.ppermute(other_acts, "core", SWAP)
    parts = exchange(parts.reshape(4, SHARE, GRADS), REST)
    parts, other_acts = lax.optimization_barrier((parts, other_acts))
    grads = exchange(hidden_grads(parts), REST).reshape(TOKENS, GRADS)
    other_grads = lax.ppermute(grads, "core", SWAP)

    dx = exchange(input_terms(place, grads, *weights), SPREAD)
    dx = jnp.sum(dx.astype(F32), axis=0).astype(BF16)
    back = [lax.ppermute(dx[i], AXES, [(b, a) for a, b in there[i]]) for i in range(2)]
    input_grad = (back[0].astype(F32) + back[1].astype(F32)).astype(BF16)

    weight_grad, z, x, xz = weight_terms(place, acts, other_acts, grads, other_grads)
    weight_grad += lax.ppermute(z, "zl", SWAP).astype(F32)
    weight_grad += lax.ppermute(x, "x0", SWAP).astype(F32)
    weight_grad += lax.ppermute(xz, ("x0", "zl"), [(i, 3 - i) for i in range(4)]).astype(F32)
    return input_grad, weight_grad


def solution(mesh):
    fine = Mesh(mesh.devices.reshape((2,) * len(AXES)), AXES)
    return jax.shard_map(
        local,
        mesh=fine,
        in_specs=(P(ROW, COL), P(ROW, COL), P(None, ROW, COL), P(None, ROW, COL)),
        out_specs=(P(ROW, COL), P(None, ROW, COL)),
        check_vma=False,
    )
```

```python
import itertools

import jax
import jax.numpy as jnp
from jax import lax
from jax.experimental import pallas as pl
from jax.experimental.pallas import tpu as pltpu
from jax.sharding import Mesh, PartitionSpec as P

F32 = jnp.float32
BF16 = jnp.bfloat16
ROW = ("yl", "x1", "x0", "core")
COL = ("yh1", "yh0", "zh1", "zh0", "zl")
AXES = ROW + COL
SPREAD = ("yh0", "zh1", "zh0")
GATHER = ("yh1",) + SPREAD
REST = ("yl", "x1")
SWAP = [(0, 1), (1, 0)]
TOK = 128
BLOCK = 256
WIDE = 2 * BLOCK
TOKENS = 2 * TOK
SHARE = TOKENS // 4
FEATURES = 4 * BLOCK
GRADS = 3 * WIDE
VMEM_LIMIT = 24 * 1024 * 1024
WHOLE = pl.BlockSpec(memory_space=pltpu.VMEM)
SCALARS = pl.BlockSpec(memory_space=pltpu.SMEM)


def turned(flip):
    pairs = []
    for bits in itertools.product(range(2), repeat=len(AXES)):
        yl, x1, x0, core, yh1, yh0, zh1, zh0, zl = bits
        there = (yh1, yh0, x0, core, yl ^ flip, zl, zh1, zh0, x1)
        pairs.append(tuple(sum(b << (8 - i) for i, b in enumerate(at)) for at in (bits, there)))
    return pairs


def dot(a, b, dims):
    return lax.dot_general(a, b, (dims, ((), ())), preferred_element_type=F32)


def params():
    return pltpu.CompilerParams(vmem_limit_bytes=VMEM_LIMIT)


def chunk(place_ref, f):
    core, x0 = place_ref[0], place_ref[1]
    core = core if f < 4 else 1 - core
    x0 = x0 if f % 4 < 2 else 1 - x0
    return 4 * (f % 2) + 2 * x0 + core


def half(place_ref, t):
    return place_ref[2] if t == 0 else 1 - place_ref[2]


def spread_kernel(acts_ref, copies_out, sems):
    copies = [pltpu.make_async_copy(acts_ref, copies_out.at[i], sems.at[i]) for i in range(16)]
    for copy in copies:
        copy.start()
    for copy in copies:
        copy.wait()


def spread(acts):
    return pl.pallas_call(
        spread_kernel,
        out_shape=jax.ShapeDtypeStruct((16,) + acts.shape, BF16),
        in_specs=[WHOLE],
        out_specs=pl.BlockSpec(memory_space=pl.ANY),
        scratch_shapes=[pltpu.SemaphoreType.DMA((16,))],
        compiler_params=params(),
        cost_estimate=pl.CostEstimate(flops=0, bytes_accessed=1100000, transcendentals=0),
        name="spread",
    )(acts)


def gates_kernel(place_ref, acts_ref, *refs):
    w_refs, parts_ref, wide_ref = refs[:8], refs[8], refs[9]
    for p in range(2):
        for t in range(2):
            for f in range(8):
                block = acts_ref[half(place_ref, t), chunk(place_ref, f), p]
                wide_ref[p, pl.ds(t * TOK, TOK), pl.ds(f * TOK, TOK)] = block
    for p in range(3):
        for j in range(2):
            total = jnp.zeros((TOKENS, BLOCK), F32)
            for s in range(4):
                total += dot(wide_ref[p // 2, :, pl.ds(s * BLOCK, BLOCK)], w_refs[2 * s + j][p], ((1,), (0,)))
            parts_ref[:, pl.ds(p * WIDE + j * BLOCK, BLOCK)] = total.astype(BF16)


def gates(place, acts, *weights):
    return pl.pallas_call(
        gates_kernel,
        out_shape=jax.ShapeDtypeStruct((TOKENS, GRADS), BF16),
        in_specs=[SCALARS] + [WHOLE] * 9,
        out_specs=WHOLE,
        scratch_shapes=[pltpu.VMEM((2, TOKENS, FEATURES), BF16)],
        compiler_params=params(),
        cost_estimate=pl.CostEstimate(flops=800000000, bytes_accessed=6000000, transcendentals=0),
        name="gates",
    )(place, acts, *weights)


def hidden_kernel(parts_ref, out_ref):
    total = parts_ref[0].astype(F32)
    for i in range(1, 4):
        total += parts_ref[i].astype(F32)
    gate, up, hidden_grad = (total[:, p * WIDE : (p + 1) * WIDE] for p in range(3))
    sig = 1.0 / (1.0 + jnp.exp(-gate))
    act = gate * sig
    gate_grad = (hidden_grad * up * sig * (1.0 + gate * (1.0 - sig))).astype(BF16)
    up_grad = (hidden_grad * act).astype(BF16)
    hidden = (act * up).astype(BF16)
    for i in range(4):
        for p, value in enumerate((gate_grad, up_grad, hidden)):
            out_ref[i, :, pl.ds(p * WIDE, WIDE)] = value


def hidden_grads(parts):
    return pl.pallas_call(
        hidden_kernel,
        out_shape=jax.ShapeDtypeStruct(parts.shape, BF16),
        in_specs=[WHOLE],
        out_specs=WHOLE,
        compiler_params=params(),
        cost_estimate=pl.CostEstimate(flops=2000000, bytes_accessed=1600000, transcendentals=32768),
        name="hidden_grads",
    )(parts)


def input_kernel(place_ref, grads_ref, *refs):
    w_refs, dx_ref = refs[:8], refs[8]
    for s in range(4):
        dx = jnp.zeros((TOKENS, BLOCK), F32)
        for p in range(2):
            for j in range(2):
                grads = grads_ref[:, pl.ds(p * WIDE + j * BLOCK, BLOCK)]
                dx += dot(grads, w_refs[2 * s + j][p], ((1,), (1,)))
        dx = dx.astype(BF16)
        for t in range(2):
            for f in range(2):
                part = dx[t * TOK : (t + 1) * TOK, f * TOK : (f + 1) * TOK]
                dx_ref[chunk(place_ref, 2 * s + f), t] = part


def input_terms(place, grads, *weights):
    return pl.pallas_call(
        input_kernel,
        out_shape=jax.ShapeDtypeStruct((8, 2, TOK, TOK), BF16),
        in_specs=[SCALARS] + [WHOLE] * 9,
        out_specs=WHOLE,
        compiler_params=params(),
        cost_estimate=pl.CostEstimate(flops=540000000, bytes_accessed=4000000, transcendentals=0),
        name="input_terms",
    )(place, grads, *weights)


def weight_kernel(
    place_ref, acts_ref, other_acts_ref, grads_ref, other_grads_ref, keep_ref, z_ref, x_ref, xz_ref, wide_ref
):
    for p in range(2):
        for t in range(2):
            for f in range(4):
                x0 = place_ref[1] if f < 2 else 1 - place_ref[1]
                cols = pl.ds(f * TOK, TOK)
                mine = acts_ref[half(place_ref, t), chunk(place_ref, f), p]
                wide_ref[p, pl.ds(t * TOK, TOK), cols] = mine
                wide_ref[p, pl.ds(TOKENS + t * TOK, TOK), cols] = other_acts_ref[half(place_ref, t), f % 2, x0, p]
    for side in (1, 0):
        for p in range(3):
            for j in range(2):
                cols = pl.ds(p * WIDE + j * BLOCK, BLOCK)
                term = jnp.zeros((BLOCK, BLOCK), F32)
                for i, ref in enumerate((grads_ref, other_grads_ref)):
                    x = wide_ref[p // 2, pl.ds(i * TOKENS, TOKENS), pl.ds(side * BLOCK, BLOCK)]
                    term += dot(x, ref[:, cols], ((0,), (0,)))
                out_ref = ((keep_ref, z_ref), (x_ref, xz_ref))[side][j]
                out_ref[p] = term.astype(out_ref.dtype)


def weight_terms(place, acts, other_acts, grads, other_grads):
    shape = (3, BLOCK, BLOCK)
    send = jax.ShapeDtypeStruct(shape, BF16)
    return pl.pallas_call(
        weight_kernel,
        out_shape=(jax.ShapeDtypeStruct(shape, F32), send, send, send),
        in_specs=[SCALARS] + [WHOLE] * 4,
        out_specs=(WHOLE,) * 4,
        scratch_shapes=[pltpu.VMEM((2, 2 * TOKENS, WIDE), BF16)],
        compiler_params=params(),
        cost_estimate=pl.CostEstimate(flops=800000000, bytes_accessed=6000000, transcendentals=0),
        name="weight_terms",
    )(place, acts, other_acts, grads, other_grads)


def exchange(pieces, axes):
    return lax.all_to_all(pieces, axes, split_axis=0, concat_axis=0, tiled=True)


def local(inputs, out_grad, codes, scales):
    place = jnp.stack([lax.axis_index("core"), lax.axis_index("x0"), lax.axis_index("yh1")])
    there = [turned(flip) for flip in range(2)]

    acts = spread(lax.ppermute(jnp.stack([inputs, out_grad]), AXES, there[0]))
    w = (codes.astype(F32) * scales.astype(F32)).astype(BF16)
    w_z = lax.ppermute(w, "zl", SWAP)
    acts, w_z = lax.optimization_barrier((acts, w_z))
    weights = [w, w_z] + [lax.ppermute(block, "x0", SWAP) for block in (w, w_z)]
    weights += [lax.ppermute(block, "core", SWAP) for block in weights]
    acts = exchange(acts, GATHER).reshape(2, 8, 2, TOK, TOK)

    parts = gates(place, acts, *weights)
    other_acts = acts.reshape(2, 2, 2, 2, 2, TOK, TOK)
    other_acts = lax.dynamic_index_in_dim(other_acts, 1 - place[0], axis=3, keepdims=False)
    other_acts = lax.ppermute(other_acts, "core", SWAP)
    parts = exchange(parts.reshape(4, SHARE, GRADS), REST)
    parts, other_acts = lax.optimization_barrier((parts, other_acts))
    grads = exchange(hidden_grads(parts), REST).reshape(TOKENS, GRADS)
    other_grads = lax.ppermute(grads, "core", SWAP)

    dx = exchange(input_terms(place, grads, *weights), SPREAD)
    dx = jnp.sum(dx.astype(F32), axis=0).astype(BF16)
    back = [lax.ppermute(dx[i], AXES, [(b, a) for a, b in there[i]]) for i in range(2)]
    input_grad = (back[0].astype(F32) + back[1].astype(F32)).astype(BF16)

    weight_grad, z, x, xz = weight_terms(place, acts, other_acts, grads, other_grads)
    weight_grad += lax.ppermute(z, "zl", SWAP).astype(F32)
    weight_grad += lax.ppermute(x, "x0", SWAP).astype(F32)
    weight_grad += lax.ppermute(xz, ("x0", "zl"), [(i, 3 - i) for i in range(4)]).astype(F32)
    return input_grad, weight_grad


def solution(mesh):
    fine = Mesh(mesh.devices.reshape((2,) * len(AXES)), AXES)
    return jax.shard_map(
        local,
        mesh=fine,
        in_specs=(P(ROW, COL), P(ROW, COL), P(None, ROW, COL), P(None, ROW, COL)),
        out_specs=(P(ROW, COL), P(None, ROW, COL)),
        check_vma=False,
    )
```

```python
import itertools

import jax
import jax.numpy as jnp
from jax import lax
from jax.experimental import pallas as pl
from jax.experimental.pallas import tpu as pltpu
from jax.sharding import Mesh, PartitionSpec as P

F32 = jnp.float32
BF16 = jnp.bfloat16
ROW = ("yl", "x1", "x0", "core")
COL = ("yh1", "yh0", "zh1", "zh0", "zl")
AXES = ROW + COL
SPREAD = ("yh0", "zh1", "zh0")
GATHER = ("yh1",) + SPREAD
REST = ("x1", "yl")
SWAP = [(0, 1), (1, 0)]
TOK = 128
BLOCK = 256
WIDE = 2 * BLOCK
TOKENS = 2 * TOK
SHARE = TOKENS // 4
FEATURES = 4 * BLOCK
GRADS = 3 * WIDE
VMEM_LIMIT = 24 * 1024 * 1024
WHOLE = pl.BlockSpec(memory_space=pltpu.VMEM)
SCALARS = pl.BlockSpec(memory_space=pltpu.SMEM)


def turned(flip):
    pairs = []
    for bits in itertools.product(range(2), repeat=len(AXES)):
        yl, x1, x0, core, yh1, yh0, zh1, zh0, zl = bits
        there = (yh1, yh0, x0, core, yl ^ flip, zl, zh1, zh0, x1)
        pairs.append(tuple(sum(b << (8 - i) for i, b in enumerate(at)) for at in (bits, there)))
    return pairs


def dot(a, b, dims):
    return lax.dot_general(a, b, (dims, ((), ())), preferred_element_type=F32)


def params():
    return pltpu.CompilerParams(vmem_limit_bytes=VMEM_LIMIT)


def chunk(place_ref, f):
    core, x0 = place_ref[0], place_ref[1]
    core = core if f < 4 else 1 - core
    x0 = x0 if f % 4 < 2 else 1 - x0
    return 4 * (f % 2) + 2 * x0 + core


def half(place_ref, t):
    return place_ref[2] if t == 0 else 1 - place_ref[2]


def spread_kernel(acts_ref, copies_out, sems):
    copies = [pltpu.make_async_copy(acts_ref, copies_out.at[i], sems.at[i]) for i in range(16)]
    for copy in copies:
        copy.start()
    for copy in copies:
        copy.wait()


def spread(acts):
    return pl.pallas_call(
        spread_kernel,
        out_shape=jax.ShapeDtypeStruct((16,) + acts.shape, BF16),
        in_specs=[WHOLE],
        out_specs=pl.BlockSpec(memory_space=pl.ANY),
        scratch_shapes=[pltpu.SemaphoreType.DMA((16,))],
        compiler_params=params(),
        cost_estimate=pl.CostEstimate(flops=0, bytes_accessed=1100000, transcendentals=0),
        name="spread",
    )(acts)


def gates_kernel(place_ref, acts_ref, *refs):
    w_refs, parts_ref, wide_ref = refs[:8], refs[8], refs[9]
    for p in range(2):
        for t in range(2):
            for f in range(8):
                block = acts_ref[half(place_ref, t), chunk(place_ref, f), p]
                wide_ref[p, pl.ds(t * TOK, TOK), pl.ds(f * TOK, TOK)] = block
    for p in range(3):
        for j in range(2):
            total = jnp.zeros((TOKENS, BLOCK), F32)
            for s in range(4):
                total += dot(wide_ref[p // 2, :, pl.ds(s * BLOCK, BLOCK)], w_refs[2 * s + j][p], ((1,), (0,)))
            parts_ref[:, pl.ds(p * WIDE + j * BLOCK, BLOCK)] = total.astype(BF16)


def gates(place, acts, *weights):
    return pl.pallas_call(
        gates_kernel,
        out_shape=jax.ShapeDtypeStruct((TOKENS, GRADS), BF16),
        in_specs=[SCALARS] + [WHOLE] * 9,
        out_specs=WHOLE,
        scratch_shapes=[pltpu.VMEM((2, TOKENS, FEATURES), BF16)],
        compiler_params=params(),
        cost_estimate=pl.CostEstimate(flops=800000000, bytes_accessed=6000000, transcendentals=0),
        name="gates",
    )(place, acts, *weights)


def hidden_kernel(parts_ref, out_ref):
    total = parts_ref[0].astype(F32)
    for i in range(1, 4):
        total += parts_ref[i].astype(F32)
    gate, up, hidden_grad = (total[:, p * WIDE : (p + 1) * WIDE] for p in range(3))
    sig = 1.0 / (1.0 + jnp.exp(-gate))
    act = gate * sig
    gate_grad = (hidden_grad * up * sig * (1.0 + gate * (1.0 - sig))).astype(BF16)
    up_grad = (hidden_grad * act).astype(BF16)
    hidden = (act * up).astype(BF16)
    for i in range(4):
        for p, value in enumerate((gate_grad, up_grad, hidden)):
            out_ref[i, :, pl.ds(p * WIDE, WIDE)] = value


def hidden_grads(parts):
    return pl.pallas_call(
        hidden_kernel,
        out_shape=jax.ShapeDtypeStruct(parts.shape, BF16),
        in_specs=[WHOLE],
        out_specs=WHOLE,
        compiler_params=params(),
        cost_estimate=pl.CostEstimate(flops=2000000, bytes_accessed=1600000, transcendentals=32768),
        name="hidden_grads",
    )(parts)


def input_kernel(place_ref, grads_ref, *refs):
    w_refs, dx_ref = refs[:8], refs[8]
    for s in range(4):
        dx = jnp.zeros((TOKENS, BLOCK), F32)
        for p in range(2):
            for j in range(2):
                grads = grads_ref[:, pl.ds(p * WIDE + j * BLOCK, BLOCK)]
                dx += dot(grads, w_refs[2 * s + j][p], ((1,), (1,)))
        dx = dx.astype(BF16)
        for t in range(2):
            for f in range(2):
                part = dx[t * TOK : (t + 1) * TOK, f * TOK : (f + 1) * TOK]
                dx_ref[chunk(place_ref, 2 * s + f), t] = part


def input_terms(place, grads, *weights):
    return pl.pallas_call(
        input_kernel,
        out_shape=jax.ShapeDtypeStruct((8, 2, TOK, TOK), BF16),
        in_specs=[SCALARS] + [WHOLE] * 9,
        out_specs=WHOLE,
        compiler_params=params(),
        cost_estimate=pl.CostEstimate(flops=540000000, bytes_accessed=4000000, transcendentals=0),
        name="input_terms",
    )(place, grads, *weights)


def weight_kernel(
    place_ref, acts_ref, other_acts_ref, grads_ref, other_grads_ref, keep_ref, z_ref, x_ref, xz_ref, wide_ref
):
    for p in range(2):
        for t in range(2):
            for f in range(4):
                x0 = place_ref[1] if f < 2 else 1 - place_ref[1]
                cols = pl.ds(f * TOK, TOK)
                mine = acts_ref[half(place_ref, t), chunk(place_ref, f), p]
                wide_ref[p, pl.ds(t * TOK, TOK), cols] = mine
                wide_ref[p, pl.ds(TOKENS + t * TOK, TOK), cols] = other_acts_ref[half(place_ref, t), f % 2, x0, p]
    for side in (1, 0):
        for p in range(3):
            for j in range(2):
                cols = pl.ds(p * WIDE + j * BLOCK, BLOCK)
                term = jnp.zeros((BLOCK, BLOCK), F32)
                for i, ref in enumerate((grads_ref, other_grads_ref)):
                    x = wide_ref[p // 2, pl.ds(i * TOKENS, TOKENS), pl.ds(side * BLOCK, BLOCK)]
                    term += dot(x, ref[:, cols], ((0,), (0,)))
                out_ref = ((keep_ref, z_ref), (x_ref, xz_ref))[side][j]
                out_ref[p] = term.astype(out_ref.dtype)


def weight_terms(place, acts, other_acts, grads, other_grads):
    shape = (3, BLOCK, BLOCK)
    send = jax.ShapeDtypeStruct(shape, BF16)
    return pl.pallas_call(
        weight_kernel,
        out_shape=(jax.ShapeDtypeStruct(shape, F32), send, send, send),
        in_specs=[SCALARS] + [WHOLE] * 4,
        out_specs=(WHOLE,) * 4,
        scratch_shapes=[pltpu.VMEM((2, 2 * TOKENS, WIDE), BF16)],
        compiler_params=params(),
        cost_estimate=pl.CostEstimate(flops=800000000, bytes_accessed=6000000, transcendentals=0),
        name="weight_terms",
    )(place, acts, other_acts, grads, other_grads)


def exchange(pieces, axes):
    return lax.all_to_all(pieces, axes, split_axis=0, concat_axis=0, tiled=True)


def local(inputs, out_grad, codes, scales):
    place = jnp.stack([lax.axis_index("core"), lax.axis_index("x0"), lax.axis_index("yh1")])
    there = [turned(flip) for flip in range(2)]

    acts = spread(lax.ppermute(jnp.stack([inputs, out_grad]), AXES, there[0]))
    w = (codes.astype(F32) * scales.astype(F32)).astype(BF16)
    w_z = lax.ppermute(w, "zl", SWAP)
    acts, w_z = lax.optimization_barrier((acts, w_z))
    weights = [w, w_z] + [lax.ppermute(block, "x0", SWAP) for block in (w, w_z)]
    weights += [lax.ppermute(block, "core", SWAP) for block in weights]
    acts = exchange(acts, GATHER).reshape(2, 8, 2, TOK, TOK)

    parts = gates(place, acts, *weights)
    other_acts = acts.reshape(2, 2, 2, 2, 2, TOK, TOK)
    other_acts = lax.dynamic_index_in_dim(other_acts, 1 - place[0], axis=3, keepdims=False)
    other_acts = lax.ppermute(other_acts, "core", SWAP)
    parts = exchange(parts.reshape(4, SHARE, GRADS), REST)
    parts, other_acts = lax.optimization_barrier((parts, other_acts))
    grads = exchange(hidden_grads(parts), REST).reshape(TOKENS, GRADS)
    other_grads = lax.ppermute(grads, "core", SWAP)

    dx = exchange(input_terms(place, grads, *weights), SPREAD)
    dx = jnp.sum(dx.astype(F32), axis=0).astype(BF16)
    back = [lax.ppermute(dx[i], AXES, [(b, a) for a, b in there[i]]) for i in range(2)]
    input_grad = (back[0].astype(F32) + back[1].astype(F32)).astype(BF16)

    weight_grad, z, x, xz = weight_terms(place, acts, other_acts, grads, other_grads)
    weight_grad += lax.ppermute(z, "zl", SWAP).astype(F32)
    weight_grad += lax.ppermute(x, "x0", SWAP).astype(F32)
    weight_grad += lax.ppermute(xz, ("x0", "zl"), [(i, 3 - i) for i in range(4)]).astype(F32)
    return input_grad, weight_grad


def solution(mesh):
    fine = Mesh(mesh.devices.reshape((2,) * len(AXES)), AXES)
    return jax.shard_map(
        local,
        mesh=fine,
        in_specs=(P(ROW, COL), P(ROW, COL), P(None, ROW, COL), P(None, ROW, COL)),
        out_specs=(P(ROW, COL), P(None, ROW, COL)),
        check_vma=False,
    )
```

```python
import itertools

import jax
import jax.numpy as jnp
from jax import lax
from jax.experimental import pallas as pl
from jax.experimental.pallas import tpu as pltpu
from jax.sharding import Mesh, PartitionSpec as P

F32 = jnp.float32
BF16 = jnp.bfloat16
ROW = ("yl", "x1", "x0", "core")
COL = ("yh1", "yh0", "zh1", "zh0", "zl")
AXES = ROW + COL
SPREAD = ("yh0", "zh1", "zh0")
GATHER = ("zh1", "zh0", "yh0", "yh1")
REST = ("x1", "yl")
SWAP = [(0, 1), (1, 0)]
TOK = 128
BLOCK = 256
WIDE = 2 * BLOCK
TOKENS = 2 * TOK
SHARE = TOKENS // 4
FEATURES = 4 * BLOCK
GRADS = 3 * WIDE
VMEM_LIMIT = 24 * 1024 * 1024
WHOLE = pl.BlockSpec(memory_space=pltpu.VMEM)
SCALARS = pl.BlockSpec(memory_space=pltpu.SMEM)


def turned(flip):
    pairs = []
    for bits in itertools.product(range(2), repeat=len(AXES)):
        yl, x1, x0, core, yh1, yh0, zh1, zh0, zl = bits
        there = (yh1, yh0, x0, core, yl ^ flip, zl, zh1, zh0, x1)
        pairs.append(tuple(sum(b << (8 - i) for i, b in enumerate(at)) for at in (bits, there)))
    return pairs


def dot(a, b, dims):
    return lax.dot_general(a, b, (dims, ((), ())), preferred_element_type=F32)


def params():
    return pltpu.CompilerParams(vmem_limit_bytes=VMEM_LIMIT)


def place_of(place_ref, f):
    core, x0 = place_ref[0], place_ref[1]
    return core if f < 4 else 1 - core, x0 if f % 4 < 2 else 1 - x0, f % 2


def gathered(place_ref, f):
    core, x0, b = place_of(place_ref, f)
    return 4 * x0 + 2 * core + b


def summed(place_ref, f):
    core, x0, b = place_of(place_ref, f)
    return 4 * b + 2 * x0 + core


def half(place_ref, t):
    return place_ref[2] if t == 0 else 1 - place_ref[2]


def spread_kernel(acts_ref, copies_out, sems):
    copies = [pltpu.make_async_copy(acts_ref, copies_out.at[i], sems.at[i]) for i in range(16)]
    for copy in copies:
        copy.start()
    for copy in copies:
        copy.wait()


def spread(acts):
    return pl.pallas_call(
        spread_kernel,
        out_shape=jax.ShapeDtypeStruct((16,) + acts.shape, BF16),
        in_specs=[WHOLE],
        out_specs=pl.BlockSpec(memory_space=pl.ANY),
        scratch_shapes=[pltpu.SemaphoreType.DMA((16,))],
        compiler_params=params(),
        cost_estimate=pl.CostEstimate(flops=0, bytes_accessed=1100000, transcendentals=0),
        name="spread",
    )(acts)


def gates_kernel(place_ref, acts_ref, *refs):
    w_refs, parts_ref, wide_ref = refs[:8], refs[8], refs[9]
    for p in range(2):
        for t in range(2):
            for f in range(8):
                block = acts_ref[gathered(place_ref, f), half(place_ref, t), p]
                wide_ref[p, pl.ds(t * TOK, TOK), pl.ds(f * TOK, TOK)] = block
    for p in range(3):
        for j in range(2):
            total = jnp.zeros((TOKENS, BLOCK), F32)
            for s in range(4):
                total += dot(wide_ref[p // 2, :, pl.ds(s * BLOCK, BLOCK)], w_refs[2 * s + j][p], ((1,), (0,)))
            parts_ref[:, pl.ds(p * WIDE + j * BLOCK, BLOCK)] = total.astype(BF16)


def gates(place, acts, *weights):
    return pl.pallas_call(
        gates_kernel,
        out_shape=jax.ShapeDtypeStruct((TOKENS, GRADS), BF16),
        in_specs=[SCALARS] + [WHOLE] * 9,
        out_specs=WHOLE,
        scratch_shapes=[pltpu.VMEM((2, TOKENS, FEATURES), BF16)],
        compiler_params=params(),
        cost_estimate=pl.CostEstimate(flops=800000000, bytes_accessed=6000000, transcendentals=0),
        name="gates",
    )(place, acts, *weights)


def hidden_kernel(parts_ref, out_ref):
    total = parts_ref[0].astype(F32)
    for i in range(1, 4):
        total += parts_ref[i].astype(F32)
    gate, up, hidden_grad = (total[:, p * WIDE : (p + 1) * WIDE] for p in range(3))
    sig = 1.0 / (1.0 + jnp.exp(-gate))
    act = gate * sig
    gate_grad = (hidden_grad * up * sig * (1.0 + gate * (1.0 - sig))).astype(BF16)
    up_grad = (hidden_grad * act).astype(BF16)
    hidden = (act * up).astype(BF16)
    for i in range(4):
        for p, value in enumerate((gate_grad, up_grad, hidden)):
            out_ref[i, :, pl.ds(p * WIDE, WIDE)] = value


def hidden_grads(parts):
    return pl.pallas_call(
        hidden_kernel,
        out_shape=jax.ShapeDtypeStruct(parts.shape, BF16),
        in_specs=[WHOLE],
        out_specs=WHOLE,
        compiler_params=params(),
        cost_estimate=pl.CostEstimate(flops=2000000, bytes_accessed=1600000, transcendentals=32768),
        name="hidden_grads",
    )(parts)


def input_kernel(place_ref, grads_ref, *refs):
    w_refs, dx_ref = refs[:8], refs[8]
    for s in range(4):
        dx = jnp.zeros((TOKENS, BLOCK), F32)
        for p in range(2):
            for j in range(2):
                grads = grads_ref[:, pl.ds(p * WIDE + j * BLOCK, BLOCK)]
                dx += dot(grads, w_refs[2 * s + j][p], ((1,), (1,)))
        dx = dx.astype(BF16)
        for t in range(2):
            for f in range(2):
                part = dx[t * TOK : (t + 1) * TOK, f * TOK : (f + 1) * TOK]
                dx_ref[summed(place_ref, 2 * s + f), t] = part


def input_terms(place, grads, *weights):
    return pl.pallas_call(
        input_kernel,
        out_shape=jax.ShapeDtypeStruct((8, 2, TOK, TOK), BF16),
        in_specs=[SCALARS] + [WHOLE] * 9,
        out_specs=WHOLE,
        compiler_params=params(),
        cost_estimate=pl.CostEstimate(flops=540000000, bytes_accessed=4000000, transcendentals=0),
        name="input_terms",
    )(place, grads, *weights)


def weight_kernel(
    place_ref, acts_ref, other_acts_ref, grads_ref, other_grads_ref, keep_ref, z_ref, x_ref, xz_ref, wide_ref
):
    for p in range(2):
        for t in range(2):
            for f in range(4):
                x0 = place_ref[1] if f < 2 else 1 - place_ref[1]
                cols = pl.ds(f * TOK, TOK)
                mine = acts_ref[gathered(place_ref, f), half(place_ref, t), p]
                wide_ref[p, pl.ds(t * TOK, TOK), cols] = mine
                wide_ref[p, pl.ds(TOKENS + t * TOK, TOK), cols] = other_acts_ref[x0, f % 2, half(place_ref, t), p]
    for side in (1, 0):
        for p in range(3):
            for j in range(2):
                cols = pl.ds(p * WIDE + j * BLOCK, BLOCK)
                term = jnp.zeros((BLOCK, BLOCK), F32)
                for i, ref in enumerate((grads_ref, other_grads_ref)):
                    x = wide_ref[p // 2, pl.ds(i * TOKENS, TOKENS), pl.ds(side * BLOCK, BLOCK)]
                    term += dot(x, ref[:, cols], ((0,), (0,)))
                out_ref = ((keep_ref, z_ref), (x_ref, xz_ref))[side][j]
                out_ref[p] = term.astype(out_ref.dtype)


def weight_terms(place, acts, other_acts, grads, other_grads):
    shape = (3, BLOCK, BLOCK)
    send = jax.ShapeDtypeStruct(shape, BF16)
    return pl.pallas_call(
        weight_kernel,
        out_shape=(jax.ShapeDtypeStruct(shape, F32), send, send, send),
        in_specs=[SCALARS] + [WHOLE] * 4,
        out_specs=(WHOLE,) * 4,
        scratch_shapes=[pltpu.VMEM((2, 2 * TOKENS, WIDE), BF16)],
        compiler_params=params(),
        cost_estimate=pl.CostEstimate(flops=800000000, bytes_accessed=6000000, transcendentals=0),
        name="weight_terms",
    )(place, acts, other_acts, grads, other_grads)


def exchange(pieces, axes):
    return lax.all_to_all(pieces, axes, split_axis=0, concat_axis=0, tiled=True)


def local(inputs, out_grad, codes, scales):
    place = jnp.stack([lax.axis_index("core"), lax.axis_index("x0"), lax.axis_index("yh1")])
    there = [turned(flip) for flip in range(2)]

    acts = spread(lax.ppermute(jnp.stack([inputs, out_grad]), AXES, there[0]))
    w = (codes.astype(F32) * scales.astype(F32)).astype(BF16)
    w_z = lax.ppermute(w, "zl", SWAP)
    acts, w_z = lax.optimization_barrier((acts, w_z))
    weights = [w, w_z] + [lax.ppermute(block, "x0", SWAP) for block in (w, w_z)]
    weights += [lax.ppermute(block, "core", SWAP) for block in weights]
    acts = exchange(acts, GATHER).reshape(8, 2, 2, TOK, TOK)

    parts = gates(place, acts, *weights)
    other_acts = acts.reshape(2, 2, 2, 2, 2, TOK, TOK)
    other_acts = lax.dynamic_index_in_dim(other_acts, 1 - place[0], axis=1, keepdims=False)
    other_acts = lax.ppermute(other_acts, "core", SWAP)
    parts = exchange(parts.reshape(4, SHARE, GRADS), REST)
    parts, other_acts = lax.optimization_barrier((parts, other_acts))
    grads = exchange(hidden_grads(parts), REST).reshape(TOKENS, GRADS)
    other_grads = lax.ppermute(grads, "core", SWAP)

    dx = exchange(input_terms(place, grads, *weights), SPREAD)
    dx = jnp.sum(dx.astype(F32), axis=0).astype(BF16)
    back = [lax.ppermute(dx[i], AXES, [(b, a) for a, b in there[i]]) for i in range(2)]
    input_grad = (back[0].astype(F32) + back[1].astype(F32)).astype(BF16)

    weight_grad, z, x, xz = weight_terms(place, acts, other_acts, grads, other_grads)
    weight_grad += lax.ppermute(z, "zl", SWAP).astype(F32)
    weight_grad += lax.ppermute(x, "x0", SWAP).astype(F32)
    weight_grad += lax.ppermute(xz, ("x0", "zl"), [(i, 3 - i) for i in range(4)]).astype(F32)
    return input_grad, weight_grad


def solution(mesh):
    fine = Mesh(mesh.devices.reshape((2,) * len(AXES)), AXES)
    return jax.shard_map(
        local,
        mesh=fine,
        in_specs=(P(ROW, COL), P(ROW, COL), P(None, ROW, COL), P(None, ROW, COL)),
        out_specs=(P(ROW, COL), P(None, ROW, COL)),
        check_vma=False,
    )
```

```python
import itertools

import jax
import jax.numpy as jnp
from jax import lax
from jax.experimental import pallas as pl
from jax.experimental.pallas import tpu as pltpu
from jax.sharding import Mesh, PartitionSpec as P

F32 = jnp.float32
BF16 = jnp.bfloat16
ROW = ("yl", "x1", "x0", "core")
COL = ("yh1", "yh0", "zh1", "zh0", "zl")
AXES = ROW + COL
SPREAD = ("yh0", "zh1", "zh0")
GATHER = ("zh0", "zh1", "yh0", "yh1")
REST = ("x1", "yl")
SWAP = [(0, 1), (1, 0)]
TOK = 128
BLOCK = 256
WIDE = 2 * BLOCK
TOKENS = 2 * TOK
SHARE = TOKENS // 4
FEATURES = 4 * BLOCK
GRADS = 3 * WIDE
VMEM_LIMIT = 24 * 1024 * 1024
WHOLE = pl.BlockSpec(memory_space=pltpu.VMEM)
SCALARS = pl.BlockSpec(memory_space=pltpu.SMEM)


def turned(flip):
    pairs = []
    for bits in itertools.product(range(2), repeat=len(AXES)):
        yl, x1, x0, core, yh1, yh0, zh1, zh0, zl = bits
        there = (yh1, yh0, x0, core, yl ^ flip, zl, zh1, zh0, x1)
        pairs.append(tuple(sum(b << (8 - i) for i, b in enumerate(at)) for at in (bits, there)))
    return pairs


def dot(a, b, dims):
    return lax.dot_general(a, b, (dims, ((), ())), preferred_element_type=F32)


def params():
    return pltpu.CompilerParams(vmem_limit_bytes=VMEM_LIMIT)


def place_of(place_ref, f):
    core, x0 = place_ref[0], place_ref[1]
    return core if f < 4 else 1 - core, x0 if f % 4 < 2 else 1 - x0, f % 2


def gathered(place_ref, f):
    core, x0, b = place_of(place_ref, f)
    return 4 * core + 2 * x0 + b


def summed(place_ref, f):
    core, x0, b = place_of(place_ref, f)
    return 4 * b + 2 * x0 + core


def half(place_ref, t):
    return place_ref[2] if t == 0 else 1 - place_ref[2]


def spread_kernel(acts_ref, copies_out, sems):
    copies = [pltpu.make_async_copy(acts_ref, copies_out.at[i], sems.at[i]) for i in range(16)]
    for copy in copies:
        copy.start()
    for copy in copies:
        copy.wait()


def spread(acts):
    return pl.pallas_call(
        spread_kernel,
        out_shape=jax.ShapeDtypeStruct((16,) + acts.shape, BF16),
        in_specs=[WHOLE],
        out_specs=pl.BlockSpec(memory_space=pl.ANY),
        scratch_shapes=[pltpu.SemaphoreType.DMA((16,))],
        compiler_params=params(),
        cost_estimate=pl.CostEstimate(flops=0, bytes_accessed=1100000, transcendentals=0),
        name="spread",
    )(acts)


def gates_kernel(place_ref, acts_ref, *refs):
    w_refs, parts_ref, wide_ref = refs[:8], refs[8], refs[9]
    for p in range(2):
        for t in range(2):
            for f in range(8):
                block = acts_ref[gathered(place_ref, f), half(place_ref, t), p]
                wide_ref[p, pl.ds(t * TOK, TOK), pl.ds(f * TOK, TOK)] = block
    for p in range(3):
        for j in range(2):
            total = jnp.zeros((TOKENS, BLOCK), F32)
            for s in range(4):
                total += dot(wide_ref[p // 2, :, pl.ds(s * BLOCK, BLOCK)], w_refs[2 * s + j][p], ((1,), (0,)))
            parts_ref[:, pl.ds(p * WIDE + j * BLOCK, BLOCK)] = total.astype(BF16)


def gates(place, acts, *weights):
    return pl.pallas_call(
        gates_kernel,
        out_shape=jax.ShapeDtypeStruct((TOKENS, GRADS), BF16),
        in_specs=[SCALARS] + [WHOLE] * 9,
        out_specs=WHOLE,
        scratch_shapes=[pltpu.VMEM((2, TOKENS, FEATURES), BF16)],
        compiler_params=params(),
        cost_estimate=pl.CostEstimate(flops=800000000, bytes_accessed=6000000, transcendentals=0),
        name="gates",
    )(place, acts, *weights)


def hidden_kernel(parts_ref, out_ref):
    total = parts_ref[0].astype(F32)
    for i in range(1, 4):
        total += parts_ref[i].astype(F32)
    gate, up, hidden_grad = (total[:, p * WIDE : (p + 1) * WIDE] for p in range(3))
    sig = 1.0 / (1.0 + jnp.exp(-gate))
    act = gate * sig
    gate_grad = (hidden_grad * up * sig * (1.0 + gate * (1.0 - sig))).astype(BF16)
    up_grad = (hidden_grad * act).astype(BF16)
    hidden = (act * up).astype(BF16)
    for i in range(4):
        for p, value in enumerate((gate_grad, up_grad, hidden)):
            out_ref[i, :, pl.ds(p * WIDE, WIDE)] = value


def hidden_grads(parts):
    return pl.pallas_call(
        hidden_kernel,
        out_shape=jax.ShapeDtypeStruct(parts.shape, BF16),
        in_specs=[WHOLE],
        out_specs=WHOLE,
        compiler_params=params(),
        cost_estimate=pl.CostEstimate(flops=2000000, bytes_accessed=1600000, transcendentals=32768),
        name="hidden_grads",
    )(parts)


def input_kernel(place_ref, grads_ref, *refs):
    w_refs, dx_ref = refs[:8], refs[8]
    for s in range(4):
        dx = jnp.zeros((TOKENS, BLOCK), F32)
        for p in range(2):
            for j in range(2):
                grads = grads_ref[:, pl.ds(p * WIDE + j * BLOCK, BLOCK)]
                dx += dot(grads, w_refs[2 * s + j][p], ((1,), (1,)))
        dx = dx.astype(BF16)
        for t in range(2):
            for f in range(2):
                part = dx[t * TOK : (t + 1) * TOK, f * TOK : (f + 1) * TOK]
                dx_ref[summed(place_ref, 2 * s + f), t] = part


def input_terms(place, grads, *weights):
    return pl.pallas_call(
        input_kernel,
        out_shape=jax.ShapeDtypeStruct((8, 2, TOK, TOK), BF16),
        in_specs=[SCALARS] + [WHOLE] * 9,
        out_specs=WHOLE,
        compiler_params=params(),
        cost_estimate=pl.CostEstimate(flops=540000000, bytes_accessed=4000000, transcendentals=0),
        name="input_terms",
    )(place, grads, *weights)


def weight_kernel(
    place_ref, acts_ref, other_acts_ref, grads_ref, other_grads_ref, keep_ref, z_ref, x_ref, xz_ref, wide_ref
):
    for p in range(2):
        for t in range(2):
            for f in range(4):
                x0 = place_ref[1] if f < 2 else 1 - place_ref[1]
                cols = pl.ds(f * TOK, TOK)
                mine = acts_ref[gathered(place_ref, f), half(place_ref, t), p]
                wide_ref[p, pl.ds(t * TOK, TOK), cols] = mine
                wide_ref[p, pl.ds(TOKENS + t * TOK, TOK), cols] = other_acts_ref[x0, f % 2, half(place_ref, t), p]
    for side in (1, 0):
        for p in range(3):
            for j in range(2):
                cols = pl.ds(p * WIDE + j * BLOCK, BLOCK)
                term = jnp.zeros((BLOCK, BLOCK), F32)
                for i, ref in enumerate((grads_ref, other_grads_ref)):
                    x = wide_ref[p // 2, pl.ds(i * TOKENS, TOKENS), pl.ds(side * BLOCK, BLOCK)]
                    term += dot(x, ref[:, cols], ((0,), (0,)))
                out_ref = ((keep_ref, z_ref), (x_ref, xz_ref))[side][j]
                out_ref[p] = term.astype(out_ref.dtype)


def weight_terms(place, acts, other_acts, grads, other_grads):
    shape = (3, BLOCK, BLOCK)
    send = jax.ShapeDtypeStruct(shape, BF16)
    return pl.pallas_call(
        weight_kernel,
        out_shape=(jax.ShapeDtypeStruct(shape, F32), send, send, send),
        in_specs=[SCALARS] + [WHOLE] * 4,
        out_specs=(WHOLE,) * 4,
        scratch_shapes=[pltpu.VMEM((2, 2 * TOKENS, WIDE), BF16)],
        compiler_params=params(),
        cost_estimate=pl.CostEstimate(flops=800000000, bytes_accessed=6000000, transcendentals=0),
        name="weight_terms",
    )(place, acts, other_acts, grads, other_grads)


def exchange(pieces, axes):
    return lax.all_to_all(pieces, axes, split_axis=0, concat_axis=0, tiled=True)


def local(inputs, out_grad, codes, scales):
    place = jnp.stack([lax.axis_index("core"), lax.axis_index("x0"), lax.axis_index("yh1")])
    there = [turned(flip) for flip in range(2)]

    acts = spread(lax.ppermute(jnp.stack([inputs, out_grad]), AXES, there[0]))
    w = (codes.astype(F32) * scales.astype(F32)).astype(BF16)
    w_z = lax.ppermute(w, "zl", SWAP)
    acts, w_z = lax.optimization_barrier((acts, w_z))
    weights = [w, w_z] + [lax.ppermute(block, "x0", SWAP) for block in (w, w_z)]
    weights += [lax.ppermute(block, "core", SWAP) for block in weights]
    acts = exchange(acts, GATHER).reshape(8, 2, 2, TOK, TOK)

    parts = gates(place, acts, *weights)
    other_acts = acts.reshape(2, 2, 2, 2, 2, TOK, TOK)
    other_acts = lax.dynamic_index_in_dim(other_acts, 1 - place[0], axis=0, keepdims=False)
    other_acts = lax.ppermute(other_acts, "core", SWAP)
    parts = exchange(parts.reshape(4, SHARE, GRADS), REST)
    parts, other_acts = lax.optimization_barrier((parts, other_acts))
    grads = exchange(hidden_grads(parts), REST).reshape(TOKENS, GRADS)
    other_grads = lax.ppermute(grads, "core", SWAP)

    dx = exchange(input_terms(place, grads, *weights), SPREAD)
    dx = jnp.sum(dx.astype(F32), axis=0).astype(BF16)
    back = [lax.ppermute(dx[i], AXES, [(b, a) for a, b in there[i]]) for i in range(2)]
    input_grad = (back[0].astype(F32) + back[1].astype(F32)).astype(BF16)

    weight_grad, z, x, xz = weight_terms(place, acts, other_acts, grads, other_grads)
    weight_grad += lax.ppermute(z, "zl", SWAP).astype(F32)
    weight_grad += lax.ppermute(x, "x0", SWAP).astype(F32)
    weight_grad += lax.ppermute(xz, ("x0", "zl"), [(i, 3 - i) for i in range(4)]).astype(F32)
    return input_grad, weight_grad


def solution(mesh):
    fine = Mesh(mesh.devices.reshape((2,) * len(AXES)), AXES)
    return jax.shard_map(
        local,
        mesh=fine,
        in_specs=(P(ROW, COL), P(ROW, COL), P(None, ROW, COL), P(None, ROW, COL)),
        out_specs=(P(ROW, COL), P(None, ROW, COL)),
        check_vma=False,
    )
```

```python
import itertools

import jax
import jax.numpy as jnp
from jax import lax
from jax.experimental import pallas as pl
from jax.experimental.pallas import tpu as pltpu
from jax.sharding import Mesh, PartitionSpec as P

F32 = jnp.float32
BF16 = jnp.bfloat16
ROW = ("yl", "x1", "x0", "core")
COL = ("yh1", "yh0", "zh1", "zh0", "zl")
AXES = ROW + COL
SPREAD = ("yh0", "zh0", "zh1")
GATHER = ("zh0", "zh1", "yh1", "yh0")
REST = ("x1", "yl")
SWAP = [(0, 1), (1, 0)]
TOK = 128
BLOCK = 256
WIDE = 2 * BLOCK
TOKENS = 2 * TOK
SHARE = TOKENS // 4
FEATURES = 4 * BLOCK
GRADS = 3 * WIDE
VMEM_LIMIT = 24 * 1024 * 1024
WHOLE = pl.BlockSpec(memory_space=pltpu.VMEM)
SCALARS = pl.BlockSpec(memory_space=pltpu.SMEM)


def turned(flip):
    pairs = []
    for bits in itertools.product(range(2), repeat=len(AXES)):
        yl, x1, x0, core, yh1, yh0, zh1, zh0, zl = bits
        there = (yh1, yh0, x0, core, yl ^ flip, zl, zh1, zh0, x1)
        pairs.append(tuple(sum(b << (8 - i) for i, b in enumerate(at)) for at in (bits, there)))
    return pairs


def dot(a, b, dims):
    return lax.dot_general(a, b, (dims, ((), ())), preferred_element_type=F32)


def params():
    return pltpu.CompilerParams(vmem_limit_bytes=VMEM_LIMIT)


def place_of(place_ref, f):
    core, x0 = place_ref[0], place_ref[1]
    return core if f < 4 else 1 - core, x0 if f % 4 < 2 else 1 - x0, f % 2


def gathered(place_ref, f):
    core, x0, unused = place_of(place_ref, f)
    return 2 * core + x0


def summed(place_ref, f):
    core, x0, b = place_of(place_ref, f)
    return 4 * b + 2 * core + x0


def half(place_ref, t):
    return place_ref[2] if t == 0 else 1 - place_ref[2]


def spread_kernel(acts_ref, copies_out, sems):
    copies = [pltpu.make_async_copy(acts_ref, copies_out.at[i], sems.at[i]) for i in range(16)]
    for copy in copies:
        copy.start()
    for copy in copies:
        copy.wait()


def spread(acts):
    return pl.pallas_call(
        spread_kernel,
        out_shape=jax.ShapeDtypeStruct((16,) + acts.shape, BF16),
        in_specs=[WHOLE],
        out_specs=pl.BlockSpec(memory_space=pl.ANY),
        scratch_shapes=[pltpu.SemaphoreType.DMA((16,))],
        compiler_params=params(),
        cost_estimate=pl.CostEstimate(flops=0, bytes_accessed=1100000, transcendentals=0),
        name="spread",
    )(acts)


def gates_kernel(place_ref, acts_ref, *refs):
    w_refs, parts_ref, wide_ref = refs[:8], refs[8], refs[9]
    for p in range(2):
        for t in range(2):
            for f in range(8):
                block = acts_ref[gathered(place_ref, f), half(place_ref, t), f % 2, p]
                wide_ref[p, pl.ds(t * TOK, TOK), pl.ds(f * TOK, TOK)] = block
    for p in range(3):
        for j in range(2):
            total = jnp.zeros((TOKENS, BLOCK), F32)
            for s in range(4):
                total += dot(wide_ref[p // 2, :, pl.ds(s * BLOCK, BLOCK)], w_refs[2 * s + j][p], ((1,), (0,)))
            parts_ref[:, pl.ds(p * WIDE + j * BLOCK, BLOCK)] = total.astype(BF16)


def gates(place, acts, *weights):
    return pl.pallas_call(
        gates_kernel,
        out_shape=jax.ShapeDtypeStruct((TOKENS, GRADS), BF16),
        in_specs=[SCALARS] + [WHOLE] * 9,
        out_specs=WHOLE,
        scratch_shapes=[pltpu.VMEM((2, TOKENS, FEATURES), BF16)],
        compiler_params=params(),
        cost_estimate=pl.CostEstimate(flops=800000000, bytes_accessed=6000000, transcendentals=0),
        name="gates",
    )(place, acts, *weights)


def hidden_kernel(parts_ref, out_ref):
    total = parts_ref[0].astype(F32)
    for i in range(1, 4):
        total += parts_ref[i].astype(F32)
    gate, up, hidden_grad = (total[:, p * WIDE : (p + 1) * WIDE] for p in range(3))
    sig = 1.0 / (1.0 + jnp.exp(-gate))
    act = gate * sig
    gate_grad = (hidden_grad * up * sig * (1.0 + gate * (1.0 - sig))).astype(BF16)
    up_grad = (hidden_grad * act).astype(BF16)
    hidden = (act * up).astype(BF16)
    for i in range(4):
        for p, value in enumerate((gate_grad, up_grad, hidden)):
            out_ref[i, :, pl.ds(p * WIDE, WIDE)] = value


def hidden_grads(parts):
    return pl.pallas_call(
        hidden_kernel,
        out_shape=jax.ShapeDtypeStruct(parts.shape, BF16),
        in_specs=[WHOLE],
        out_specs=WHOLE,
        compiler_params=params(),
        cost_estimate=pl.CostEstimate(flops=2000000, bytes_accessed=1600000, transcendentals=32768),
        name="hidden_grads",
    )(parts)


def input_kernel(place_ref, grads_ref, *refs):
    w_refs, dx_ref = refs[:8], refs[8]
    for s in range(4):
        dx = jnp.zeros((TOKENS, BLOCK), F32)
        for p in range(2):
            for j in range(2):
                grads = grads_ref[:, pl.ds(p * WIDE + j * BLOCK, BLOCK)]
                dx += dot(grads, w_refs[2 * s + j][p], ((1,), (1,)))
        dx = dx.astype(BF16)
        for t in range(2):
            for f in range(2):
                part = dx[t * TOK : (t + 1) * TOK, f * TOK : (f + 1) * TOK]
                dx_ref[summed(place_ref, 2 * s + f), t] = part


def input_terms(place, grads, *weights):
    return pl.pallas_call(
        input_kernel,
        out_shape=jax.ShapeDtypeStruct((8, 2, TOK, TOK), BF16),
        in_specs=[SCALARS] + [WHOLE] * 9,
        out_specs=WHOLE,
        compiler_params=params(),
        cost_estimate=pl.CostEstimate(flops=540000000, bytes_accessed=4000000, transcendentals=0),
        name="input_terms",
    )(place, grads, *weights)


def weight_kernel(
    place_ref, acts_ref, other_acts_ref, grads_ref, other_grads_ref, keep_ref, z_ref, x_ref, xz_ref, wide_ref
):
    for p in range(2):
        for t in range(2):
            for f in range(4):
                x0 = place_ref[1] if f < 2 else 1 - place_ref[1]
                cols = pl.ds(f * TOK, TOK)
                mine = acts_ref[gathered(place_ref, f), half(place_ref, t), f % 2, p]
                wide_ref[p, pl.ds(t * TOK, TOK), cols] = mine
                wide_ref[p, pl.ds(TOKENS + t * TOK, TOK), cols] = other_acts_ref[x0, half(place_ref, t), f % 2, p]
    for side in (1, 0):
        for p in range(3):
            for j in range(2):
                cols = pl.ds(p * WIDE + j * BLOCK, BLOCK)
                term = jnp.zeros((BLOCK, BLOCK), F32)
                for i, ref in enumerate((grads_ref, other_grads_ref)):
                    x = wide_ref[p // 2, pl.ds(i * TOKENS, TOKENS), pl.ds(side * BLOCK, BLOCK)]
                    term += dot(x, ref[:, cols], ((0,), (0,)))
                out_ref = ((keep_ref, z_ref), (x_ref, xz_ref))[side][j]
                out_ref[p] = term.astype(out_ref.dtype)


def weight_terms(place, acts, other_acts, grads, other_grads):
    shape = (3, BLOCK, BLOCK)
    send = jax.ShapeDtypeStruct(shape, BF16)
    return pl.pallas_call(
        weight_kernel,
        out_shape=(jax.ShapeDtypeStruct(shape, F32), send, send, send),
        in_specs=[SCALARS] + [WHOLE] * 4,
        out_specs=(WHOLE,) * 4,
        scratch_shapes=[pltpu.VMEM((2, 2 * TOKENS, WIDE), BF16)],
        compiler_params=params(),
        cost_estimate=pl.CostEstimate(flops=800000000, bytes_accessed=6000000, transcendentals=0),
        name="weight_terms",
    )(place, acts, other_acts, grads, other_grads)


def exchange(pieces, axes):
    return lax.all_to_all(pieces, axes, split_axis=0, concat_axis=0, tiled=True)


def local(inputs, out_grad, codes, scales):
    place = jnp.stack([lax.axis_index("core"), lax.axis_index("x0"), lax.axis_index("yh1")])
    there = [turned(flip) for flip in range(2)]

    acts = spread(lax.ppermute(jnp.stack([inputs, out_grad]), AXES, there[0]))
    w = (codes.astype(F32) * scales.astype(F32)).astype(BF16)
    w_z = lax.ppermute(w, "zl", SWAP)
    acts, w_z = lax.optimization_barrier((acts, w_z))
    weights = [w, w_z] + [lax.ppermute(block, "x0", SWAP) for block in (w, w_z)]
    weights += [lax.ppermute(block, "core", SWAP) for block in weights]
    acts = exchange(acts, GATHER).reshape(4, 2, 2, 2, TOK, TOK)

    parts = gates(place, acts, *weights)
    other_acts = acts.reshape(2, 2, 2, 2, 2, TOK, TOK)
    other_acts = lax.dynamic_index_in_dim(other_acts, 1 - place[0], axis=0, keepdims=False)
    other_acts = lax.ppermute(other_acts, "core", SWAP)
    parts = exchange(parts.reshape(4, SHARE, GRADS), REST)
    parts, other_acts = lax.optimization_barrier((parts, other_acts))
    grads = exchange(hidden_grads(parts), REST).reshape(TOKENS, GRADS)
    other_grads = lax.ppermute(grads, "core", SWAP)

    dx = exchange(input_terms(place, grads, *weights), SPREAD)
    dx = jnp.sum(dx.astype(F32), axis=0).astype(BF16)
    back = [lax.ppermute(dx[i], AXES, [(b, a) for a, b in there[i]]) for i in range(2)]
    input_grad = (back[0].astype(F32) + back[1].astype(F32)).astype(BF16)

    weight_grad, z, x, xz = weight_terms(place, acts, other_acts, grads, other_grads)
    weight_grad += lax.ppermute(z, "zl", SWAP).astype(F32)
    weight_grad += lax.ppermute(x, "x0", SWAP).astype(F32)
    weight_grad += lax.ppermute(xz, ("x0", "zl"), [(i, 3 - i) for i in range(4)]).astype(F32)
    return input_grad, weight_grad


def solution(mesh):
    fine = Mesh(mesh.devices.reshape((2,) * len(AXES)), AXES)
    return jax.shard_map(
        local,
        mesh=fine,
        in_specs=(P(ROW, COL), P(ROW, COL), P(None, ROW, COL), P(None, ROW, COL)),
        out_specs=(P(ROW, COL), P(None, ROW, COL)),
        check_vma=False,
    )
```
